256 devices in a mesh: segment: 8 (over y, core), fsdp: 32 (over z, x).
Axes of the slice: x: 4, y: 4, z: 8, core: 2. Of those that a mesh axis runs over, the one named last changes fastest.
Arguments:
- tokens: bfloat16 [1024, 6144], P('segment', 'fsdp'), may hold values from -6 to 6
- router_logits: float32 [1024, 2], P('segment'), may hold values from -6 to 6
- routes: int32 [1024, 2], P('segment'), may hold values from 0 to 7, as said below
- loss_weights: int32 [1024], P('segment'), may hold values from 1024 to 8192
- cotangent: bfloat16 [1024, 6144], P('segment', 'fsdp'), may hold values from -6 to 6
- gate_weight: bfloat16 [8, 6144, 8192], P('segment', None, 'fsdp'), may hold values from -0.078125 to 0.078125
- up_weight: bfloat16 [8, 6144, 8192], P('segment', None, 'fsdp'), may hold values from -0.078125 to 0.078125
- down_weight: bfloat16 [8, 8192, 6144], P('segment', 'fsdp'), may hold values from -0.0625 to 0.0625
Outputs:
- output: bfloat16 [1024, 6144], P('segment', 'fsdp')
- input_grad: bfloat16 [1024, 6144], P('segment', 'fsdp')
- down_grad: bfloat16 [8, 8192, 6144], P('segment', 'fsdp')
The draws below stay inside these ranges and needn't reach their ends.
Inputs may be any that keep to these rules, and one draw needn't show every extreme that they name: `routes`: each row names two different experts. Among the 128 tokens of one index of segment no expert is named more than 64 times, and one expert, the same for every index, is named exactly 64 times by those tokens.
All inputs are finite; a program needn't handle non-finite values.
Results may differ from the reference program's by a relative error of at most 0.035.
Values may be sent and summed in bfloat16 or wider, within the bound.
A program may use at most 128 MiB of HBM per device.

```python
import jax
import jax.numpy as jnp
from jax import lax

D = 6144
FF = 8192
EXPERTS = 8
TOK_DEV = 128
CAP = 64
TOKENS = 1024
SLOTS = 512
N_FSDP = 32


def draw_routes(key, part):
    key = jax.random.fold_in(key, 11)
    hot_key, block_key = jax.random.split(key)
    block_count = TOKENS // TOK_DEV
    hot = jax.random.randint(hot_key, (), 0, EXPERTS).astype(jnp.int32)
    others = ((hot + 1 + jnp.arange(EXPERTS - 1, dtype=jnp.int32)) % EXPERTS).astype(jnp.int32)
    pool = jnp.repeat(others, CAP)
    needed = 2 * TOK_DEV - CAP

    def one_block(block_seed):
        pick_key, order_key = jax.random.split(block_seed)
        taken = jnp.sort(jax.random.permutation(pick_key, pool)[:needed])
        listing = jnp.concatenate([jnp.full((CAP,), hot, jnp.int32), taken.astype(jnp.int32)])
        table = listing.reshape(2, TOK_DEV).T
        order = jax.random.permutation(order_key, TOK_DEV)
        return table[order]
    seeds = jax.random.split(block_key, block_count)
    return jax.vmap(one_block)(seeds).reshape(block_count * TOK_DEV, 2).astype(jnp.int32)


def set_ends(entries, rng, least, largest):
    index_at = [jax.random.randint(jax.random.fold_in(rng, axis), (), 0, length) for axis, length in enumerate(entries.shape)]
    main_axis = entries.shape.index(max(entries.shape))
    next_to = index_at[:main_axis] + [(index_at[main_axis] + 1) % entries.shape[main_axis]] + index_at[main_axis + 1:]
    return entries.at[tuple(index_at)].set(least).at[tuple(next_to)].set(largest)


def shard_levels(key, dims, pieces, least, high):
    def one(dim, shards_of):
        steps = jax.random.uniform(jax.random.fold_in(jax.random.fold_in(key, 6), dim), (shards_of,), jnp.float32, least / len(pieces), high / len(pieces))
        return jnp.repeat(jnp.exp(steps), dims[dim] // shards_of).reshape((-1,) + (1,) * (len(dims) - dim - 1))

    loudness = one(*pieces[0])
    for cut in pieces[1:]:
        loudness = loudness * one(*cut)
    return loudness


def noise(own_key, dims, deviation, limit, shards=(), kind=jnp.bfloat16):
    level = shard_levels(own_key, dims, shards, -0.22, 0.18) if shards else 1.0
    values = jax.random.normal(own_key, dims, jnp.float32) * deviation * level
    return jnp.minimum(jnp.maximum(values, -limit), limit).astype(kind)


def setup_inputs(seed: int = 0) -> dict:
    arg_keys = jax.random.split(jax.random.key(seed), 9)
    return {
        "tokens": noise(arg_keys[0], (TOKENS, D), 1.0, 6.0, ((0, 8), (1, 32))),
        "router_logits": noise(arg_keys[1], (TOKENS, 2), 1.5, 6.0, ((0, 8),), jnp.float32),
        "routes": draw_routes(jax.random.fold_in(arg_keys[8], 71), 0),
        "loss_weights": set_ends(jax.random.randint(arg_keys[3], (TOKENS,), 1024, 8193), jax.random.fold_in(arg_keys[3], 1), 1024, 8192).astype(jnp.int32),
        "cotangent": noise(arg_keys[4], (TOKENS, D), 1.0, 6.0, ((0, 8), (1, 32))),
        "gate_weight": noise(arg_keys[5], (EXPERTS, D, FF), D ** -0.5, 0.078125, ((0, 8), (2, 32))),
        "up_weight": noise(arg_keys[6], (EXPERTS, D, FF), D ** -0.5, 0.078125, ((0, 8), (2, 32))),
        "down_weight": noise(arg_keys[7], (EXPERTS, FF, D), FF ** -0.5, 0.0625, ((0, 8), (1, 32))),
    }


def expert_pass(rows, grads, gate_part, up_part, down_part):
    gate = jnp.dot(rows, gate_part, preferred_element_type=jnp.float32)
    upward = jnp.dot(rows, up_part, preferred_element_type=jnp.float32)
    sigma = jax.nn.sigmoid(gate)
    active = gate * sigma
    hidden = (active * upward).astype(jnp.bfloat16)
    contract_last = (((1,), (1,)), ((), ()))
    contract_first = (((0,), (0,)), ((), ()))
    hidden_grad = lax.dot_general(grads, down_part, contract_last, preferred_element_type=jnp.float32)
    gate_grad = (hidden_grad * upward * (sigma * (1.0 + gate * (1.0 - sigma)))).astype(jnp.bfloat16)
    up_grad = (hidden_grad * active).astype(jnp.bfloat16)
    group = FF // N_FSDP
    row_count = rows.shape[0]

    def add_group(index, carry):
        out_total, in_total = carry
        start = (index * group).astype(jnp.int32)
        hidden_piece = lax.dynamic_slice_in_dim(hidden, start, group, 1)
        gate_piece = lax.dynamic_slice_in_dim(gate_grad, start, group, 1)
        up_piece = lax.dynamic_slice_in_dim(up_grad, start, group, 1)
        down_rows = lax.dynamic_slice_in_dim(down_part, start, group, 0)
        gate_cols = lax.dynamic_slice_in_dim(gate_part, start, group, 1)
        up_cols = lax.dynamic_slice_in_dim(up_part, start, group, 1)
        part_out = jnp.dot(hidden_piece, down_rows, preferred_element_type=jnp.float32)
        part_in = lax.dot_general(gate_piece, gate_cols, contract_last, preferred_element_type=jnp.float32) + lax.dot_general(up_piece, up_cols, contract_last, preferred_element_type=jnp.float32)
        out_total = out_total + lax.optimization_barrier(part_out.astype(jnp.bfloat16)).astype(jnp.float32)
        in_total = in_total + lax.optimization_barrier(part_in.astype(jnp.bfloat16)).astype(jnp.float32)
        return out_total, in_total

    empty = jnp.zeros((row_count, D), jnp.float32)
    out_total, in_total = lax.fori_loop(0, N_FSDP, add_group, (empty, empty))
    down_grad = lax.dot_general(hidden, grads, contract_first, preferred_element_type=jnp.float32).astype(jnp.bfloat16)
    return out_total.astype(jnp.bfloat16), in_total.astype(jnp.bfloat16), down_grad


def reference(tokens, router_logits, routes, loss_weights, cotangent, gate_weight, up_weight, down_weight):
    share = jax.nn.sigmoid(router_logits[:, 0] - router_logits[:, 1])
    combine = jnp.stack([share, 1.0 - share], axis=1)
    scaled = cotangent.astype(jnp.float32) * (loss_weights.astype(jnp.float32) / 4096.0)[:, None]
    first_grad = (combine[:, 0:1] * scaled).astype(jnp.bfloat16)
    second_grad = (combine[:, 1:2] * scaled).astype(jnp.bfloat16)
    pad_row = jnp.zeros((1, D), jnp.bfloat16)
    padded_tokens = jnp.concatenate([tokens, pad_row], axis=0)
    output_total = jnp.zeros((TOKENS, D), jnp.float32)
    grad_total = jnp.zeros((TOKENS, D), jnp.float32)
    down_grads = []
    for expert in range(EXPERTS):
        first = routes[:, 0] == expert
        second = routes[:, 1] == expert
        named = first | second
        chosen = jnp.nonzero(named, size=SLOTS, fill_value=TOKENS)[0].astype(jnp.int32)
        rows = padded_tokens[chosen]
        token_grads = jnp.where(first[:, None], first_grad, second_grad)
        grads = jnp.concatenate([token_grads, pad_row], axis=0)[chosen]
        expert_out, expert_in, down_part_grad = expert_pass(rows, grads, gate_weight[expert], up_weight[expert], down_weight[expert])
        spread_out = jnp.zeros((TOKENS + 1, D), jnp.float32).at[chosen].set(expert_out.astype(jnp.float32))[:TOKENS]
        spread_in = jnp.zeros((TOKENS + 1, D), jnp.float32).at[chosen].set(expert_in.astype(jnp.float32))[:TOKENS]
        output_total = output_total + jnp.where(first[:, None], combine[:, 0:1] * spread_out, 0.0) + jnp.where(second[:, None], combine[:, 1:2] * spread_out, 0.0)
        grad_total = grad_total + jnp.where(named[:, None], spread_in, 0.0)
        down_grads.append(down_part_grad)
    return output_total.astype(jnp.bfloat16), grad_total.astype(jnp.bfloat16), jnp.stack(down_grads, axis=0)
```

```python
import functools

import jax
import jax.numpy as jnp
from jax import lax
from jax.experimental import pallas as pl
from jax.experimental.pallas import tpu as pltpu
from jax.sharding import PartitionSpec as P

MESH = pl.DeviceIdType.MESH
BF = jnp.bfloat16
F32 = jnp.float32
NX, NY, NZ = 4, 4, 8
FEAT, TOK = 64, 128


def dot(a, b):
    return lax.dot_general(a, b, (((1,), (0,)), ((), ())), preferred_element_type=F32)


def dot_nt(a, b):
    return lax.dot_general(a, b, (((1,), (1,)), ((), ())), preferred_element_type=F32)


class Place:
    def __init__(self):
        seg, fsdp = lax.axis_index("segment"), lax.axis_index("fsdp")
        self.seg = seg
        self.y, self.c = seg // 2, seg % 2
        self.z, self.x = fsdp // NX, fsdp % NX

    def at(self, dx=0, dy=0, dz=0, sibling=False):
        x = (self.x + dx) % NX
        y = (self.y + dy) % NY
        z = (self.z + dz) % NZ
        c = 1 - self.c if sibling else self.c
        return (y * 2 + c, z * NX + x)

    def others(self):
        found = [self.at(sibling=True)]
        found += [self.at(dx=d) for d in range(1, NX)]
        found += [self.at(dy=d) for d in range(1, NY)]
        found += [self.at(dz=d) for d in range(1, NZ)]
        return found


def enter(devices):
    barrier = pltpu.get_barrier_semaphore()
    for device in devices:
        pl.semaphore_signal(barrier, inc=1, device_id=device, device_id_type=MESH)
    return lambda: pl.semaphore_wait(barrier, len(devices))


def a_base(y, z, half):
    return z * 4 + 2 * half


def brick_of(bases, t):
    base = bases[0]
    for k in range(1, len(bases)):
        base = jnp.where(t // 2 == k, bases[k], base)
    return base + t % 2


def weight_of(b):
    in_b = 8 + ((b - 32) // 8) * 2 + b % 2
    in_c = 16 + (((b - 64) // 2) % 4) * 2 + b % 2
    return jnp.where(b < 32, b // 4, jnp.where(b < 64, in_b, in_c))


def row_of(b):
    return jnp.where(b < 32, b % 4, jnp.where(b < 64, ((b - 32) // 2) % 4, (b - 64) // 8))


def mult(value, of):
    return pl.multiple_of(value, of)


class Copies:
    def __init__(self, send, recv):
        self.send, self.recv = send, recv
        self.index = {}
        self.sent = []

    def number(self, key):
        return self.index.setdefault(key, len(self.index))

    def make(self, key, src, dst, device):
        i = self.number(key)
        return pltpu.make_async_remote_copy(
            src_ref=src,
            dst_ref=dst,
            send_sem=self.send.at[i],
            recv_sem=self.recv.at[i],
            device_id=device,
            device_id_type=MESH,
        )

    def start(self, key, src, dst, device):
        copy = self.make(key, src, dst, device)
        copy.start()
        self.sent.append(copy)

    def arrived(self, key, ref, device):
        self.make(key, ref, ref, device).wait_recv()

    def drain(self):
        for copy in self.sent:
            copy.wait_send()


class Gather:
    def __init__(self, name, place, copies, buf):
        self.name, self.at, self.copies, self.buf = name, place, copies, buf

    def key(self, *rest):
        return (self.name,) + rest

    def atoms(self, x, z):
        p = self.at
        low = mult((z % 4) * FEAT, FEAT)
        return (
            self.buf.at[p.c, z * 4 + p.y, pl.ds(mult(x * FEAT, FEAT), FEAT)],
            self.buf.at[p.c, 32 + (x * 4 + p.y) * 2 + z // 4, pl.ds(low, FEAT)],
            self.buf.at[p.c, 64 + (p.y * 4 + x) * 2 + z // 4, pl.ds(low, FEAT)],
        )

    def put_own(self, block_t):
        p = self.at
        low = mult((p.z % 4) * FEAT, FEAT)
        self.buf[p.c, p.z * 4 + p.y, pl.ds(mult(p.x * FEAT, FEAT), FEAT), :] = block_t[0:64]
        self.buf[p.c, 32 + (p.x * 4 + p.y) * 2 + p.z // 4, pl.ds(low, FEAT), :] = block_t[64:128]
        self.buf[p.c, 64 + (p.y * 4 + p.x) * 2 + p.z // 4, pl.ds(low, FEAT), :] = block_t[128:192]

    def send_first(self):
        p = self.at
        a, b, c = self.atoms(p.x, p.z)
        for d in range(1, NX):
            self.copies.start(self.key("a1", d), a, a, p.at(dx=d))
        for d in range(1, NZ):
            self.copies.start(self.key("b1", d), b, b, p.at(dz=d))
            self.copies.start(self.key("c1", d), c, c, p.at(dz=d))

    def wait_first_a(self):
        p = self.at
        for d in range(1, NX):
            a, _, _ = self.atoms((p.x - d) % NX, p.z)
            self.copies.arrived(self.key("a1", d), a, p.at(dx=-d))

    def wait_first_bc(self):
        p = self.at
        for d in range(1, NZ):
            _, b, c = self.atoms(p.x, (p.z - d) % NZ)
            self.copies.arrived(self.key("b1", d), b, p.at(dz=-d))
            self.copies.arrived(self.key("c1", d), c, p.at(dz=-d))

    def second(self, part, d):
        p = self.at
        if part == "a":
            return self.buf.at[p.c, pl.ds(p.z * 4 + (p.y - d) % NY, 1)], p.at(dy=-d)
        if part == "b":
            return self.buf.at[p.c, pl.ds(32 + (p.x * 4 + (p.y - d) % NY) * 2, 2)], p.at(dy=-d)
        return self.buf.at[p.c, pl.ds(64 + (p.y * 4 + (p.x - d) % NX) * 2, 2)], p.at(dx=-d)

    def send_second(self, part):
        p = self.at
        block, _ = self.second(part, 0)
        for d in range(1, 4):
            device = p.at(dx=d) if part == "c" else p.at(dy=d)
            self.copies.start(self.key(part + "2", d), block, block, device)

    def wait_second(self, part):
        for d in range(1, 4):
            block, device = self.second(part, d)
            self.copies.arrived(self.key(part + "2", d), block, device)

    def chunk(self, base):
        return self.buf.at[self.at.c, pl.ds(base, 2)]

    def neighbour(self, part, sign):
        p = self.at
        return {"a": p.at(dz=sign), "b": p.at(dx=sign), "c": p.at(dy=sign)}[part]

    def base(self, part, sign, m):
        p = self.at
        if part == "a":
            z = (p.z - sign * (1 + m // 2)) % NZ
            half = m % 2 if sign > 0 else 1 - m % 2
            return z * 4 + 2 * half
        hop = 1 if m < 4 else 2
        q = m % 4 if sign > 0 else (m + 2) % 4
        if part == "b":
            return 32 + (((p.x - sign * hop) % NX) * 4 + q) * 2
        return 64 + (((p.y - sign * hop) % NY) * 4 + q) * 2

    def own_base(self, part, sign, m):
        p = self.at
        if part == "a":
            return p.z * 4 + 2 * (m % 2 if sign > 0 else 1 - m % 2)
        q = m % 4 if sign > 0 else (m + 2) % 4
        if part == "b":
            return 32 + (p.x * 4 + q) * 2
        return 64 + (p.y * 4 + q) * 2

    def own_span(self, part):
        p = self.at
        if part == "a":
            return self.buf.at[p.c, pl.ds(p.z * 4, 4)]
        if part == "b":
            return self.buf.at[p.c, pl.ds(32 + p.x * 8, 8)]
        return self.buf.at[p.c, pl.ds(64 + p.y * 8, 8)]

    def other_span(self, part):
        p = self.at
        if part == "a":
            return self.buf.at[1 - p.c, pl.ds(p.z * 4, 4)]
        if part == "b":
            return self.buf.at[1 - p.c, pl.ds(32 + p.x * 8, 8)]
        return self.buf.at[1 - p.c, pl.ds(64 + p.y * 8, 8)]

    def start_ring(self, part):
        for m in range(2 if part == "a" else 4):
            for sign in (1, -1):
                ref = self.chunk(self.own_base(part, sign, m))
                self.copies.start(self.key(part, sign, m), ref, ref, self.neighbour(part, sign))
        ref = self.own_span(part)
        self.copies.start(self.key("own", part), ref, ref, self.at.at(sibling=True))

    def messages(self, m):
        return [
            (part, sign)
            for part in ("a", "b", "c")
            if m < (7 if part == "a" else 6)
            for sign in (1, -1)
        ]

    def bases(self, m):
        return [self.base(part, sign, m) for part, sign in self.messages(m)]

    def ring_round(self, m):
        for part, sign in self.messages(m):
            ref = self.chunk(self.base(part, sign, m))
            self.copies.arrived(self.key(part, sign, m), ref, self.neighbour(part, -sign))
            step = 2 if part == "a" else 4
            if m + step < (7 if part == "a" else 6):
                self.copies.start(
                    self.key(part, sign, m + step), ref, ref, self.neighbour(part, sign)
                )
            self.copies.start(self.key("sib", part, sign, m), ref, ref, self.at.at(sibling=True))

    def wait_other(self, m):
        p = self.at
        for part, sign in self.messages(m):
            ref = self.buf.at[1 - p.c, pl.ds(self.base(part, sign, m), 2)]
            self.copies.arrived(self.key("sib", part, sign, m), ref, p.at(sibling=True))

    def wait_other_own(self):
        for part in ("a", "b", "c"):
            self.copies.arrived(
                self.key("own", part), self.other_span(part), self.at.at(sibling=True)
            )

    def multiply(self, weights, total, bricks, count):
        def step(t, carry):
            b = bricks(t)
            row = row_of(b)
            rhs = jnp.concatenate([self.buf[0, b], self.buf[1, b]], axis=1)
            total[row] += dot(weights(weight_of(b)), rhs)
            return carry

        lax.fori_loop(0, count, step, 0)

    def multiply_own(self, weights, total):
        p = self.at

        def bricks(t):
            return jnp.where(
                t < 4,
                p.z * 4 + t,
                jnp.where(t < 12, 32 + p.x * 8 + t - 4, 64 + p.y * 8 + t - 12),
            )

        self.multiply(weights, total, bricks, 20)

    def multiply_round(self, weights, total, m):
        bases = self.bases(m)
        self.multiply(weights, total, lambda t: brick_of(bases, t), 2 * len(bases))


def load_blocks(hbm, part_ref, sem):
    for z in range(NZ):
        pltpu.make_async_copy(hbm.at[z, :, 0], part_ref(z), sem).start()
    for x in range(NX):
        for h in range(2):
            for part, first in ((1, 8), (2, 16)):
                pltpu.make_async_copy(
                    hbm.at[pl.ds(h * 4, 4), x, part], part_ref(first + x * 2 + h), sem
                ).start()


def gather_kernel(
    meta_ref,
    tok_ref,
    cot_ref,
    gate_hbm,
    up_hbm,
    down_hbm,
    hid_ref,
    grads_ref,
    wd_ref,
    dgrad_hbm,
    tok_buf,
    cot_buf,
    wgu,
    wdt,
    flat,
    total,
    hgrad,
    scaled,
    meta,
    wsem,
    osem,
    send,
    recv,
):
    p = Place()
    copies = Copies(send, recv)
    tok = Gather("tok", p, copies, tok_buf)
    cot = Gather("cot", p, copies, cot_buf)
    far = [((p.seg + d) % 8, p.z * NX + p.x) for d in range(1, 8)]
    line = [p.at(dx=d) for d in range(1, NX)] + [p.at(dz=d) for d in range(1, NZ)]
    entered = enter(line + far)

    load_blocks(gate_hbm, lambda w: wgu.at[w, 0], wsem.at[0])
    load_blocks(up_hbm, lambda w: wgu.at[w, 1], wsem.at[0])
    pltpu.make_async_copy(down_hbm, flat, wsem.at[1]).start()

    tok.put_own(tok_ref[...].astype(F32).T.astype(BF))
    cot.put_own(cot_ref[...].astype(F32).T.astype(BF))
    meta[p.seg] = meta_ref[p.seg]
    total[...] = jnp.zeros_like(total)
    hgrad[...] = jnp.zeros_like(hgrad)
    entered()

    tok.send_first()
    for d in range(1, 8):
        copies.start(("meta", d), meta_ref.at[(p.seg + d) % 8], meta.at[p.seg], far[d - 1])

    pltpu.make_async_copy(wgu, wgu, wsem.at[0]).wait()

    def turn_gu(w, carry):
        for k in range(2):
            block = wgu[w, k].reshape(256, 256)
            wgu[w, k] = block.T.reshape(4, 64, 256)
        return carry

    lax.fori_loop(0, 6, turn_gu, 0)
    tok.wait_first_a()
    tok.send_second("a")
    lax.fori_loop(6, 12, turn_gu, 0)
    tok.wait_first_bc()
    tok.send_second("b")
    tok.send_second("c")
    tok.wait_second("a")
    tok.start_ring("a")
    cot.send_first()
    lax.fori_loop(12, 24, turn_gu, 0)
    tok.wait_second("b")
    tok.start_ring("b")
    tok.wait_second("c")
    tok.start_ring("c")
    pltpu.make_async_copy(down_hbm, flat, wsem.at[1]).wait()

    def turn_down(i, carry):
        block = flat[:, pl.ds(mult(i * 384, 384), 384)].T
        z, x = i // 2, (i % 2) * 2
        for k in range(2):
            rows = block[k * 192 : (k + 1) * 192]
            wd_ref[z, x + k] = rows[0:64]
            wd_ref[8 + (x + k) * 2 + z // 4, z % 4] = rows[64:128]
            wd_ref[16 + (x + k) * 2 + z // 4, z % 4] = rows[128:192]
        return carry

    def turn_back(w, carry):
        wdt[w] = wd_ref[w].reshape(256, 256).T
        return carry

    def w_gu(w):
        return wgu[w].reshape(512, 256)

    def w_down(w):
        return wdt[w]

    for m in range(7):
        tok.ring_round(m)
        if m == 0:
            tok.wait_other_own()
            tok.multiply_own(w_gu, total)
        else:
            tok.wait_other(m - 1)
            tok.multiply_round(w_gu, total, m - 1)
        if m == 1:
            cot.wait_first_a()
            cot.send_second("a")
            cot.wait_first_bc()
            cot.send_second("b")
            cot.send_second("c")
            lax.fori_loop(0, 8, turn_down, 0)
        if m == 2:
            lax.fori_loop(8, 16, turn_down, 0)
        if m == 3:
            lax.fori_loop(0, 12, turn_back, 0)
        if m == 4:
            for part in ("a", "b", "c"):
                cot.wait_second(part)
                cot.start_ring(part)
            lax.fori_loop(12, 24, turn_back, 0)
    cot.ring_round(0)
    tok.wait_other(6)
    tok.multiply_round(w_gu, total, 6)
    for d in range(1, 8):
        copies.arrived(("meta", d), meta.at[(p.seg - d) % 8], far[7 - d])

    def activate(i, carry):
        y, r = i // 4, i % 4
        low = mult(r * 64, 64)
        gate = total[y, pl.ds(low, 64)]
        upward = total[y, pl.ds(mult(256 + r * 64, 64), 64)]
        first, second = meta[2 * y], meta[2 * y + 1]
        share = jnp.concatenate([first[0:1], second[0:1]], axis=1)
        scale = jnp.concatenate([first[1:2], second[1:2]], axis=1)
        sigma = jax.nn.sigmoid(gate)
        active = gate * sigma
        hidden = active * upward
        weighted = (hidden * share).astype(BF)
        hid_ref[y, 0, pl.ds(low, 64)] = weighted[:, 0:128]
        hid_ref[y, 1, pl.ds(low, 64)] = weighted[:, 128:256]
        scaled[y, pl.ds(low, 64)] = (hidden * scale).astype(BF)
        total[y, pl.ds(low, 64)] = upward * (sigma * (1.0 + gate * (1.0 - sigma))) * scale
        total[y, pl.ds(mult(256 + r * 64, 64), 64)] = active * scale
        return carry

    lax.fori_loop(0, 16, activate, 0)

    for m in range(7):
        if m > 0:
            cot.ring_round(m)
        if m == 0:
            cot.wait_other_own()
            cot.multiply_own(w_down, hgrad)
        else:
            cot.wait_other(m - 1)
            cot.multiply_round(w_down, hgrad, m - 1)
    cot.wait_other(6)
    cot.multiply_round(w_down, hgrad, 6)

    def backward(i, carry):
        y, r = i // 4, i % 4
        low = mult(r * 64, 64)
        high = mult(256 + r * 64, 64)
        grad = hgrad[y, pl.ds(low, 64)]
        gate_grad = (grad * total[y, pl.ds(low, 64)]).astype(BF)
        up_grad = (grad * total[y, pl.ds(high, 64)]).astype(BF)
        for c in range(2):
            grads_ref[y, c, pl.ds(low, 64)] = gate_grad[:, c * 128 : (c + 1) * 128]
            grads_ref[y, c, pl.ds(high, 64)] = up_grad[:, c * 128 : (c + 1) * 128]
        return carry

    lax.fori_loop(0, 16, backward, 0)

    def weight_grad(i, carry):
        z, x = i // 2, (i % 2) * 2
        low = mult((z % 4) * FEAT, FEAT)
        acc = jnp.zeros((256, 384), F32)
        for y in range(NY):
            halves = []
            for c in range(2):
                rows = []
                for k in range(2):
                    xk = x + k
                    rows.append(cot_buf[c, z * 4 + y, pl.ds(mult(xk * FEAT, FEAT), FEAT), :])
                    rows.append(cot_buf[c, 32 + (xk * 4 + y) * 2 + z // 4, pl.ds(low, FEAT), :])
                    rows.append(cot_buf[c, 64 + (y * 4 + xk) * 2 + z // 4, pl.ds(low, FEAT), :])
                halves.append(jnp.concatenate(rows, axis=0))
            acc += dot_nt(scaled[y], jnp.concatenate(halves, axis=1))
        flat[:, pl.ds(mult(i * 384, 384), 384)] = acc.astype(BF)
        return carry

    lax.fori_loop(0, 16, weight_grad, 0)
    out = pltpu.make_async_copy(flat, dgrad_hbm, osem)
    out.start()
    copies.drain()
    out.wait()


RING = (("a", 1), ("a", -1), ("b", 1), ("b", -1), ("c", 1), ("c", -1))


class Scatter:
    def __init__(self, name, place, copies, lhs, rhs, pairs, ring, stage, bufs):
        self.name, self.at, self.copies = name, place, copies
        self.lhs, self.rhs, self.pairs, self.ring, self.stage = lhs, rhs, pairs, ring, stage
        self.two, self.three_a, self.three_bc, self.sums = bufs

    def key(self, *rest):
        return (self.name,) + rest

    def base(self, part, sign, m):
        p = self.at
        if part == "a":
            hop = 4 - (m + 1) // 2
            half = m % 2 if sign > 0 else 1 - m % 2
            return ((p.z + sign * hop) % NZ) * 4 + 2 * half
        hop = 2 if m < 2 else 1
        q = m % 4 if sign > 0 else (m + 2) % 4
        if part == "b":
            return 32 + (((p.x + sign * hop) % NX) * 4 + q) * 2
        return 64 + (((p.y + sign * hop) % NY) * 4 + q) * 2

    def own(self, part, q):
        p = self.at
        if part == "a":
            return p.z * 4 + 2 * q
        if part == "b":
            return 32 + (p.x * 4 + q) * 2
        return 64 + (p.y * 4 + q) * 2

    def groups(self, j):
        if j < 6:
            return [self.base(part, sign, j) for part, sign in RING]
        if j == 6:
            return [self.base("a", 1, 6), self.base("a", -1, 6)] + [
                self.own(part, q) for part in ("a", "b") for q in range(2)
            ]
        return [self.own("b", 2), self.own("b", 3)] + [self.own("c", q) for q in range(4)]

    def keys(self, j):
        if j < 6:
            return [(part, sign, j) for part, sign in RING]
        if j == 6:
            return [("a", 1, 6), ("a", -1, 6)] + [
                ("own", part, q) for part in ("a", "b") for q in range(2)
            ]
        return [("own", "b", 2), ("own", "b", 3)] + [("own", "c", q) for q in range(4)]

    def product(self, b, c):
        return dot(self.lhs(weight_of(b)), self.rhs(row_of(b), c))

    def hand_over(self, j, slot):
        p = self.at
        bases = self.groups(j)

        def step(t, carry):
            b = brick_of(bases, t)
            self.stage[slot, t] = self.product(b, 1 - p.c).astype(BF)
            return carry

        lax.fori_loop(0, 12, step, 0)
        for k, (key, base) in enumerate(zip(self.keys(j), bases)):
            self.copies.start(
                self.key("sib") + key,
                self.stage.at[slot, pl.ds(2 * k, 2)],
                self.pairs.at[pl.ds(base, 2)],
                p.at(sibling=True),
            )

    def handed(self, key, base):
        self.copies.arrived(
            self.key("sib") + key, self.pairs.at[pl.ds(base, 2)], self.at.at(sibling=True)
        )

    def neighbour(self, part, sign):
        p = self.at
        return {"a": p.at(dz=sign), "b": p.at(dx=sign), "c": p.at(dy=sign)}[part]

    def came(self, k, m):
        part, sign = RING[k]
        self.copies.arrived(
            self.key(part, sign, m), self.ring.at[k, m], self.neighbour(part, -sign)
        )

    def send_round(self, m):
        p = self.at
        for k, (part, sign) in enumerate(RING):
            if m >= (7 if part == "a" else 6):
                continue
            base = self.base(part, sign, m)
            self.handed((part, sign, m), base)
            back = m - (2 if part == "a" else 4)
            if back >= 0:
                self.came(k, back)

            def step(t, carry):
                b = base + t
                value = self.product(b, p.c) + self.pairs[b].astype(F32)
                if back >= 0:
                    value += self.ring[k, back, t].astype(F32)
                self.pairs[b] = value.astype(BF)
                return carry

            lax.fori_loop(0, 2, step, 0)
            self.copies.start(
                self.key(part, sign, m),
                self.pairs.at[pl.ds(base, 2)],
                self.ring.at[k, m],
                self.neighbour(part, sign),
            )

    def finish_ring(self):
        p = self.at
        for part, first, count in (("a", 0, 2), ("b", 2, 4), ("c", 4, 4)):
            for q in range(count):
                base = self.own(part, q)
                self.handed(("own", part, q), base)
                if part == "a":
                    plus, minus = 6 - q, 5 + q
                else:
                    plus, minus = 2 + (q + 2) % 4, 2 + q
                self.came(first, plus)
                self.came(first + 1, minus)

                def step(t, carry):
                    b = base + t
                    value = self.product(b, p.c) + self.pairs[b].astype(F32)
                    value += self.ring[first, plus, t].astype(F32)
                    value += self.ring[first + 1, minus, t].astype(F32)
                    self.pairs[b] = value.astype(BF)
                    return carry

                lax.fori_loop(0, 2, step, 0)

    def second(self, part, d):
        p = self.at
        if part == "a":
            return pl.ds(p.z * 4 + (p.y + d) % NY, 1), pl.ds(0, 1), p.at(dy=d)
        if part == "b":
            return pl.ds(32 + (p.x * 4 + (p.y + d) % NY) * 2, 2), pl.ds(1, 2), p.at(dy=d)
        return pl.ds(64 + (p.y * 4 + (p.x + d) % NX) * 2, 2), pl.ds(3, 2), p.at(dx=d)

    def send_second(self):
        for part in ("a", "b", "c"):
            for d in range(1, 4):
                bricks, slot, device = self.second(part, d)
                self.copies.start(
                    self.key(part + "2", d),
                    self.pairs.at[bricks],
                    self.two.at[d - 1, slot],
                    device,
                )

    def sum_second(self):
        p = self.at
        for part, slots in (("a", (0,)), ("b", (1, 2)), ("c", (3, 4))):
            for d in range(1, 4):
                _, slot, _ = self.second(part, d)
                device = p.at(dx=-d) if part == "c" else p.at(dy=-d)
                self.copies.arrived(self.key(part + "2", d), self.two.at[d - 1, slot], device)
            for t, slot in enumerate(slots):
                mine = {
                    "a": p.z * 4 + p.y,
                    "b": 32 + (p.x * 4 + p.y) * 2 + t,
                    "c": 64 + (p.y * 4 + p.x) * 2 + t,
                }[part]
                value = self.pairs[mine].astype(F32)
                for d in range(3):
                    value += self.two[d, slot].astype(F32)
                self.sums[slot] = value.astype(BF).reshape(4, 64, TOK)
        for d in range(1, NX):
            x = (p.x + d) % NX
            self.copies.start(
                self.key("a3", d), self.sums.at[0, x], self.three_a.at[d - 1], p.at(dx=d)
            )
        for d in range(1, NZ):
            z = (p.z + d) % NZ
            for part, first, i in (("b", 1, 0), ("c", 3, 1)):
                self.copies.start(
                    self.key(part + "3", d),
                    self.sums.at[first + z // 4, z % 4],
                    self.three_bc.at[i, d - 1],
                    p.at(dz=d),
                )

    def sum_third(self, out_ref):
        p = self.at
        rows = [self.sums[0, p.x].astype(F32)]
        for d in range(1, NX):
            self.copies.arrived(self.key("a3", d), self.three_a.at[d - 1], p.at(dx=-d))
            rows[0] += self.three_a[d - 1].astype(F32)
        for part, first, i in (("b", 1, 0), ("c", 3, 1)):
            value = self.sums[first + p.z // 4, p.z % 4].astype(F32)
            for d in range(1, NZ):
                self.copies.arrived(
                    self.key(part + "3", d), self.three_bc.at[i, d - 1], p.at(dz=-d)
                )
                value += self.three_bc[i, d - 1].astype(F32)
            rows.append(value)
        out_ref[...] = jnp.concatenate(rows, axis=0).T.astype(BF)


def scatter_kernel(
    hid_ref,
    grads_ref,
    gate_hbm,
    up_hbm,
    wd_ref,
    out_ref,
    in_ref,
    wgu,
    pairs,
    ring,
    stage,
    two,
    three_a,
    three_bc,
    sums,
    wsem,
    send,
    recv,
):
    p = Place()
    copies = Copies(send, recv)
    entered = enter(p.others())
    load_blocks(gate_hbm, lambda w: wgu.at[0, w], wsem.at[0])
    load_blocks(up_hbm, lambda w: wgu.at[1, w], wsem.at[0])

    def bufs(i):
        return (two.at[i], three_a.at[i], three_bc.at[i], sums.at[i])

    def lhs_in(w):
        return jnp.concatenate(
            [wgu[0, w].reshape(256, 256), wgu[1, w].reshape(256, 256)], axis=1
        )

    out = Scatter(
        "out", p, copies, lambda w: wd_ref[w].reshape(256, 256), lambda y, c: hid_ref[y, c],
        pairs.at[0], ring.at[0], stage, bufs(0),
    )
    inp = Scatter(
        "in", p, copies, lhs_in, lambda y, c: grads_ref[y, c],
        pairs.at[1], ring.at[1], stage, bufs(1),
    )
    entered()

    steps = [(out, j) for j in range(8)] + [(inp, j) for j in range(8)]
    sent = []

    def hand_over(n):
        which, j = steps[n]
        if n >= 2:
            for copy in sent[n - 2]:
                copy.wait_send()
        before = len(copies.sent)
        which.hand_over(j, n % 2)
        sent.append(copies.sent[before:])
        del copies.sent[before:]

    hand_over(0)
    hand_over(1)
    for m in range(7):
        out.send_round(m)
        if m < 6:
            hand_over(m + 2)
    pltpu.make_async_copy(wgu, wgu, wsem.at[0]).wait()
    hand_over(8)
    hand_over(9)
    inp.send_round(0)
    hand_over(10)
    out.finish_ring()
    out.send_second()
    for m in range(1, 7):
        inp.send_round(m)
        if m < 6:
            hand_over(m + 10)
        if m == 2:
            out.sum_second()
        if m == 4:
            out.sum_third(out_ref)
    inp.finish_ring()
    inp.send_second()
    inp.sum_second()
    inp.sum_third(in_ref)
    for group in sent[14:]:
        for copy in group:
            copy.wait_send()
    copies.drain()


def per_device(
    tokens, router_logits, routes, loss_weights, cotangent, gate_weight, up_weight, down_weight
):
    share = jax.nn.sigmoid(router_logits[:, 0] - router_logits[:, 1])
    experts = jnp.arange(8, dtype=jnp.int32)[:, None]
    combine = jnp.where(routes[None, :, 0] == experts, share[None, :], 0.0) + jnp.where(
        routes[None, :, 1] == experts, 1.0 - share[None, :], 0.0
    )
    scale = combine * (loss_weights.astype(F32) / 4096.0)[None, :]
    row = jnp.arange(8)[None, :, None]
    meta = jnp.where(row == 0, combine[:, None, :], jnp.where(row == 1, scale[:, None, :], 0.0))

    gate5 = gate_weight.reshape(NZ, NX, 3, FEAT, 256)
    up5 = up_weight.reshape(NZ, NX, 3, FEAT, 256)
    down2 = down_weight.reshape(256, 6144)
    vmem = pl.BlockSpec(memory_space=pltpu.VMEM)
    hbm = pl.BlockSpec(memory_space=pl.ANY)
    n_gather, n_scatter = 232, 288

    hid, grads, wd, dgrad = pl.pallas_call(
        gather_kernel,
        name="gather_hidden",
        out_shape=(
            jax.ShapeDtypeStruct((NY, 2, 256, TOK), BF),
            jax.ShapeDtypeStruct((NY, 2, 512, TOK), BF),
            jax.ShapeDtypeStruct((24, 4, 64, 256), BF),
            jax.ShapeDtypeStruct((256, 6144), BF),
        ),
        in_specs=[vmem, vmem, vmem, hbm, hbm, hbm],
        out_specs=(vmem, vmem, vmem, hbm),
        scratch_shapes=[
            pltpu.VMEM((2, 96, 256, TOK), BF),
            pltpu.VMEM((2, 96, 256, TOK), BF),
            pltpu.VMEM((24, 2, 4, 64, 256), BF),
            pltpu.VMEM((24, 256, 256), BF),
            pltpu.VMEM((256, 6144), BF),
            pltpu.VMEM((NY, 512, 256), F32),
            pltpu.VMEM((NY, 256, 256), F32),
            pltpu.VMEM((NY, 256, 256), BF),
            pltpu.VMEM((8, 8, TOK), F32),
            pltpu.SemaphoreType.DMA((2,)),
            pltpu.SemaphoreType.DMA,
            pltpu.SemaphoreType.DMA((n_gather,)),
            pltpu.SemaphoreType.DMA((n_gather,)),
        ],
        compiler_params=pltpu.CompilerParams(
            collective_id=1, has_side_effects=True, vmem_limit_bytes=60 * 2**20
        ),
    )(meta, tokens, cotangent, gate5, up5, down2)

    output, input_grad = pl.pallas_call(
        scatter_kernel,
        name="scatter_sums",
        out_shape=(
            jax.ShapeDtypeStruct((TOK, 192), BF),
            jax.ShapeDtypeStruct((TOK, 192), BF),
        ),
        in_specs=[vmem, vmem, hbm, hbm, vmem],
        out_specs=(vmem, vmem),
        scratch_shapes=[
            pltpu.VMEM((2, 24, 4, 64, 256), BF),
            pltpu.VMEM((2, 96, 256, TOK), BF),
            pltpu.VMEM((2, 6, 7, 2, 256, TOK), BF),
            pltpu.VMEM((2, 12, 256, TOK), BF),
            pltpu.VMEM((2, 3, 5, 256, TOK), BF),
            pltpu.VMEM((2, 3, 64, TOK), BF),
            pltpu.VMEM((2, 2, 7, 64, TOK), BF),
            pltpu.VMEM((2, 5, 4, 64, TOK), BF),
            pltpu.SemaphoreType.DMA((1,)),
            pltpu.SemaphoreType.DMA((n_scatter,)),
            pltpu.SemaphoreType.DMA((n_scatter,)),
        ],
        compiler_params=pltpu.CompilerParams(
            collective_id=2, has_side_effects=True, vmem_limit_bytes=60 * 2**20
        ),
    )(hid, grads, gate5, up5, wd)
    return (output, input_grad, dgrad.reshape(1, 256, 6144))


def solution(mesh):
    in_specs = (
        P("segment", "fsdp"),
        P("segment", None),
        P("segment", None),
        P("segment"),
        P("segment", "fsdp"),
        P("segment", None, "fsdp"),
        P("segment", None, "fsdp"),
        P("segment", "fsdp", None),
    )
    out_specs = (P("segment", "fsdp"), P("segment", "fsdp"), P("segment", "fsdp", None))
    return jax.shard_map(
        per_device, mesh=mesh, in_specs=in_specs, out_specs=out_specs, check_vma=False
    )
```

```python
import functools

import jax
import jax.numpy as jnp
from jax import lax
from jax.experimental import pallas as pl
from jax.experimental.pallas import tpu as pltpu
from jax.sharding import PartitionSpec as P

MESH = pl.DeviceIdType.MESH
BF = jnp.bfloat16
F32 = jnp.float32
NX, NY, NZ = 4, 4, 8
SLOTS = 6
FEAT, TOK = 64, 128


def dot(a, b):
    return lax.dot_general(a, b, (((1,), (0,)), ((), ())), preferred_element_type=F32)


def dot_nt(a, b):
    return lax.dot_general(a, b, (((1,), (1,)), ((), ())), preferred_element_type=F32)


class Place:
    def __init__(self):
        seg, fsdp = lax.axis_index("segment"), lax.axis_index("fsdp")
        self.seg = seg
        self.y, self.c = seg // 2, seg % 2
        self.z, self.x = fsdp // NX, fsdp % NX

    def at(self, dx=0, dy=0, dz=0, sibling=False):
        x = (self.x + dx) % NX
        y = (self.y + dy) % NY
        z = (self.z + dz) % NZ
        c = 1 - self.c if sibling else self.c
        return (y * 2 + c, z * NX + x)

    def others(self):
        found = [self.at(sibling=True)]
        found += [self.at(dx=d) for d in range(1, NX)]
        found += [self.at(dy=d) for d in range(1, NY)]
        found += [self.at(dz=d) for d in range(1, NZ)]
        return found


def enter(devices):
    barrier = pltpu.get_barrier_semaphore()
    for device in devices:
        pl.semaphore_signal(barrier, inc=1, device_id=device, device_id_type=MESH)
    return lambda: pl.semaphore_wait(barrier, len(devices))


SIZE = {"a": 1, "b": 2, "c": 2}
PARTS = ("a", "b", "c")


def ring_to(p, part, sign):
    return {"a": p.at(dz=sign), "b": p.at(dx=sign), "c": p.at(dy=sign)}[part]


def gather_order(part, sign):
    hops = 3 if part == "a" else 1
    rows, last = ((0, 1, 3, 2), (0, 1)) if sign > 0 else ((0, 3, 2, 1), (3, 2))
    return [(h, r) for h in range(1, hops + 1) for r in rows] + [(hops + 1, r) for r in last]


def scatter_order(part, sign):
    if part == "a":
        rows, last = ((0, 1, 2, 3), (2, 3)) if sign > 0 else ((2, 3, 0, 1), (0, 1))
        return [(4, r) for r in last] + [(h, r) for h in (3, 2, 1) for r in rows]
    rows, last = ((1, 2, 3, 0), (2, 0)) if sign > 0 else ((2, 1, 3, 0), (1, 3))
    return [(2, r) for r in last] + [(1, r) for r in rows]


def weight_of(b):
    in_b = 8 + ((b - 32) // 8) * 2 + b % 2
    in_c = 16 + (((b - 64) // 2) % 4) * 2 + b % 2
    return jnp.where(b < 32, b // 4, jnp.where(b < 64, in_b, in_c))


def row_of(b):
    return jnp.where(b < 32, b % 4, jnp.where(b < 64, ((b - 32) // 2) % 4, (b - 64) // 8))


def mult(value, of):
    return pl.multiple_of(value, of)


class Copies:
    def __init__(self, send, recv):
        self.send, self.recv = send, recv
        self.index = {}
        self.sent = []

    def number(self, key):
        return self.index.setdefault(key, len(self.index))

    def make(self, key, src, dst, device):
        i = self.number(key)
        return pltpu.make_async_remote_copy(
            src_ref=src,
            dst_ref=dst,
            send_sem=self.send.at[i],
            recv_sem=self.recv.at[i],
            device_id=device,
            device_id_type=MESH,
        )

    def start(self, key, src, dst, device):
        copy = self.make(key, src, dst, device)
        copy.start()
        self.sent.append(copy)

    def arrived(self, key, ref, device):
        self.make(key, ref, ref, device).wait_recv()

    def drain(self):
        for copy in self.sent:
            copy.wait_send()


class Gather:
    def __init__(self, name, place, copies, buf):
        self.name, self.at, self.copies, self.buf = name, place, copies, buf

    def key(self, *rest):
        return (self.name,) + rest

    def atoms(self, x, z):
        p = self.at
        low = mult((z % 4) * FEAT, FEAT)
        return (
            self.buf.at[p.c, z * 4 + p.y, pl.ds(mult(x * FEAT, FEAT), FEAT)],
            self.buf.at[p.c, 32 + (x * 4 + p.y) * 2 + z // 4, pl.ds(low, FEAT)],
            self.buf.at[p.c, 64 + (p.y * 4 + x) * 2 + z // 4, pl.ds(low, FEAT)],
        )

    def put_own(self, block_t):
        p = self.at
        low = mult((p.z % 4) * FEAT, FEAT)
        self.buf[p.c, p.z * 4 + p.y, pl.ds(mult(p.x * FEAT, FEAT), FEAT), :] = block_t[0:64]
        self.buf[p.c, 32 + (p.x * 4 + p.y) * 2 + p.z // 4, pl.ds(low, FEAT), :] = block_t[64:128]
        self.buf[p.c, 64 + (p.y * 4 + p.x) * 2 + p.z // 4, pl.ds(low, FEAT), :] = block_t[128:192]

    def send_first(self):
        p = self.at
        a, b, c = self.atoms(p.x, p.z)
        for d in range(1, NX):
            self.copies.start(self.key("a1", d), a, a, p.at(dx=d))
        for d in range(1, NZ):
            self.copies.start(self.key("b1", d), b, b, p.at(dz=d))
            self.copies.start(self.key("c1", d), c, c, p.at(dz=d))

    def wait_first_a(self):
        p = self.at
        for d in range(1, NX):
            a, _, _ = self.atoms((p.x - d) % NX, p.z)
            self.copies.arrived(self.key("a1", d), a, p.at(dx=-d))

    def wait_first_bc(self):
        p = self.at
        for d in range(1, NZ):
            _, b, c = self.atoms(p.x, (p.z - d) % NZ)
            self.copies.arrived(self.key("b1", d), b, p.at(dz=-d))
            self.copies.arrived(self.key("c1", d), c, p.at(dz=-d))

    def second(self, part, d):
        p = self.at
        if part == "a":
            return self.buf.at[p.c, pl.ds(p.z * 4 + (p.y - d) % NY, 1)], p.at(dy=-d)
        if part == "b":
            return self.buf.at[p.c, pl.ds(32 + (p.x * 4 + (p.y - d) % NY) * 2, 2)], p.at(dy=-d)
        return self.buf.at[p.c, pl.ds(64 + (p.y * 4 + (p.x - d) % NX) * 2, 2)], p.at(dx=-d)

    def send_second(self, part):
        p = self.at
        block, _ = self.second(part, 0)
        for d in range(1, 4):
            device = p.at(dx=d) if part == "c" else p.at(dy=d)
            self.copies.start(self.key(part + "2", d), block, block, device)

    def wait_second(self, part):
        for d in range(1, 4):
            block, device = self.second(part, d)
            self.copies.arrived(self.key(part + "2", d), block, device)

    def chunk(self, part, base):
        return self.buf.at[self.at.c, pl.ds(base, SIZE[part])]

    def base(self, part, back, rel):
        p = self.at
        if part == "a":
            return ((p.z - back) % NZ) * 4 + (p.y + rel) % NY
        if part == "b":
            return 32 + (((p.x - back) % NX) * 4 + (p.y + rel) % NY) * 2
        return 64 + (((p.y - back) % NY) * 4 + (p.x + rel) % NX) * 2

    def span(self, part, c):
        p = self.at
        first, count = {
            "a": (p.z * 4, 4), "b": (32 + p.x * 8, 8), "c": (64 + p.y * 8, 8)
        }[part]
        return self.buf.at[c, pl.ds(first, count)]

    def send_own(self, part, rels):
        for rel in rels:
            ref = self.chunk(part, self.base(part, 0, rel))
            for sign in (1, -1):
                self.copies.start(self.key(part, sign, 1, rel), ref, ref, ring_to(self.at, part, sign))

    def finish_second(self, part):
        for rel in (1, 3, 2):
            d = (4 - rel) % 4
            block, device = self.second(part, d)
            self.copies.arrived(self.key(part + "2", d), block, device)
            self.send_own(part, (rel,))
        ref = self.span(part, self.at.c)
        self.copies.start(self.key("own", part), ref, ref, self.at.at(sibling=True))

    def messages(self, s):
        found = [("a", sign) + gather_order("a", sign)[s] for sign in (1, -1)]
        part, n = ("b", "c")[s % 2], s // 2
        if n < 6:
            found += [(part, sign) + gather_order(part, sign)[n] for sign in (1, -1)]
        return found

    def ring_round(self, s):
        for part, sign, hop, rel in self.messages(s):
            ref = self.chunk(part, self.base(part, sign * hop, rel))
            self.copies.arrived(self.key(part, sign, hop, rel), ref, ring_to(self.at, part, -sign))
            if (hop + 1, rel) in gather_order(part, sign):
                self.copies.start(
                    self.key(part, sign, hop + 1, rel), ref, ref, ring_to(self.at, part, sign)
                )
            self.copies.start(
                self.key("sib", part, sign, hop, rel), ref, ref, self.at.at(sibling=True)
            )

    def wait_other(self, s):
        p = self.at
        for part, sign, hop, rel in self.messages(s):
            ref = self.buf.at[1 - p.c, pl.ds(self.base(part, sign * hop, rel), SIZE[part])]
            self.copies.arrived(self.key("sib", part, sign, hop, rel), ref, p.at(sibling=True))

    def wait_other_own(self):
        for part in ("a", "b", "c"):
            self.copies.arrived(
                self.key("own", part), self.span(part, 1 - self.at.c), self.at.at(sibling=True)
            )

    def both(self, b):
        return jnp.concatenate([self.buf[0, b], self.buf[1, b]], axis=1)

    def multiply_single(self, weights, total, b):
        total[b % 4] += dot(weights(b // 4), self.both(b))

    def multiply_chunk(self, weights, total, b):
        w = weight_of(b)
        rhs = jnp.concatenate([self.both(b), self.both(b + 1)], axis=0)
        total[row_of(b)] += dot(jnp.concatenate([weights(w), weights(w + 1)], axis=1), rhs)

    def multiply_own(self, weights, total):
        p = self.at

        def step(t, carry):
            self.multiply_single(weights, total, p.z * 4 + t)
            self.multiply_chunk(weights, total, 32 + p.x * 8 + 2 * t)
            self.multiply_chunk(weights, total, 64 + p.y * 8 + 2 * t)
            return carry

        lax.fori_loop(0, 4, step, 0)

    def multiply_round(self, weights, total, s):
        bases = [self.base(part, sign * hop, rel) for part, sign, hop, rel in self.messages(s)]

        def step(t, carry):
            self.multiply_single(weights, total, jnp.where(t == 0, bases[0], bases[1]))
            if len(bases) > 2:
                self.multiply_chunk(weights, total, jnp.where(t == 0, bases[2], bases[3]))
            return carry

        lax.fori_loop(0, 2, step, 0)


def load_blocks(hbm, part_ref, sem):
    for z in range(NZ):
        pltpu.make_async_copy(hbm.at[z, :, 0], part_ref(z), sem).start()
    for x in range(NX):
        for h in range(2):
            for part, first in ((1, 8), (2, 16)):
                pltpu.make_async_copy(
                    hbm.at[pl.ds(h * 4, 4), x, part], part_ref(first + x * 2 + h), sem
                ).start()


def gather_kernel(
    meta_ref,
    tok_ref,
    cot_ref,
    gate_hbm,
    up_hbm,
    down_hbm,
    hid_ref,
    grads_ref,
    wd_ref,
    dgrad_hbm,
    tok_buf,
    cot_buf,
    wgu,
    wdt,
    flat,
    total,
    hgrad,
    scaled,
    meta,
    wsem,
    osem,
    send,
    recv,
):
    p = Place()
    copies = Copies(send, recv)
    tok = Gather("tok", p, copies, tok_buf)
    cot = Gather("cot", p, copies, cot_buf)
    far = [((p.seg + d) % 8, p.z * NX + p.x) for d in range(1, 8)]
    line = [p.at(dx=d) for d in range(1, NX)] + [p.at(dz=d) for d in range(1, NZ)]
    entered = enter(line + far)

    load_blocks(gate_hbm, lambda w: wgu.at[w, 0], wsem.at[0])
    load_blocks(up_hbm, lambda w: wgu.at[w, 1], wsem.at[0])
    pltpu.make_async_copy(down_hbm, flat, wsem.at[1]).start()

    tok.put_own(tok_ref)
    cot.put_own(cot_ref)
    meta[p.seg] = meta_ref[p.seg]
    total[...] = jnp.zeros_like(total)
    hgrad[...] = jnp.zeros_like(hgrad)
    entered()

    tok.send_first()
    for d in range(1, 8):
        copies.start(("meta", d), meta_ref.at[(p.seg + d) % 8], meta.at[p.seg], far[d - 1])

    def turn_gu(w, carry):
        for k in range(2):
            block = wgu[w, k].reshape(256, 256)
            wgu[w, k] = block.T.reshape(4, 64, 256)
        return carry

    def turn_down(i, carry):
        block = flat[:, pl.ds(mult(i * 384, 384), 384)].T
        z, x = i // 2, (i % 2) * 2
        for k in range(2):
            rows = block[k * 192 : (k + 1) * 192]
            wd_ref[z, x + k] = rows[0:64]
            wd_ref[8 + (x + k) * 2 + z // 4, z % 4] = rows[64:128]
            wd_ref[16 + (x + k) * 2 + z // 4, z % 4] = rows[128:192]
        return carry

    def turn_back(w, carry):
        wdt[w] = wd_ref[w].reshape(256, 256).T
        return carry

    def w_gu(w):
        return wgu[w].reshape(512, 256)

    def w_down(w):
        return wdt[w]

    tok.wait_first_a()
    tok.send_own("a", (0,))
    tok.send_second("a")
    pltpu.make_async_copy(wgu, wgu, wsem.at[0]).wait()
    lax.fori_loop(0, 4, turn_gu, 0)
    tok.finish_second("a")
    tok.wait_first_bc()
    tok.send_own("b", (0,))
    tok.send_own("c", (0,))
    tok.send_second("b")
    tok.send_second("c")
    cot.send_first()
    lax.fori_loop(4, 8, turn_gu, 0)
    lax.fori_loop(8, 14, turn_gu, 0)
    tok.finish_second("b")
    tok.finish_second("c")
    lax.fori_loop(14, 24, turn_gu, 0)
    pltpu.make_async_copy(down_hbm, flat, wsem.at[1]).wait()

    for s in range(14):
        tok.ring_round(s)
        if s == 0:
            tok.wait_other_own()
            tok.multiply_own(w_gu, total)
        else:
            tok.wait_other(s - 1)
            tok.multiply_round(w_gu, total, s - 1)
        if s == 2:
            cot.wait_first_a()
            cot.send_second("a")
            cot.wait_first_bc()
            cot.send_second("b")
            cot.send_second("c")
        if 3 <= s < 7:
            lax.fori_loop(4 * s - 12, 4 * s - 8, turn_down, 0)
        if 7 <= s < 10:
            lax.fori_loop(8 * s - 56, 8 * s - 48, turn_back, 0)
        if s == 6:
            cot.send_own("b", (0,))
            cot.finish_second("b")
            cot.send_own("c", (0,))
            cot.finish_second("c")
        if s == 9:
            cot.send_own("a", (0,))
            cot.finish_second("a")
    cot.ring_round(0)
    tok.wait_other(13)
    tok.multiply_round(w_gu, total, 13)
    for d in range(1, 8):
        copies.arrived(("meta", d), meta.at[(p.seg - d) % 8], far[7 - d])

    def activate(i, carry):
        y, r = i // 4, i % 4
        low = mult(r * 64, 64)
        gate = total[y, pl.ds(low, 64)]
        upward = total[y, pl.ds(mult(256 + r * 64, 64), 64)]
        first, second = meta[2 * y], meta[2 * y + 1]
        share = jnp.concatenate([first[0:1], second[0:1]], axis=1)
        scale = jnp.concatenate([first[1:2], second[1:2]], axis=1)
        sigma = jax.nn.sigmoid(gate)
        active = gate * sigma
        hidden = active * upward
        weighted = (hidden * share).astype(BF)
        hid_ref[y, 0, pl.ds(low, 64)] = weighted[:, 0:128]
        hid_ref[y, 1, pl.ds(low, 64)] = weighted[:, 128:256]
        scaled[y, pl.ds(low, 64)] = (hidden * scale).astype(BF)
        total[y, pl.ds(low, 64)] = upward * (sigma * (1.0 + gate * (1.0 - sigma))) * scale
        total[y, pl.ds(mult(256 + r * 64, 64), 64)] = active * scale
        return carry

    lax.fori_loop(0, 16, activate, 0)

    for s in range(14):
        if s > 0:
            cot.ring_round(s)
        if s == 0:
            cot.wait_other_own()
            cot.multiply_own(w_down, hgrad)
        else:
            cot.wait_other(s - 1)
            cot.multiply_round(w_down, hgrad, s - 1)
    cot.wait_other(13)
    cot.multiply_round(w_down, hgrad, 13)

    def backward(i, carry):
        y, r = i // 4, i % 4
        low = mult(r * 64, 64)
        high = mult(256 + r * 64, 64)
        grad = hgrad[y, pl.ds(low, 64)]
        gate_grad = (grad * total[y, pl.ds(low, 64)]).astype(BF)
        up_grad = (grad * total[y, pl.ds(high, 64)]).astype(BF)
        for c in range(2):
            grads_ref[y, c, pl.ds(low, 64)] = gate_grad[:, c * 128 : (c + 1) * 128]
            grads_ref[y, c, pl.ds(high, 64)] = up_grad[:, c * 128 : (c + 1) * 128]
        return carry

    lax.fori_loop(0, 16, backward, 0)

    def weight_grad(i, carry):
        z, x = i // 2, (i % 2) * 2
        low = mult((z % 4) * FEAT, FEAT)
        acc = jnp.zeros((256, 384), F32)
        for y in range(NY):
            halves = []
            for c in range(2):
                rows = []
                for k in range(2):
                    xk = x + k
                    rows.append(cot_buf[c, z * 4 + y, pl.ds(mult(xk * FEAT, FEAT), FEAT), :])
                    rows.append(cot_buf[c, 32 + (xk * 4 + y) * 2 + z // 4, pl.ds(low, FEAT), :])
                    rows.append(cot_buf[c, 64 + (y * 4 + xk) * 2 + z // 4, pl.ds(low, FEAT), :])
                halves.append(jnp.concatenate(rows, axis=0))
            acc += dot_nt(scaled[y], jnp.concatenate(halves, axis=1))
        flat[:, pl.ds(mult(i * 384, 384), 384)] = acc.astype(BF)
        return carry

    lax.fori_loop(0, 16, weight_grad, 0)
    out = pltpu.make_async_copy(flat, dgrad_hbm, osem)
    out.start()
    copies.drain()
    out.wait()


class Scatter:
    def __init__(
        self, name, first, place, copies, lhs, rhs, pairs, ring_a, ring_bc, mine, stage, bufs
    ):
        self.name, self.first, self.at, self.copies = name, first, place, copies
        self.lhs, self.rhs, self.pairs = lhs, rhs, pairs
        self.ring_a, self.ring_bc, self.mine, self.stage = ring_a, ring_bc, mine, stage
        self.two, self.three_a, self.three_bc, self.sums = bufs

    def key(self, *rest):
        return (self.name,) + rest

    def base(self, part, ahead, rel):
        p = self.at
        if part == "a":
            return ((p.z + ahead) % NZ) * 4 + (p.y + rel) % NY
        if part == "b":
            return 32 + (((p.x + ahead) % NX) * 4 + (p.y + rel) % NY) * 2
        return 64 + (((p.y + ahead) % NY) * 4 + (p.x + rel) % NX) * 2

    def chunks(self, j):
        found = []
        for i, sign in enumerate((1, -1)):
            if j < 14:
                found.append(("a", sign) + scatter_order("a", sign)[j])
            else:
                found.append(("a", 0, 0, ((1, 2), (3, 0))[j - 14][i]))
        part, n = ("b", "c")[j % 2], j // 2
        for i, sign in enumerate((1, -1)):
            if n < 6:
                found.append((part, sign) + scatter_order(part, sign)[n])
            else:
                found.append((part, 0, 0, ((1, 2), (3, 0))[n - 6][i]))
        return found

    def place_of(self, chunk):
        for j in range(16):
            chunks = self.chunks(j)
            if chunk in chunks:
                k = chunks.index(chunk)
                return (self.first + j) % SLOTS, (0, 1, 2, 4)[k]

    def produce(self, j):
        p = self.at
        slot = (self.first + j) % SLOTS
        chunks = self.chunks(j)
        bases = [self.base(part, sign * hop, rel) for part, sign, hop, rel in chunks]

        def one(w, rhs, at):
            value = dot(self.lhs(w), rhs).astype(BF)
            self.mine[slot, at] = value[:, 0:TOK]
            self.stage[slot, at] = value[:, TOK:]

        def rhs_of(row):
            return jnp.concatenate([self.rhs(row, p.c), self.rhs(row, 1 - p.c)], axis=1)

        def step(t, carry):
            b = jnp.where(t == 0, bases[0], bases[1])
            one(b // 4, rhs_of(b % 4), t)
            b = jnp.where(t == 0, bases[2], bases[3])
            w, rhs = weight_of(b), rhs_of(row_of(b))
            one(w, rhs, 2 + 2 * t)
            one(w + 1, rhs, 3 + 2 * t)
            return carry

        lax.fori_loop(0, 2, step, 0)
        for chunk, base in zip(chunks, bases):
            _, at = self.place_of(chunk)
            size = SIZE[chunk[0]]
            self.copies.start(
                self.key("sib") + chunk,
                self.stage.at[slot, pl.ds(at, size)],
                self.pairs.at[pl.ds(base, size)],
                p.at(sibling=True),
            )

    def landing(self, part, sign, i):
        side = 0 if sign > 0 else 1
        if part == "a":
            return self.ring_a.at[side, pl.ds(i, 1)]
        return self.ring_bc.at[("b", "c").index(part), side, pl.ds(2 * i, 2)]

    def came(self, part, sign, i):
        ref = self.landing(part, sign, i)
        self.copies.arrived(self.key(part, sign, i), ref, ring_to(self.at, part, -sign))
        return ref

    def gather_up(self, chunk, base, arrivals):
        part = chunk[0]
        size = SIZE[part]
        ref = self.pairs.at[pl.ds(base, size)]
        self.copies.arrived(self.key("sib") + chunk, ref, self.at.at(sibling=True))
        slot, at = self.place_of(chunk)
        refs = [self.came(part, sign, i) for sign, i in arrivals]
        for t in range(size):
            value = self.mine[slot, at + t].astype(F32) + self.pairs[base + t].astype(F32)
            for came in refs:
                value += came[t].astype(F32)
            self.pairs[base + t] = value.astype(BF)
        return ref

    def send_round(self, s):
        for chunk in self.chunks(s):
            part, sign, hop, rel = chunk
            if sign == 0:
                continue
            order = scatter_order(part, sign)
            arrivals = [(sign, order.index((hop + 1, rel)))] if (hop + 1, rel) in order else []
            i = order.index((hop, rel))
            ref = self.gather_up(chunk, self.base(part, sign * hop, rel), arrivals)
            self.copies.start(
                self.key(part, sign, i), ref, self.landing(part, sign, i), ring_to(self.at, part, sign)
            )

    def finish_ring(self, part, rels):
        for rel in rels:
            arrivals = [(sign, scatter_order(part, sign).index((1, rel))) for sign in (1, -1)]
            self.gather_up((part, 0, 0, rel), self.base(part, 0, rel), arrivals)
            if rel:
                bricks, slot, device = self.second(part, rel)
                self.copies.start(
                    self.key(part + "2", rel),
                    self.pairs.at[bricks],
                    self.two.at[rel - 1, slot],
                    device,
                )

    def second(self, part, d):
        p = self.at
        if part == "a":
            return pl.ds(p.z * 4 + (p.y + d) % NY, 1), pl.ds(0, 1), p.at(dy=d)
        if part == "b":
            return pl.ds(32 + (p.x * 4 + (p.y + d) % NY) * 2, 2), pl.ds(1, 2), p.at(dy=d)
        return pl.ds(64 + (p.y * 4 + (p.x + d) % NX) * 2, 2), pl.ds(3, 2), p.at(dx=d)

    def sum_second(self):
        p = self.at
        for part, slots in (("a", (0,)), ("b", (1, 2)), ("c", (3, 4))):
            for d in range(1, 4):
                _, slot, _ = self.second(part, d)
                device = p.at(dx=-d) if part == "c" else p.at(dy=-d)
                self.copies.arrived(self.key(part + "2", d), self.two.at[d - 1, slot], device)
            for t, slot in enumerate(slots):
                mine = {
                    "a": p.z * 4 + p.y,
                    "b": 32 + (p.x * 4 + p.y) * 2 + t,
                    "c": 64 + (p.y * 4 + p.x) * 2 + t,
                }[part]
                value = self.pairs[mine].astype(F32)
                for d in range(3):
                    value += self.two[d, slot].astype(F32)
                self.sums[slot] = value.astype(BF).reshape(4, 64, TOK)
        for d in range(1, NX):
            x = (p.x + d) % NX
            self.copies.start(
                self.key("a3", d), self.sums.at[0, x], self.three_a.at[d - 1], p.at(dx=d)
            )
        for d in range(1, NZ):
            z = (p.z + d) % NZ
            for part, first, i in (("b", 1, 0), ("c", 3, 1)):
                self.copies.start(
                    self.key(part + "3", d),
                    self.sums.at[first + z // 4, z % 4],
                    self.three_bc.at[i, d - 1],
                    p.at(dz=d),
                )

    def sum_third(self, out_ref):
        p = self.at
        rows = [self.sums[0, p.x].astype(F32)]
        for d in range(1, NX):
            self.copies.arrived(self.key("a3", d), self.three_a.at[d - 1], p.at(dx=-d))
            rows[0] += self.three_a[d - 1].astype(F32)
        for part, first, i in (("b", 1, 0), ("c", 3, 1)):
            value = self.sums[first + p.z // 4, p.z % 4].astype(F32)
            for d in range(1, NZ):
                self.copies.arrived(
                    self.key(part + "3", d), self.three_bc.at[i, d - 1], p.at(dz=-d)
                )
                value += self.three_bc[i, d - 1].astype(F32)
            rows.append(value)
        for k in range(3):
            out_ref[k * FEAT : (k + 1) * FEAT] = rows[k].astype(BF)


def scatter_kernel(
    hid_ref,
    grads_ref,
    gate_hbm,
    up_hbm,
    wd_ref,
    out_ref,
    in_ref,
    wgu,
    pairs,
    ring_a,
    ring_bc,
    mine,
    stage,
    two,
    three_a,
    three_bc,
    sums,
    wsem,
    send,
    recv,
):
    p = Place()
    copies = Copies(send, recv)
    entered = enter(p.others())
    load_blocks(gate_hbm, lambda w: wgu.at[0, w], wsem.at[0])
    load_blocks(up_hbm, lambda w: wgu.at[1, w], wsem.at[0])

    def bufs(i):
        return (two.at[i], three_a.at[i], three_bc.at[i], sums.at[i])

    def lhs_in(w):
        return jnp.concatenate(
            [wgu[0, w].reshape(256, 256), wgu[1, w].reshape(256, 256)], axis=1
        )

    out = Scatter(
        "out", 0, p, copies, lambda w: wd_ref[w].reshape(256, 256), lambda y, c: hid_ref[y, c],
        pairs.at[0], ring_a.at[0], ring_bc.at[0], mine, stage, bufs(0),
    )
    inp = Scatter(
        "in", 16, p, copies, lhs_in, lambda y, c: grads_ref[y, c],
        pairs.at[1], ring_a.at[1], ring_bc.at[1], mine, stage, bufs(1),
    )
    entered()

    steps = [(out, j) for j in range(16)] + [(inp, j) for j in range(16)]
    sent = []

    def produce(n):
        which, j = steps[n]
        if n >= SLOTS:
            for copy in sent[n - SLOTS]:
                copy.wait_send()
        before = len(copies.sent)
        which.produce(j)
        sent.append(copies.sent[before:])
        del copies.sent[before:]

    for n in range(2):
        produce(n)
    for s in range(14):
        out.send_round(s)
        produce(s + 2)
        if s == 12:
            out.finish_ring("b", (1, 2))
        if s == 13:
            out.finish_ring("c", (1, 2))
    pltpu.make_async_copy(wgu, wgu, wsem.at[0]).wait()
    produce(16)
    inp.send_round(0)
    produce(17)
    inp.send_round(1)
    out.finish_ring("a", (1, 2))
    out.finish_ring("b", (3, 0))
    produce(18)
    inp.send_round(2)
    out.finish_ring("a", (3, 0))
    out.finish_ring("c", (3, 0))
    produce(19)
    for s in range(3, 14):
        inp.send_round(s)
        produce(s + 17)
        if s == 4:
            out.sum_second()
        if s == 7:
            out.sum_third(out_ref)
        if s == 12:
            inp.finish_ring("b", (1, 2))
        if s == 13:
            inp.finish_ring("c", (1, 2))
    produce(31)
    inp.finish_ring("b", (3, 0))
    inp.finish_ring("c", (3, 0))
    inp.finish_ring("a", (1, 2, 3, 0))
    inp.sum_second()
    inp.sum_third(in_ref)
    for group in sent[32 - SLOTS :]:
        for copy in group:
            copy.wait_send()
    copies.drain()


def per_device(
    tokens, router_logits, routes, loss_weights, cotangent, gate_weight, up_weight, down_weight
):
    share = jax.nn.sigmoid(router_logits[:, 0] - router_logits[:, 1])
    experts = jnp.arange(8, dtype=jnp.int32)[:, None]
    combine = jnp.where(routes[None, :, 0] == experts, share[None, :], 0.0) + jnp.where(
        routes[None, :, 1] == experts, 1.0 - share[None, :], 0.0
    )
    scale = combine * (loss_weights.astype(F32) / 4096.0)[None, :]
    row = jnp.arange(8)[None, :, None]
    meta = jnp.where(row == 0, combine[:, None, :], jnp.where(row == 1, scale[:, None, :], 0.0))

    gate5 = gate_weight.reshape(NZ, NX, 3, FEAT, 256)
    up5 = up_weight.reshape(NZ, NX, 3, FEAT, 256)
    down2 = down_weight.reshape(256, 6144)
    vmem = pl.BlockSpec(memory_space=pltpu.VMEM)
    hbm = pl.BlockSpec(memory_space=pl.ANY)
    n_gather, n_scatter = 288, 288

    hid, grads, wd, dgrad = pl.pallas_call(
        gather_kernel,
        name="gather_hidden",
        out_shape=(
            jax.ShapeDtypeStruct((NY, 2, 256, TOK), BF),
            jax.ShapeDtypeStruct((NY, 2, 512, TOK), BF),
            jax.ShapeDtypeStruct((24, 4, 64, 256), BF),
            jax.ShapeDtypeStruct((256, 6144), BF),
        ),
        in_specs=[vmem, vmem, vmem, hbm, hbm, hbm],
        out_specs=(vmem, vmem, vmem, hbm),
        scratch_shapes=[
            pltpu.VMEM((2, 96, 256, TOK), BF),
            pltpu.VMEM((2, 96, 256, TOK), BF),
            pltpu.VMEM((24, 2, 4, 64, 256), BF),
            pltpu.VMEM((24, 256, 256), BF),
            pltpu.VMEM((256, 6144), BF),
            pltpu.VMEM((NY, 512, 256), F32),
            pltpu.VMEM((NY, 256, 256), F32),
            pltpu.VMEM((NY, 256, 256), BF),
            pltpu.VMEM((8, 8, TOK), F32),
            pltpu.SemaphoreType.DMA((2,)),
            pltpu.SemaphoreType.DMA,
            pltpu.SemaphoreType.DMA((n_gather,)),
            pltpu.SemaphoreType.DMA((n_gather,)),
        ],
        compiler_params=pltpu.CompilerParams(
            collective_id=1, has_side_effects=True, vmem_limit_bytes=60 * 2**20
        ),
    )(meta, tokens.T, cotangent.T, gate5, up5, down2)

    output, input_grad = pl.pallas_call(
        scatter_kernel,
        name="scatter_sums",
        out_shape=(
            jax.ShapeDtypeStruct((192, TOK), BF),
            jax.ShapeDtypeStruct((192, TOK), BF),
        ),
        in_specs=[vmem, vmem, hbm, hbm, vmem],
        out_specs=(vmem, vmem),
        scratch_shapes=[
            pltpu.VMEM((2, 24, 4, 64, 256), BF),
            pltpu.VMEM((2, 96, 256, TOK), BF),
            pltpu.VMEM((2, 2, 14, 256, TOK), BF),
            pltpu.VMEM((2, 2, 2, 12, 256, TOK), BF),
            pltpu.VMEM((SLOTS, 6, 256, TOK), BF),
            pltpu.VMEM((SLOTS, 6, 256, TOK), BF),
            pltpu.VMEM((2, 3, 5, 256, TOK), BF),
            pltpu.VMEM((2, 3, 64, TOK), BF),
            pltpu.VMEM((2, 2, 7, 64, TOK), BF),
            pltpu.VMEM((2, 5, 4, 64, TOK), BF),
            pltpu.SemaphoreType.DMA((1,)),
            pltpu.SemaphoreType.DMA((n_scatter,)),
            pltpu.SemaphoreType.DMA((n_scatter,)),
        ],
        compiler_params=pltpu.CompilerParams(
            collective_id=2, has_side_effects=True, vmem_limit_bytes=60 * 2**20
        ),
    )(hid, grads, gate5, up5, wd)
    return (output.T, input_grad.T, dgrad.reshape(1, 256, 6144))


def solution(mesh):
    in_specs = (
        P("segment", "fsdp"),
        P("segment", None),
        P("segment", None),
        P("segment"),
        P("segment", "fsdp"),
        P("segment", None, "fsdp"),
        P("segment", None, "fsdp"),
        P("segment", "fsdp", None),
    )
    out_specs = (P("segment", "fsdp"), P("segment", "fsdp"), P("segment", "fsdp", None))
    return jax.shard_map(
        per_device, mesh=mesh, in_specs=in_specs, out_specs=out_specs, check_vma=False
    )
```

```python
import functools

import jax
import jax.numpy as jnp
from jax import lax
from jax.experimental import pallas as pl
from jax.experimental.pallas import tpu as pltpu
from jax.sharding import PartitionSpec as P

MESH = pl.DeviceIdType.MESH
BF = jnp.bfloat16
F32 = jnp.float32
NX, NY, NZ = 4, 4, 8
SLOTS = 4
FEAT, TOK = 64, 128


def dot(a, b):
    return lax.dot_general(a, b, (((1,), (0,)), ((), ())), preferred_element_type=F32)


def dot_nt(a, b):
    return lax.dot_general(a, b, (((1,), (1,)), ((), ())), preferred_element_type=F32)


class Place:
    def __init__(self):
        seg, fsdp = lax.axis_index("segment"), lax.axis_index("fsdp")
        self.seg = seg
        self.y, self.c = seg // 2, seg % 2
        self.z, self.x = fsdp // NX, fsdp % NX

    def at(self, dx=0, dy=0, dz=0, sibling=False):
        x = (self.x + dx) % NX
        y = (self.y + dy) % NY
        z = (self.z + dz) % NZ
        c = 1 - self.c if sibling else self.c
        return (y * 2 + c, z * NX + x)

    def others(self):
        found = [self.at(sibling=True)]
        found += [self.at(dx=d) for d in range(1, NX)]
        found += [self.at(dy=d) for d in range(1, NY)]
        found += [self.at(dz=d) for d in range(1, NZ)]
        return found


def enter(devices):
    barrier = pltpu.get_barrier_semaphore()
    for device in devices:
        pl.semaphore_signal(barrier, inc=1, device_id=device, device_id_type=MESH)
    return lambda: pl.semaphore_wait(barrier, len(devices))


SIZE = {"a": 1, "b": 2, "c": 2}
PARTS = ("a", "b", "c")


def ring_to(p, part, sign):
    return {"a": p.at(dz=sign), "b": p.at(dx=sign), "c": p.at(dy=sign)}[part]


def gather_order(part, sign):
    hops = 3 if part == "a" else 1
    rows, last = ((0, 1, 3, 2), (0, 1)) if sign > 0 else ((0, 3, 2, 1), (3, 2))
    return [(h, r) for h in range(1, hops + 1) for r in rows] + [(hops + 1, r) for r in last]


def scatter_order(part, sign):
    if part == "a":
        rows, last = ((0, 1, 2, 3), (2, 3)) if sign > 0 else ((2, 3, 0, 1), (0, 1))
        return [(4, r) for r in last] + [(h, r) for h in (3, 2, 1) for r in rows]
    rows, last = ((1, 2, 3, 0), (2, 0)) if sign > 0 else ((2, 1, 3, 0), (1, 3))
    return [(2, r) for r in last] + [(1, r) for r in rows]


def weight_of(b):
    in_b = 8 + ((b - 32) // 8) * 2 + b % 2
    in_c = 16 + (((b - 64) // 2) % 4) * 2 + b % 2
    return jnp.where(b < 32, b // 4, jnp.where(b < 64, in_b, in_c))


def row_of(b):
    return jnp.where(b < 32, b % 4, jnp.where(b < 64, ((b - 32) // 2) % 4, (b - 64) // 8))


def mult(value, of):
    return pl.multiple_of(value, of)


class Copies:
    def __init__(self, send, recv):
        self.send, self.recv = send, recv
        self.index = {}
        self.sent = []

    def number(self, key):
        return self.index.setdefault(key, len(self.index))

    def make(self, key, src, dst, device):
        i = self.number(key)
        return pltpu.make_async_remote_copy(
            src_ref=src,
            dst_ref=dst,
            send_sem=self.send.at[i],
            recv_sem=self.recv.at[i],
            device_id=device,
            device_id_type=MESH,
        )

    def start(self, key, src, dst, device):
        copy = self.make(key, src, dst, device)
        copy.start()
        self.sent.append(copy)

    def arrived(self, key, ref, device):
        self.make(key, ref, ref, device).wait_recv()

    def drain(self):
        for copy in self.sent:
            copy.wait_send()
        self.sent.clear()

    def take(self, start):
        kept, self.sent = self.sent, []
        start()
        taken, self.sent = self.sent, kept
        return taken


class Gather:
    def __init__(self, name, place, copies, buf):
        self.name, self.at, self.copies, self.buf = name, place, copies, buf

    def key(self, *rest):
        return (self.name,) + rest

    def atoms(self, x, z):
        p = self.at
        low = mult((z % 4) * FEAT, FEAT)
        return (
            self.buf.at[p.c, z * 4 + p.y, pl.ds(mult(x * FEAT, FEAT), FEAT)],
            self.buf.at[p.c, 32 + (x * 4 + p.y) * 2 + z // 4, pl.ds(low, FEAT)],
            self.buf.at[p.c, 64 + (p.y * 4 + x) * 2 + z // 4, pl.ds(low, FEAT)],
        )

    def put_own(self, block_t):
        p = self.at
        low = mult((p.z % 4) * FEAT, FEAT)
        self.buf[p.c, p.z * 4 + p.y, pl.ds(mult(p.x * FEAT, FEAT), FEAT), :] = block_t[0:64]
        self.buf[p.c, 32 + (p.x * 4 + p.y) * 2 + p.z // 4, pl.ds(low, FEAT), :] = block_t[64:128]
        self.buf[p.c, 64 + (p.y * 4 + p.x) * 2 + p.z // 4, pl.ds(low, FEAT), :] = block_t[128:192]

    def send_first(self):
        p = self.at
        a, b, c = self.atoms(p.x, p.z)
        for d in range(1, NX):
            self.copies.start(self.key("a1", d), a, a, p.at(dx=d))
        for d in range(1, NZ):
            self.copies.start(self.key("b1", d), b, b, p.at(dz=d))
            self.copies.start(self.key("c1", d), c, c, p.at(dz=d))

    def wait_first_a(self):
        p = self.at
        for d in range(1, NX):
            a, _, _ = self.atoms((p.x - d) % NX, p.z)
            self.copies.arrived(self.key("a1", d), a, p.at(dx=-d))

    def wait_first_bc(self):
        p = self.at
        for d in range(1, NZ):
            _, b, c = self.atoms(p.x, (p.z - d) % NZ)
            self.copies.arrived(self.key("b1", d), b, p.at(dz=-d))
            self.copies.arrived(self.key("c1", d), c, p.at(dz=-d))

    def second(self, part, rel):
        p = self.at
        if part == "a":
            return self.buf.at[p.c, p.z * 4 + (p.y + rel) % NY]
        if part == "b":
            return self.buf.at[p.c, pl.ds(32 + (p.x * 4 + (p.y + rel) % NY) * 2, 2)]
        return self.buf.at[p.c, pl.ds(64 + (p.y * 4 + (p.x + rel) % NX) * 2, 2)]

    def half(self, part, rel, sign):
        block = self.second(part, rel)
        if part == "a":
            return block.at[pl.ds(0 if sign > 0 else 128, 128)]
        return block.at[pl.ds(0 if sign > 0 else 1, 1)]

    def second_to(self, part, sign):
        return self.at.at(dx=sign) if part == "c" else self.at.at(dy=sign)

    def send_second(self, part):
        block = self.second(part, 0)
        for sign in (1, -1):
            self.copies.start(self.key(part + "2", sign), block, block, self.second_to(part, sign))

    def second_near(self, part):
        for sign in (-1, 1):
            rel = -sign % 4
            self.copies.arrived(
                self.key(part + "2", sign), self.second(part, rel), self.second_to(part, -sign)
            )
            half = self.half(part, rel, sign)
            self.copies.start(self.key(part + "2far", sign), half, half, self.second_to(part, sign))
            self.send_own(part, (rel,))

    def second_far(self, part):
        for sign in (1, -1):
            half = self.half(part, 2, sign)
            self.copies.arrived(
                self.key(part + "2far", sign), half, self.second_to(part, -sign)
            )
        self.send_own(part, (2,))
        ref = self.span(part, self.at.c)
        self.copies.start(self.key("own", part), ref, ref, self.at.at(sibling=True))

    def chunk(self, part, base):
        return self.buf.at[self.at.c, pl.ds(base, SIZE[part])]

    def base(self, part, back, rel):
        p = self.at
        if part == "a":
            return ((p.z - back) % NZ) * 4 + (p.y + rel) % NY
        if part == "b":
            return 32 + (((p.x - back) % NX) * 4 + (p.y + rel) % NY) * 2
        return 64 + (((p.y - back) % NY) * 4 + (p.x + rel) % NX) * 2

    def span(self, part, c):
        p = self.at
        first, count = {
            "a": (p.z * 4, 4), "b": (32 + p.x * 8, 8), "c": (64 + p.y * 8, 8)
        }[part]
        return self.buf.at[c, pl.ds(first, count)]

    def send_own(self, part, rels):
        for rel in rels:
            ref = self.chunk(part, self.base(part, 0, rel))
            for sign in (1, -1):
                self.copies.start(self.key(part, sign, 1, rel), ref, ref, ring_to(self.at, part, sign))

    def messages(self, s):
        found = [("a", sign) + gather_order("a", sign)[s] for sign in (1, -1)]
        part, n = ("b", "c")[s % 2], s // 2
        if n < 6:
            found += [(part, sign) + gather_order(part, sign)[n] for sign in (1, -1)]
        return found

    def ring_round(self, s):
        for part, sign, hop, rel in self.messages(s):
            ref = self.chunk(part, self.base(part, sign * hop, rel))
            self.copies.arrived(self.key(part, sign, hop, rel), ref, ring_to(self.at, part, -sign))
            if (hop + 1, rel) in gather_order(part, sign):
                self.copies.start(
                    self.key(part, sign, hop + 1, rel), ref, ref, ring_to(self.at, part, sign)
                )
            self.copies.start(
                self.key("sib", part, sign, hop, rel), ref, ref, self.at.at(sibling=True)
            )

    def wait_other(self, s):
        p = self.at
        for part, sign, hop, rel in self.messages(s):
            ref = self.buf.at[1 - p.c, pl.ds(self.base(part, sign * hop, rel), SIZE[part])]
            self.copies.arrived(self.key("sib", part, sign, hop, rel), ref, p.at(sibling=True))

    def wait_other_own(self):
        for part in ("a", "b", "c"):
            self.copies.arrived(
                self.key("own", part), self.span(part, 1 - self.at.c), self.at.at(sibling=True)
            )

    def both(self, b):
        return jnp.concatenate([self.buf[0, b], self.buf[1, b]], axis=1)

    def multiply_single(self, weights, total, b):
        total[b % 4] += dot(weights(b // 4), self.both(b))

    def multiply_chunk(self, weights, total, b):
        w = weight_of(b)
        rhs = jnp.concatenate([self.both(b), self.both(b + 1)], axis=0)
        total[row_of(b)] += dot(jnp.concatenate([weights(w), weights(w + 1)], axis=1), rhs)

    def multiply_own(self, weights, total):
        p = self.at

        def step(t, carry):
            self.multiply_single(weights, total, p.z * 4 + t)
            self.multiply_chunk(weights, total, 32 + p.x * 8 + 2 * t)
            self.multiply_chunk(weights, total, 64 + p.y * 8 + 2 * t)
            return carry

        lax.fori_loop(0, 4, step, 0)

    def multiply_round(self, weights, total, s):
        bases = [self.base(part, sign * hop, rel) for part, sign, hop, rel in self.messages(s)]

        def step(t, carry):
            self.multiply_single(weights, total, jnp.where(t == 0, bases[0], bases[1]))
            if len(bases) > 2:
                self.multiply_chunk(weights, total, jnp.where(t == 0, bases[2], bases[3]))
            return carry

        lax.fori_loop(0, 2, step, 0)


def load_blocks(hbm, part_ref, sem):
    for z in range(NZ):
        pltpu.make_async_copy(hbm.at[z, :, 0], part_ref(z), sem).start()
    for x in range(NX):
        for h in range(2):
            for part, first in ((1, 8), (2, 16)):
                pltpu.make_async_copy(
                    hbm.at[pl.ds(h * 4, 4), x, part], part_ref(first + x * 2 + h), sem
                ).start()


class Scatter:
    def __init__(
        self, name, first, place, copies, lhs, rhs, pairs, ring_a, ring_bc, mine, stage, bufs
    ):
        self.name, self.first, self.at, self.copies = name, first, place, copies
        self.lhs, self.rhs, self.pairs = lhs, rhs, pairs
        self.ring_a, self.ring_bc, self.mine, self.stage = ring_a, ring_bc, mine, stage
        self.two, self.three_a, self.three_bc, self.sums = bufs

    def key(self, *rest):
        return (self.name,) + rest

    def base(self, part, ahead, rel):
        p = self.at
        if part == "a":
            return ((p.z + ahead) % NZ) * 4 + (p.y + rel) % NY
        if part == "b":
            return 32 + (((p.x + ahead) % NX) * 4 + (p.y + rel) % NY) * 2
        return 64 + (((p.y + ahead) % NY) * 4 + (p.x + rel) % NX) * 2

    def chunks(self, j):
        found = []
        for i, sign in enumerate((1, -1)):
            if j < 14:
                found.append(("a", sign) + scatter_order("a", sign)[j])
            else:
                found.append(("a", 0, 0, ((1, 2), (3, 0))[j - 14][i]))
        part, n = ("b", "c")[j % 2], j // 2
        for i, sign in enumerate((1, -1)):
            if n < 6:
                found.append((part, sign) + scatter_order(part, sign)[n])
            else:
                found.append((part, 0, 0, ((1, 2), (3, 0))[n - 6][i]))
        return found

    def place_of(self, chunk):
        for j in range(16):
            chunks = self.chunks(j)
            if chunk in chunks:
                k = chunks.index(chunk)
                return (self.first + j) % SLOTS, (0, 1, 2, 4)[k]

    def produce(self, j):
        p = self.at
        slot = (self.first + j) % SLOTS
        chunks = self.chunks(j)
        bases = [self.base(part, sign * hop, rel) for part, sign, hop, rel in chunks]

        def one(w, rhs, at):
            value = dot(self.lhs(w), rhs).astype(BF)
            self.mine[slot, at] = value[:, 0:TOK]
            self.stage[slot, at] = value[:, TOK:]

        def rhs_of(row):
            return jnp.concatenate([self.rhs(row, p.c), self.rhs(row, 1 - p.c)], axis=1)

        def step(t, carry):
            b = jnp.where(t == 0, bases[0], bases[1])
            one(b // 4, rhs_of(b % 4), t)
            b = jnp.where(t == 0, bases[2], bases[3])
            w, rhs = weight_of(b), rhs_of(row_of(b))
            one(w, rhs, 2 + 2 * t)
            one(w + 1, rhs, 3 + 2 * t)
            return carry

        lax.fori_loop(0, 2, step, 0)
        for chunk, base in zip(chunks, bases):
            _, at = self.place_of(chunk)
            size = SIZE[chunk[0]]
            self.copies.start(
                self.key("sib") + chunk,
                self.stage.at[slot, pl.ds(at, size)],
                self.pairs.at[pl.ds(base, size)],
                p.at(sibling=True),
            )

    def landing(self, part, sign, i):
        side = 0 if sign > 0 else 1
        if part == "a":
            return self.ring_a.at[side, pl.ds(i, 1)]
        return self.ring_bc.at[("b", "c").index(part), side, pl.ds(2 * i, 2)]

    def came(self, part, sign, i):
        ref = self.landing(part, sign, i)
        self.copies.arrived(self.key(part, sign, i), ref, ring_to(self.at, part, -sign))
        return ref

    def gather_up(self, chunk, base, arrivals):
        part = chunk[0]
        size = SIZE[part]
        ref = self.pairs.at[pl.ds(base, size)]
        self.copies.arrived(self.key("sib") + chunk, ref, self.at.at(sibling=True))
        slot, at = self.place_of(chunk)
        refs = [self.came(part, sign, i) for sign, i in arrivals]
        for t in range(size):
            value = self.mine[slot, at + t].astype(F32) + self.pairs[base + t].astype(F32)
            for came in refs:
                value += came[t].astype(F32)
            self.pairs[base + t] = value.astype(BF)
        return ref

    def send_round(self, s):
        for chunk in self.chunks(s):
            part, sign, hop, rel = chunk
            if sign == 0:
                continue
            order = scatter_order(part, sign)
            arrivals = [(sign, order.index((hop + 1, rel)))] if (hop + 1, rel) in order else []
            i = order.index((hop, rel))
            ref = self.gather_up(chunk, self.base(part, sign * hop, rel), arrivals)
            self.copies.start(
                self.key(part, sign, i), ref, self.landing(part, sign, i), ring_to(self.at, part, sign)
            )

    def finish_ring(self, part, rels):
        for rel in rels:
            arrivals = [(sign, scatter_order(part, sign).index((1, rel))) for sign in (1, -1)]
            self.gather_up((part, 0, 0, rel), self.base(part, 0, rel), arrivals)
            if rel:
                bricks, slot, device = self.second(part, rel)
                self.copies.start(
                    self.key(part + "2", rel),
                    self.pairs.at[bricks],
                    self.two.at[rel - 1, slot],
                    device,
                )

    def second(self, part, d):
        p = self.at
        if part == "a":
            return pl.ds(p.z * 4 + (p.y + d) % NY, 1), pl.ds(0, 1), p.at(dy=d)
        if part == "b":
            return pl.ds(32 + (p.x * 4 + (p.y + d) % NY) * 2, 2), pl.ds(1, 2), p.at(dy=d)
        return pl.ds(64 + (p.y * 4 + (p.x + d) % NX) * 2, 2), pl.ds(3, 2), p.at(dx=d)

    def sum_second(self):
        p = self.at
        for part, slots in (("a", (0,)), ("b", (1, 2)), ("c", (3, 4))):
            for d in range(1, 4):
                _, slot, _ = self.second(part, d)
                device = p.at(dx=-d) if part == "c" else p.at(dy=-d)
                self.copies.arrived(self.key(part + "2", d), self.two.at[d - 1, slot], device)
            for t, slot in enumerate(slots):
                mine = {
                    "a": p.z * 4 + p.y,
                    "b": 32 + (p.x * 4 + p.y) * 2 + t,
                    "c": 64 + (p.y * 4 + p.x) * 2 + t,
                }[part]
                value = self.pairs[mine].astype(F32)
                for d in range(3):
                    value += self.two[d, slot].astype(F32)
                self.sums[slot] = value.astype(BF).reshape(4, 64, TOK)
        for d in range(1, NX):
            x = (p.x + d) % NX
            self.copies.start(
                self.key("a3", d), self.sums.at[0, x], self.three_a.at[d - 1], p.at(dx=d)
            )
        for d in range(1, NZ):
            z = (p.z + d) % NZ
            for part, first, i in (("b", 1, 0), ("c", 3, 1)):
                self.copies.start(
                    self.key(part + "3", d),
                    self.sums.at[first + z // 4, z % 4],
                    self.three_bc.at[i, d - 1],
                    p.at(dz=d),
                )

    def sum_third(self, out_ref):
        p = self.at
        rows = [self.sums[0, p.x].astype(F32)]
        for d in range(1, NX):
            self.copies.arrived(self.key("a3", d), self.three_a.at[d - 1], p.at(dx=-d))
            rows[0] += self.three_a[d - 1].astype(F32)
        for part, first, i in (("b", 1, 0), ("c", 3, 1)):
            value = self.sums[first + p.z // 4, p.z % 4].astype(F32)
            for d in range(1, NZ):
                self.copies.arrived(
                    self.key(part + "3", d), self.three_bc.at[i, d - 1], p.at(dz=-d)
                )
                value += self.three_bc[i, d - 1].astype(F32)
            rows.append(value)
        for k in range(3):
            out_ref[k * FEAT : (k + 1) * FEAT] = rows[k].astype(BF)


def moe_kernel(
    meta_ref,
    tok_ref,
    cot_ref,
    gate_hbm,
    up_hbm,
    down_hbm,
    out_ref,
    in_ref,
    dgrad_hbm,
    tok_buf,
    cot_buf,
    wgu,
    wd,
    wdt,
    flat,
    total,
    hgrad,
    scaled,
    hid,
    grads,
    meta,
    ring_a,
    ring_bc,
    mine,
    stage,
    two,
    three_a,
    three_bc,
    sums,
    wsem,
    osem,
    free,
    send,
    recv,
    send2,
    recv2,
):
    p = Place()
    copies = Copies(send, recv)
    back = Copies(send2, recv2)
    tok = Gather("tok", p, copies, tok_buf)
    cot = Gather("cot", p, copies, cot_buf)
    far = [((p.seg + d) % 8, p.z * NX + p.x) for d in range(1, 8)]
    line = [p.at(dx=d) for d in range(1, NX)] + [p.at(dz=d) for d in range(1, NZ)]
    entered = enter(line + far)

    def load_gate_up():
        load_blocks(gate_hbm, lambda w: wgu.at[w, 0], wsem.at[0])
        load_blocks(up_hbm, lambda w: wgu.at[w, 1], wsem.at[0])

    def wait_gate_up():
        pltpu.make_async_copy(wgu, wgu, wsem.at[0]).wait()

    load_gate_up()
    pltpu.make_async_copy(down_hbm, flat, wsem.at[1]).start()

    tok.put_own(tok_ref)
    cot.put_own(cot_ref)
    meta[p.seg] = meta_ref[p.seg]
    total[...] = jnp.zeros_like(total)
    hgrad[...] = jnp.zeros_like(hgrad)
    entered()

    tok.send_first()
    for d in range(1, 8):
        copies.start(("meta", d), meta_ref.at[(p.seg + d) % 8], meta.at[p.seg], far[d - 1])

    def turn_gu(w, carry):
        for k in range(2):
            block = wgu[w, k].reshape(256, 256)
            wgu[w, k] = block.T.reshape(4, 64, 256)
        return carry

    def turn_down(i, carry):
        block = flat[:, pl.ds(mult(i * 384, 384), 384)].T
        z, x = i // 2, (i % 2) * 2
        for k in range(2):
            rows = block[k * 192 : (k + 1) * 192]
            wd[z, x + k] = rows[0:64]
            wd[8 + (x + k) * 2 + z // 4, z % 4] = rows[64:128]
            wd[16 + (x + k) * 2 + z // 4, z % 4] = rows[128:192]
        return carry

    def turn_back(w, carry):
        wdt[w] = wd[w].reshape(256, 256).T
        return carry

    def w_gu(w):
        return wgu[w].reshape(512, 256)

    def w_down(w):
        return wdt[w]

    tok.wait_first_a()
    tok.send_second("a")
    tok.send_own("a", (0,))
    wait_gate_up()
    lax.fori_loop(0, 8, turn_gu, 0)
    tok.second_near("a")
    tok.wait_first_bc()
    for part in ("b", "c"):
        tok.send_second(part)
        tok.send_own(part, (0,))
    tok.second_far("a")
    cot.send_first()
    lax.fori_loop(8, 24, turn_gu, 0)
    tok.second_near("b")
    tok.second_near("c")
    pltpu.make_async_copy(down_hbm, flat, wsem.at[1]).wait()
    tok.second_far("b")
    tok.second_far("c")

    for s in range(14):
        tok.ring_round(s)
        if s == 0:
            tok.wait_other_own()
            tok.multiply_own(w_gu, total)
        else:
            tok.wait_other(s - 1)
            tok.multiply_round(w_gu, total, s - 1)
        if s == 1:
            cot.wait_first_a()
            cot.send_second("a")
        if s == 2:
            cot.wait_first_bc()
            cot.send_second("b")
            cot.send_second("c")
        if 3 <= s < 7:
            lax.fori_loop(4 * s - 12, 4 * s - 8, turn_down, 0)
        if s == 6:
            cot.send_own("b", (0,))
            cot.second_near("b")
            cot.send_own("c", (0,))
            cot.second_near("c")
        if 7 <= s < 10:
            lax.fori_loop(8 * s - 56, 8 * s - 48, turn_back, 0)
        if s == 8:
            cot.second_far("b")
            cot.second_far("c")
        if s == 9:
            cot.send_own("a", (0,))
            cot.second_near("a")
        if s == 10:
            cot.second_far("a")
    cot.ring_round(0)
    tok.wait_other(13)
    tok.multiply_round(w_gu, total, 13)
    load_gate_up()
    for d in range(1, 8):
        copies.arrived(("meta", d), meta.at[(p.seg - d) % 8], far[7 - d])

    def activate(i, carry):
        y, r = i // 4, i % 4
        low = mult(r * 64, 64)
        gate = total[y, pl.ds(low, 64)]
        upward = total[y, pl.ds(mult(256 + r * 64, 64), 64)]
        first, second = meta[2 * y], meta[2 * y + 1]
        share = jnp.concatenate([first[0:1], second[0:1]], axis=1)
        scale = jnp.concatenate([first[1:2], second[1:2]], axis=1)
        sigma = jax.nn.sigmoid(gate)
        active = gate * sigma
        hidden = active * upward
        weighted = (hidden * share).astype(BF)
        hid[y, 0, pl.ds(low, 64)] = weighted[:, 0:128]
        hid[y, 1, pl.ds(low, 64)] = weighted[:, 128:256]
        scaled[y, pl.ds(low, 64)] = (hidden * scale).astype(BF)
        total[y, pl.ds(low, 64)] = upward * (sigma * (1.0 + gate * (1.0 - sigma))) * scale
        total[y, pl.ds(mult(256 + r * 64, 64), 64)] = active * scale
        return carry

    lax.fori_loop(0, 16, activate, 0)

    pairs = tok_buf

    def lhs_in(w):
        return jnp.concatenate(
            [wgu[w, 0].reshape(256, 256), wgu[w, 1].reshape(256, 256)], axis=1
        )

    def bufs(i):
        return (two.at[i], three_a.at[i], three_bc.at[i], sums.at[i])

    out = Scatter(
        "out", 0, p, back, lambda w: wd[w].reshape(256, 256), lambda y, c: hid[y, c],
        pairs.at[0], ring_a.at[0], ring_bc.at[0], mine, stage, bufs(0),
    )
    inp = Scatter(
        "in", 16, p, back, lhs_in, lambda y, c: grads[y, c],
        pairs.at[1], ring_a.at[1], ring_bc.at[1], mine, stage, bufs(1),
    )
    sent = []

    def produce(n):
        which, j = (out, n) if n < 16 else (inp, n - 16)
        if n >= SLOTS:
            for copy in sent[n - SLOTS]:
                copy.wait_send()
        sent.append(back.take(lambda: which.produce(j)))

    for s in range(14):
        if s > 0:
            cot.ring_round(s)
        if s == 0:
            cot.wait_other_own()
            cot.multiply_own(w_down, hgrad)
        else:
            cot.wait_other(s - 1)
            cot.multiply_round(w_down, hgrad, s - 1)
        if s == 9:
            copies.drain()
            pl.semaphore_signal(
                free, inc=1, device_id=p.at(sibling=True), device_id_type=MESH
            )
        if s == 10:
            pl.semaphore_wait(free, 1)
            produce(0)
        if s == 11:
            produce(1)
            out.send_round(0)
        if s == 12:
            produce(2)
            out.send_round(1)
        if s == 13:
            produce(3)
            out.send_round(2)
    cot.wait_other(13)
    cot.multiply_round(w_down, hgrad, 13)

    def backward(i, carry):
        y, r = i // 4, i % 4
        low = mult(r * 64, 64)
        high = mult(256 + r * 64, 64)
        grad = hgrad[y, pl.ds(low, 64)]
        gate_grad = (grad * total[y, pl.ds(low, 64)]).astype(BF)
        up_grad = (grad * total[y, pl.ds(high, 64)]).astype(BF)
        for c in range(2):
            grads[y, c, pl.ds(low, 64)] = gate_grad[:, c * 128 : (c + 1) * 128]
            grads[y, c, pl.ds(high, 64)] = up_grad[:, c * 128 : (c + 1) * 128]
        return carry

    lax.fori_loop(0, 16, backward, 0)

    def weight_grad(i, carry):
        z, x = i // 2, (i % 2) * 2
        low = mult((z % 4) * FEAT, FEAT)
        acc = jnp.zeros((256, 384), F32)
        for y in range(NY):
            halves = []
            for c in range(2):
                rows = []
                for k in range(2):
                    xk = x + k
                    rows.append(cot_buf[c, z * 4 + y, pl.ds(mult(xk * FEAT, FEAT), FEAT), :])
                    rows.append(cot_buf[c, 32 + (xk * 4 + y) * 2 + z // 4, pl.ds(low, FEAT), :])
                    rows.append(cot_buf[c, 64 + (y * 4 + xk) * 2 + z // 4, pl.ds(low, FEAT), :])
                halves.append(jnp.concatenate(rows, axis=0))
            acc += dot_nt(scaled[y], jnp.concatenate(halves, axis=1))
        flat[:, pl.ds(mult(i * 384, 384), 384)] = acc.astype(BF)
        return carry

    produce(4)
    for s in range(3, 14):
        out.send_round(s)
        produce(s + 2)
        if s in (4, 6, 8, 10):
            lax.fori_loop(2 * s - 8, 2 * s - 4, weight_grad, 0)
        if s == 10:
            dgrad = pltpu.make_async_copy(flat, dgrad_hbm, osem)
            dgrad.start()
        if s == 12:
            out.finish_ring("b", (1, 2))
        if s == 13:
            out.finish_ring("c", (1, 2))
    wait_gate_up()
    produce(16)
    inp.send_round(0)
    produce(17)
    inp.send_round(1)
    out.finish_ring("a", (1, 2))
    out.finish_ring("b", (3, 0))
    produce(18)
    inp.send_round(2)
    out.finish_ring("a", (3, 0))
    out.finish_ring("c", (3, 0))
    produce(19)
    for s in range(3, 14):
        inp.send_round(s)
        produce(s + 17)
        if s == 4:
            out.sum_second()
        if s == 7:
            out.sum_third(out_ref)
        if s == 12:
            inp.finish_ring("b", (1, 2))
        if s == 13:
            inp.finish_ring("c", (1, 2))
    produce(31)
    inp.finish_ring("b", (3, 0))
    inp.finish_ring("c", (3, 0))
    inp.finish_ring("a", (1, 2, 3, 0))
    inp.sum_second()
    inp.sum_third(in_ref)
    for group in sent[32 - SLOTS :]:
        for copy in group:
            copy.wait_send()
    copies.drain()
    back.drain()
    dgrad.wait()


def per_device(
    tokens, router_logits, routes, loss_weights, cotangent, gate_weight, up_weight, down_weight
):
    share = jax.nn.sigmoid(router_logits[:, 0] - router_logits[:, 1])
    experts = jnp.arange(8, dtype=jnp.int32)[:, None]
    combine = jnp.where(routes[None, :, 0] == experts, share[None, :], 0.0) + jnp.where(
        routes[None, :, 1] == experts, 1.0 - share[None, :], 0.0
    )
    scale = combine * (loss_weights.astype(F32) / 4096.0)[None, :]
    row = jnp.arange(8)[None, :, None]
    meta = jnp.where(row == 0, combine[:, None, :], jnp.where(row == 1, scale[:, None, :], 0.0))

    gate5 = gate_weight.reshape(NZ, NX, 3, FEAT, 256)
    up5 = up_weight.reshape(NZ, NX, 3, FEAT, 256)
    down2 = down_weight.reshape(256, 6144)
    vmem = pl.BlockSpec(memory_space=pltpu.VMEM)
    hbm = pl.BlockSpec(memory_space=pl.ANY)
    n_gather, n_scatter = 288, 288

    output, input_grad, dgrad = pl.pallas_call(
        moe_kernel,
        name="moe",
        out_shape=(
            jax.ShapeDtypeStruct((192, TOK), BF),
            jax.ShapeDtypeStruct((192, TOK), BF),
            jax.ShapeDtypeStruct((256, 6144), BF),
        ),
        in_specs=[vmem, vmem, vmem, hbm, hbm, hbm],
        out_specs=(vmem, vmem, hbm),
        scratch_shapes=[
            pltpu.VMEM((2, 96, 256, TOK), BF),
            pltpu.VMEM((2, 96, 256, TOK), BF),
            pltpu.VMEM((24, 2, 4, 64, 256), BF),
            pltpu.VMEM((24, 4, 64, 256), BF),
            pltpu.VMEM((24, 256, 256), BF),
            pltpu.VMEM((256, 6144), BF),
            pltpu.VMEM((NY, 512, 256), F32),
            pltpu.VMEM((NY, 256, 256), F32),
            pltpu.VMEM((NY, 256, 256), BF),
            pltpu.VMEM((NY, 2, 256, TOK), BF),
            pltpu.VMEM((NY, 2, 512, TOK), BF),
            pltpu.VMEM((8, 8, TOK), F32),
            pltpu.VMEM((2, 2, 14, 256, TOK), BF),
            pltpu.VMEM((2, 2, 2, 12, 256, TOK), BF),
            pltpu.VMEM((SLOTS, 6, 256, TOK), BF),
            pltpu.VMEM((SLOTS, 6, 256, TOK), BF),
            pltpu.VMEM((2, 3, 5, 256, TOK), BF),
            pltpu.VMEM((2, 3, 64, TOK), BF),
            pltpu.VMEM((2, 2, 7, 64, TOK), BF),
            pltpu.VMEM((2, 5, 4, 64, TOK), BF),
            pltpu.SemaphoreType.DMA((2,)),
            pltpu.SemaphoreType.DMA,
            pltpu.SemaphoreType.REGULAR,
            pltpu.SemaphoreType.DMA((n_gather,)),
            pltpu.SemaphoreType.DMA((n_gather,)),
            pltpu.SemaphoreType.DMA((n_scatter,)),
            pltpu.SemaphoreType.DMA((n_scatter,)),
        ],
        compiler_params=pltpu.CompilerParams(
            collective_id=1, has_side_effects=True, vmem_limit_bytes=62 * 2**20
        ),
    )(meta, tokens.T, cotangent.T, gate5, up5, down2)
    return (output.T, input_grad.T, dgrad.reshape(1, 256, 6144))


def solution(mesh):
    in_specs = (
        P("segment", "fsdp"),
        P("segment", None),
        P("segment", None),
        P("segment"),
        P("segment", "fsdp"),
        P("segment", None, "fsdp"),
        P("segment", None, "fsdp"),
        P("segment", "fsdp", None),
    )
    out_specs = (P("segment", "fsdp"), P("segment", "fsdp"), P("segment", "fsdp", None))
    return jax.shard_map(
        per_device, mesh=mesh, in_specs=in_specs, out_specs=out_specs, check_vma=False
    )
```

```python
import functools

import jax
import jax.numpy as jnp
from jax import lax
from jax.experimental import pallas as pl
from jax.experimental.pallas import tpu as pltpu
from jax.sharding import PartitionSpec as P

MESH = pl.DeviceIdType.MESH
BF = jnp.bfloat16
F32 = jnp.float32
NX, NY, NZ = 4, 4, 8
SLOTS = 4
FEAT, TOK = 64, 128


def dot(a, b):
    return lax.dot_general(a, b, (((1,), (0,)), ((), ())), preferred_element_type=F32)


def dot_nt(a, b):
    return lax.dot_general(a, b, (((1,), (1,)), ((), ())), preferred_element_type=F32)


class Place:
    def __init__(self):
        seg, fsdp = lax.axis_index("segment"), lax.axis_index("fsdp")
        self.seg = seg
        self.y, self.c = seg // 2, seg % 2
        self.z, self.x = fsdp // NX, fsdp % NX

    def at(self, dx=0, dy=0, dz=0, sibling=False):
        x = (self.x + dx) % NX
        y = (self.y + dy) % NY
        z = (self.z + dz) % NZ
        c = 1 - self.c if sibling else self.c
        return (y * 2 + c, z * NX + x)

    def others(self):
        found = [self.at(sibling=True)]
        found += [self.at(dx=d) for d in range(1, NX)]
        found += [self.at(dy=d) for d in range(1, NY)]
        found += [self.at(dz=d) for d in range(1, NZ)]
        return found


def enter(devices):
    barrier = pltpu.get_barrier_semaphore()
    for device in devices:
        pl.semaphore_signal(barrier, inc=1, device_id=device, device_id_type=MESH)
    return lambda: pl.semaphore_wait(barrier, len(devices))


SIZE = {"a": 1, "b": 2, "c": 2}
PARTS = ("a", "b", "c")


def ring_to(p, part, sign):
    return {"a": p.at(dz=sign), "b": p.at(dx=sign), "c": p.at(dy=sign)}[part]


def gather_order(part, sign):
    hops = 3 if part == "a" else 1
    rows, last = ((0, 1, 3, 2), (0, 1)) if sign > 0 else ((0, 3, 2, 1), (3, 2))
    return [(h, r) for h in range(1, hops + 1) for r in rows] + [(hops + 1, r) for r in last]


def scatter_order(part, sign):
    if part == "a":
        rows, last = ((0, 1, 2, 3), (2, 3)) if sign > 0 else ((2, 3, 0, 1), (0, 1))
        return [(4, r) for r in last] + [(h, r) for h in (3, 2, 1) for r in rows]
    rows, last = ((1, 2, 3, 0), (2, 0)) if sign > 0 else ((2, 1, 3, 0), (1, 3))
    return [(2, r) for r in last] + [(1, r) for r in rows]


def weight_of(b):
    in_b = 8 + ((b - 32) // 8) * 2 + b % 2
    in_c = 16 + (((b - 64) // 2) % 4) * 2 + b % 2
    return jnp.where(b < 32, b // 4, jnp.where(b < 64, in_b, in_c))


def row_of(b):
    return jnp.where(b < 32, b % 4, jnp.where(b < 64, ((b - 32) // 2) % 4, (b - 64) // 8))


def mult(value, of):
    return pl.multiple_of(value, of)


class Copies:
    def __init__(self, send, recv):
        self.send, self.recv = send, recv
        self.index = {}
        self.sent = []

    def number(self, key):
        return self.index.setdefault(key, len(self.index))

    def make(self, key, src, dst, device):
        i = self.number(key)
        return pltpu.make_async_remote_copy(
            src_ref=src,
            dst_ref=dst,
            send_sem=self.send.at[i],
            recv_sem=self.recv.at[i],
            device_id=device,
            device_id_type=MESH,
        )

    def start(self, key, src, dst, device):
        copy = self.make(key, src, dst, device)
        copy.start()
        self.sent.append(copy)

    def arrived(self, key, ref, device):
        self.make(key, ref, ref, device).wait_recv()

    def drain(self):
        for copy in self.sent:
            copy.wait_send()
        self.sent.clear()

    def take(self, start):
        kept, self.sent = self.sent, []
        start()
        taken, self.sent = self.sent, kept
        return taken


class Gather:
    def __init__(self, name, place, copies, buf):
        self.name, self.at, self.copies, self.buf = name, place, copies, buf

    def key(self, *rest):
        return (self.name,) + rest

    def atoms(self, x, z):
        p = self.at
        low = mult((z % 4) * FEAT, FEAT)
        return (
            self.buf.at[p.c, z * 4 + p.y, pl.ds(mult(x * FEAT, FEAT), FEAT)],
            self.buf.at[p.c, 32 + (x * 4 + p.y) * 2 + z // 4, pl.ds(low, FEAT)],
            self.buf.at[p.c, 64 + (p.y * 4 + x) * 2 + z // 4, pl.ds(low, FEAT)],
        )

    def put_own(self, block_t):
        p = self.at
        low = mult((p.z % 4) * FEAT, FEAT)
        self.buf[p.c, p.z * 4 + p.y, pl.ds(mult(p.x * FEAT, FEAT), FEAT), :] = block_t[0:64]
        self.buf[p.c, 32 + (p.x * 4 + p.y) * 2 + p.z // 4, pl.ds(low, FEAT), :] = block_t[64:128]
        self.buf[p.c, 64 + (p.y * 4 + p.x) * 2 + p.z // 4, pl.ds(low, FEAT), :] = block_t[128:192]

    def send_first(self):
        p = self.at
        a, b, c = self.atoms(p.x, p.z)
        for d in range(1, NX):
            self.copies.start(self.key("a1", d), a, a, p.at(dx=d))
        for d in range(1, NZ):
            self.copies.start(self.key("b1", d), b, b, p.at(dz=d))
            self.copies.start(self.key("c1", d), c, c, p.at(dz=d))

    def wait_first_a(self):
        p = self.at
        for d in range(1, NX):
            a, _, _ = self.atoms((p.x - d) % NX, p.z)
            self.copies.arrived(self.key("a1", d), a, p.at(dx=-d))

    def wait_first_bc(self):
        p = self.at
        for d in range(1, NZ):
            _, b, c = self.atoms(p.x, (p.z - d) % NZ)
            self.copies.arrived(self.key("b1", d), b, p.at(dz=-d))
            self.copies.arrived(self.key("c1", d), c, p.at(dz=-d))

    def second(self, part, rel):
        p = self.at
        if part == "a":
            return self.buf.at[p.c, p.z * 4 + (p.y + rel) % NY]
        if part == "b":
            return self.buf.at[p.c, pl.ds(32 + (p.x * 4 + (p.y + rel) % NY) * 2, 2)]
        return self.buf.at[p.c, pl.ds(64 + (p.y * 4 + (p.x + rel) % NX) * 2, 2)]

    def half(self, part, rel, sign):
        block = self.second(part, rel)
        if part == "a":
            return block.at[pl.ds(0 if sign > 0 else 128, 128)]
        return block.at[pl.ds(0 if sign > 0 else 1, 1)]

    def second_to(self, part, sign):
        return self.at.at(dx=sign) if part == "c" else self.at.at(dy=sign)

    def send_second(self, part):
        block = self.second(part, 0)
        for sign in (1, -1):
            self.copies.start(self.key(part + "2", sign), block, block, self.second_to(part, sign))

    def second_near(self, part):
        for sign in (-1, 1):
            rel = -sign % 4
            self.copies.arrived(
                self.key(part + "2", sign), self.second(part, rel), self.second_to(part, -sign)
            )
            half = self.half(part, rel, sign)
            self.copies.start(self.key(part + "2far", sign), half, half, self.second_to(part, sign))
            self.send_own(part, (rel,))

    def second_far(self, part):
        for sign in (1, -1):
            half = self.half(part, 2, sign)
            self.copies.arrived(
                self.key(part + "2far", sign), half, self.second_to(part, -sign)
            )
        self.send_own(part, (2,))
        ref = self.span(part, self.at.c)
        self.copies.start(self.key("own", part), ref, ref, self.at.at(sibling=True))

    def chunk(self, part, base):
        return self.buf.at[self.at.c, pl.ds(base, SIZE[part])]

    def base(self, part, back, rel):
        p = self.at
        if part == "a":
            return ((p.z - back) % NZ) * 4 + (p.y + rel) % NY
        if part == "b":
            return 32 + (((p.x - back) % NX) * 4 + (p.y + rel) % NY) * 2
        return 64 + (((p.y - back) % NY) * 4 + (p.x + rel) % NX) * 2

    def span(self, part, c):
        p = self.at
        first, count = {
            "a": (p.z * 4, 4), "b": (32 + p.x * 8, 8), "c": (64 + p.y * 8, 8)
        }[part]
        return self.buf.at[c, pl.ds(first, count)]

    def send_own(self, part, rels):
        for rel in rels:
            ref = self.chunk(part, self.base(part, 0, rel))
            for sign in (1, -1):
                self.copies.start(self.key(part, sign, 1, rel), ref, ref, ring_to(self.at, part, sign))

    def messages(self, s, u):
        found = []
        if 0 <= s < 14:
            found += [("a", sign) + gather_order("a", sign)[s] for sign in (1, -1)]
        if 0 <= u < 12:
            part = ("b", "c")[u % 2]
            found += [(part, sign) + gather_order(part, sign)[u // 2] for sign in (1, -1)]
        return found

    def ring_round(self, s, u):
        for part, sign, hop, rel in self.messages(s, u):
            ref = self.chunk(part, self.base(part, sign * hop, rel))
            self.copies.arrived(self.key(part, sign, hop, rel), ref, ring_to(self.at, part, -sign))
            if (hop + 1, rel) in gather_order(part, sign):
                self.copies.start(
                    self.key(part, sign, hop + 1, rel), ref, ref, ring_to(self.at, part, sign)
                )
            self.copies.start(
                self.key("sib", part, sign, hop, rel), ref, ref, self.at.at(sibling=True)
            )

    def wait_other(self, s, u):
        p = self.at
        for part, sign, hop, rel in self.messages(s, u):
            ref = self.buf.at[1 - p.c, pl.ds(self.base(part, sign * hop, rel), SIZE[part])]
            self.copies.arrived(self.key("sib", part, sign, hop, rel), ref, p.at(sibling=True))

    def wait_other_own(self):
        for part in ("a", "b", "c"):
            self.copies.arrived(
                self.key("own", part), self.span(part, 1 - self.at.c), self.at.at(sibling=True)
            )

    def both(self, b):
        return jnp.concatenate([self.buf[0, b], self.buf[1, b]], axis=1)

    def multiply_single(self, weights, total, b):
        total[b % 4] += dot(weights(b // 4), self.both(b))

    def multiply_chunk(self, weights, total, b):
        w = weight_of(b)
        rhs = jnp.concatenate([self.both(b), self.both(b + 1)], axis=0)
        total[row_of(b)] += dot(jnp.concatenate([weights(w), weights(w + 1)], axis=1), rhs)

    def multiply_own(self, weights, total):
        p = self.at

        def step(t, carry):
            self.multiply_single(weights, total, p.z * 4 + t)
            self.multiply_chunk(weights, total, 32 + p.x * 8 + 2 * t)
            self.multiply_chunk(weights, total, 64 + p.y * 8 + 2 * t)
            return carry

        lax.fori_loop(0, 4, step, 0)

    def multiply_round(self, weights, total, s, u):
        messages = self.messages(s, u)
        bases = [self.base(part, sign * hop, rel) for part, sign, hop, rel in messages]
        if not bases:
            return

        def step(t, carry):
            if messages[0][0] == "a":
                self.multiply_single(weights, total, jnp.where(t == 0, bases[0], bases[1]))
            if messages[-1][0] != "a":
                self.multiply_chunk(weights, total, jnp.where(t == 0, bases[-2], bases[-1]))
            return carry

        lax.fori_loop(0, 2, step, 0)


def load_blocks(hbm, part_ref, sem):
    for z in range(NZ):
        pltpu.make_async_copy(hbm.at[z, :, 0], part_ref(z), sem).start()
    for x in range(NX):
        for h in range(2):
            for part, first in ((1, 8), (2, 16)):
                pltpu.make_async_copy(
                    hbm.at[pl.ds(h * 4, 4), x, part], part_ref(first + x * 2 + h), sem
                ).start()


class Scatter:
    def __init__(
        self, name, first, place, copies, lhs, rhs, pairs, ring_a, ring_bc, mine, stage, bufs
    ):
        self.name, self.first, self.at, self.copies = name, first, place, copies
        self.lhs, self.rhs, self.pairs = lhs, rhs, pairs
        self.ring_a, self.ring_bc, self.mine, self.stage = ring_a, ring_bc, mine, stage
        self.two, self.three_a, self.three_bc, self.sums = bufs

    def key(self, *rest):
        return (self.name,) + rest

    def base(self, part, ahead, rel):
        p = self.at
        if part == "a":
            return ((p.z + ahead) % NZ) * 4 + (p.y + rel) % NY
        if part == "b":
            return 32 + (((p.x + ahead) % NX) * 4 + (p.y + rel) % NY) * 2
        return 64 + (((p.y + ahead) % NY) * 4 + (p.x + rel) % NX) * 2

    def chunks(self, kind, j):
        part, n = ("a", j) if kind == "a" else (("b", "c")[j % 2], j // 2)
        count = 14 if kind == "a" else 6
        if n < count:
            return [(part, sign) + scatter_order(part, sign)[n] for sign in (1, -1)]
        return [(part, 0, 0, rel) for rel in ((1, 2), (3, 0))[n - count]]

    def place_of(self, chunk):
        kind = "a" if chunk[0] == "a" else "bc"
        for j in range(16):
            chunks = self.chunks(kind, j)
            if chunk in chunks:
                k = chunks.index(chunk)
                return (self.first + j) % SLOTS, (k if kind == "a" else 2 + 2 * k)

    def produce(self, kind, j):
        p = self.at
        slot = (self.first + j) % SLOTS
        chunks = self.chunks(kind, j)
        bases = [self.base(part, sign * hop, rel) for part, sign, hop, rel in chunks]

        def one(w, rhs, at):
            value = dot(self.lhs(w), rhs).astype(BF)
            self.mine[slot, at] = value[:, 0:TOK]
            self.stage[slot, at] = value[:, TOK:]

        def rhs_of(row):
            return jnp.concatenate([self.rhs(row, p.c), self.rhs(row, 1 - p.c)], axis=1)

        def step(t, carry):
            b = jnp.where(t == 0, bases[0], bases[1])
            if kind == "a":
                one(b // 4, rhs_of(b % 4), t)
            else:
                w, rhs = weight_of(b), rhs_of(row_of(b))
                one(w, rhs, 2 + 2 * t)
                one(w + 1, rhs, 3 + 2 * t)
            return carry

        lax.fori_loop(0, 2, step, 0)
        for chunk, base in zip(chunks, bases):
            _, at = self.place_of(chunk)
            size = SIZE[chunk[0]]
            self.copies.start(
                self.key("sib") + chunk,
                self.stage.at[slot, pl.ds(at, size)],
                self.pairs.at[pl.ds(base, size)],
                p.at(sibling=True),
            )

    def landing(self, part, sign, i):
        side = 0 if sign > 0 else 1
        if part == "a":
            return self.ring_a.at[side, pl.ds(i, 1)]
        return self.ring_bc.at[("b", "c").index(part), side, pl.ds(2 * i, 2)]

    def came(self, part, sign, i):
        ref = self.landing(part, sign, i)
        self.copies.arrived(self.key(part, sign, i), ref, ring_to(self.at, part, -sign))
        return ref

    def gather_up(self, chunk, base, arrivals):
        part = chunk[0]
        size = SIZE[part]
        ref = self.pairs.at[pl.ds(base, size)]
        self.copies.arrived(self.key("sib") + chunk, ref, self.at.at(sibling=True))
        slot, at = self.place_of(chunk)
        refs = [self.came(part, sign, i) for sign, i in arrivals]
        for t in range(size):
            value = self.mine[slot, at + t].astype(F32) + self.pairs[base + t].astype(F32)
            for came in refs:
                value += came[t].astype(F32)
            self.pairs[base + t] = value.astype(BF)
        return ref

    def send_round(self, kind, j):
        for chunk in self.chunks(kind, j):
            part, sign, hop, rel = chunk
            if sign == 0:
                continue
            order = scatter_order(part, sign)
            arrivals = [(sign, order.index((hop + 1, rel)))] if (hop + 1, rel) in order else []
            i = order.index((hop, rel))
            ref = self.gather_up(chunk, self.base(part, sign * hop, rel), arrivals)
            self.copies.start(
                self.key(part, sign, i), ref, self.landing(part, sign, i), ring_to(self.at, part, sign)
            )

    def finish_ring(self, part, rels):
        for rel in rels:
            arrivals = [(sign, scatter_order(part, sign).index((1, rel))) for sign in (1, -1)]
            self.gather_up((part, 0, 0, rel), self.base(part, 0, rel), arrivals)
            if rel:
                bricks, slot, device = self.second(part, rel)
                self.copies.start(
                    self.key(part + "2", rel),
                    self.pairs.at[bricks],
                    self.two.at[rel - 1, slot],
                    device,
                )

    def second(self, part, d):
        p = self.at
        if part == "a":
            return pl.ds(p.z * 4 + (p.y + d) % NY, 1), pl.ds(0, 1), p.at(dy=d)
        if part == "b":
            return pl.ds(32 + (p.x * 4 + (p.y + d) % NY) * 2, 2), pl.ds(1, 2), p.at(dy=d)
        return pl.ds(64 + (p.y * 4 + (p.x + d) % NX) * 2, 2), pl.ds(3, 2), p.at(dx=d)

    def sum_second(self, part):
        p = self.at
        slots = {"a": (0,), "b": (1, 2), "c": (3, 4)}[part]
        for d in range(1, 4):
            _, slot, _ = self.second(part, d)
            device = p.at(dx=-d) if part == "c" else p.at(dy=-d)
            self.copies.arrived(self.key(part + "2", d), self.two.at[d - 1, slot], device)
        for t, slot in enumerate(slots):
            mine = {
                "a": p.z * 4 + p.y,
                "b": 32 + (p.x * 4 + p.y) * 2 + t,
                "c": 64 + (p.y * 4 + p.x) * 2 + t,
            }[part]
            value = self.pairs[mine].astype(F32)
            for d in range(3):
                value += self.two[d, slot].astype(F32)
            self.sums[slot] = value.astype(BF).reshape(4, 64, TOK)
        if part == "a":
            for d in range(1, NX):
                x = (p.x + d) % NX
                self.copies.start(
                    self.key("a3", d), self.sums.at[0, x], self.three_a.at[d - 1], p.at(dx=d)
                )
            return
        first, i = {"b": (1, 0), "c": (3, 1)}[part]
        for d in range(1, NZ):
            z = (p.z + d) % NZ
            self.copies.start(
                self.key(part + "3", d),
                self.sums.at[first + z // 4, z % 4],
                self.three_bc.at[i, d - 1],
                p.at(dz=d),
            )

    def sum_third(self, part, out_ref):
        p = self.at
        if part == "a":
            value = self.sums[0, p.x].astype(F32)
            for d in range(1, NX):
                self.copies.arrived(self.key("a3", d), self.three_a.at[d - 1], p.at(dx=-d))
                value += self.three_a[d - 1].astype(F32)
            out_ref[0:FEAT] = value.astype(BF)
            return
        first, i = {"b": (1, 0), "c": (3, 1)}[part]
        value = self.sums[first + p.z // 4, p.z % 4].astype(F32)
        for d in range(1, NZ):
            self.copies.arrived(self.key(part + "3", d), self.three_bc.at[i, d - 1], p.at(dz=-d))
            value += self.three_bc[i, d - 1].astype(F32)
        out_ref[(i + 1) * FEAT : (i + 2) * FEAT] = value.astype(BF)


def moe_kernel(
    meta_ref,
    tok_ref,
    cot_ref,
    gate_hbm,
    up_hbm,
    down_hbm,
    out_ref,
    in_ref,
    dgrad_hbm,
    tok_buf,
    cot_buf,
    wgu,
    wd,
    wdt,
    flat,
    total,
    hgrad,
    scaled,
    hid,
    grads,
    meta,
    ring_a,
    ring_bc,
    mine,
    stage,
    two,
    three_a,
    three_bc,
    sums,
    wsem,
    osem,
    free,
    send,
    recv,
    send2,
    recv2,
):
    p = Place()
    copies = Copies(send, recv)
    back = Copies(send2, recv2)
    tok = Gather("tok", p, copies, tok_buf)
    cot = Gather("cot", p, copies, cot_buf)
    far = [((p.seg + d) % 8, p.z * NX + p.x) for d in range(1, 8)]
    line = [p.at(dx=d) for d in range(1, NX)] + [p.at(dz=d) for d in range(1, NZ)]
    entered = enter(line + far)

    def load_gate_up():
        load_blocks(gate_hbm, lambda w: wgu.at[w, 0], wsem.at[0])
        load_blocks(up_hbm, lambda w: wgu.at[w, 1], wsem.at[0])

    def wait_gate_up():
        pltpu.make_async_copy(wgu, wgu, wsem.at[0]).wait()

    load_gate_up()
    pltpu.make_async_copy(down_hbm, flat, wsem.at[1]).start()

    tok.put_own(tok_ref)
    cot.put_own(cot_ref)
    meta[p.seg] = meta_ref[p.seg]
    total[...] = jnp.zeros_like(total)
    hgrad[...] = jnp.zeros_like(hgrad)
    entered()

    tok.send_first()
    for d in range(1, 8):
        copies.start(("meta", d), meta_ref.at[(p.seg + d) % 8], meta.at[p.seg], far[d - 1])

    def turn_gu(w, carry):
        for k in range(2):
            block = wgu[w, k].reshape(256, 256)
            wgu[w, k] = block.T.reshape(4, 64, 256)
        return carry

    def turn_down(i, carry):
        block = flat[:, pl.ds(mult(i * 384, 384), 384)].T
        z, x = i // 2, (i % 2) * 2
        for k in range(2):
            rows = block[k * 192 : (k + 1) * 192]
            wd[z, x + k] = rows[0:64]
            wd[8 + (x + k) * 2 + z // 4, z % 4] = rows[64:128]
            wd[16 + (x + k) * 2 + z // 4, z % 4] = rows[128:192]
        return carry

    def turn_back(w, carry):
        wdt[w] = wd[w].reshape(256, 256).T
        return carry

    def w_gu(w):
        return wgu[w].reshape(512, 256)

    def w_down(w):
        return wdt[w]

    def activate(i, carry):
        y, r = i // 4, i % 4
        low = mult(r * 64, 64)
        gate = total[y, pl.ds(low, 64)]
        upward = total[y, pl.ds(mult(256 + r * 64, 64), 64)]
        first, second = meta[2 * y], meta[2 * y + 1]
        share = jnp.concatenate([first[0:1], second[0:1]], axis=1)
        scale = jnp.concatenate([first[1:2], second[1:2]], axis=1)
        sigma = jax.nn.sigmoid(gate)
        active = gate * sigma
        hidden = active * upward
        weighted = (hidden * share).astype(BF)
        hid[y, 0, pl.ds(low, 64)] = weighted[:, 0:128]
        hid[y, 1, pl.ds(low, 64)] = weighted[:, 128:256]
        scaled[y, pl.ds(low, 64)] = (hidden * scale).astype(BF)
        total[y, pl.ds(low, 64)] = upward * (sigma * (1.0 + gate * (1.0 - sigma))) * scale
        total[y, pl.ds(mult(256 + r * 64, 64), 64)] = active * scale
        return carry

    def backward(i, carry):
        y, r = i // 4, i % 4
        low = mult(r * 64, 64)
        high = mult(256 + r * 64, 64)
        grad = hgrad[y, pl.ds(low, 64)]
        gate_grad = (grad * total[y, pl.ds(low, 64)]).astype(BF)
        up_grad = (grad * total[y, pl.ds(high, 64)]).astype(BF)
        for c in range(2):
            grads[y, c, pl.ds(low, 64)] = gate_grad[:, c * 128 : (c + 1) * 128]
            grads[y, c, pl.ds(high, 64)] = up_grad[:, c * 128 : (c + 1) * 128]
        return carry

    def weight_grad(i, carry):
        z, x = i // 2, (i % 2) * 2
        low = mult((z % 4) * FEAT, FEAT)
        acc = jnp.zeros((256, 384), F32)
        for y in range(NY):
            halves = []
            for c in range(2):
                rows = []
                for k in range(2):
                    xk = x + k
                    rows.append(cot_buf[c, z * 4 + y, pl.ds(mult(xk * FEAT, FEAT), FEAT), :])
                    rows.append(cot_buf[c, 32 + (xk * 4 + y) * 2 + z // 4, pl.ds(low, FEAT), :])
                    rows.append(cot_buf[c, 64 + (y * 4 + xk) * 2 + z // 4, pl.ds(low, FEAT), :])
                halves.append(jnp.concatenate(rows, axis=0))
            acc += dot_nt(scaled[y], jnp.concatenate(halves, axis=1))
        flat[:, pl.ds(mult(i * 384, 384), 384)] = acc.astype(BF)
        return carry

    pairs = tok_buf

    def lhs_in(w):
        return jnp.concatenate(
            [wgu[w, 0].reshape(256, 256), wgu[w, 1].reshape(256, 256)], axis=1
        )

    def bufs(i):
        return (two.at[i], three_a.at[i], three_bc.at[i], sums.at[i])

    out = Scatter(
        "out", 0, p, back, lambda w: wd[w].reshape(256, 256), lambda y, c: hid[y, c],
        pairs.at[0], ring_a.at[0], ring_bc.at[0], mine, stage, bufs(0),
    )
    inp = Scatter(
        "in", 16, p, back, lhs_in, lambda y, c: grads[y, c],
        pairs.at[1], ring_a.at[1], ring_bc.at[1], mine, stage, bufs(1),
    )
    sent = {"a": [], "bc": []}

    def step_of(n):
        return (out, n) if n < 16 else (inp, n - 16)

    def produce(kind, n):
        if not 0 <= n < 32:
            return
        which, j = step_of(n)
        if n >= SLOTS:
            for copy in sent[kind][n - SLOTS]:
                copy.wait_send()
        sent[kind].append(back.take(lambda: which.produce(kind, j)))

    def turn(kind, n):
        if not 0 <= n < 32:
            return
        which, j = step_of(n)
        if kind == "a":
            if j < 14:
                which.send_round("a", j)
            else:
                which.finish_ring("a", ((1, 2), (3, 0))[j - 14])
        elif j < 12:
            which.send_round("bc", j)
        else:
            which.finish_ring(("b", "c")[j % 2], ((1, 2), (3, 0))[(j - 12) // 2])

    tok.wait_first_a()
    tok.send_second("a")
    tok.send_own("a", (0,))
    wait_gate_up()
    lax.fori_loop(0, 8, turn_gu, 0)
    tok.second_near("a")
    tok.wait_first_bc()
    for part in ("b", "c"):
        tok.send_second(part)
        tok.send_own(part, (0,))
    tok.second_far("a")
    lax.fori_loop(8, 16, turn_gu, 0)

    lag, first_bc, first_a = 4, 23, 27
    for n in range(first_a + 32):
        if n < 14:
            tok.ring_round(n, -1)
        elif n < 28:
            cot.ring_round(n - 14, -1)
        if lag <= n < 12 + lag:
            tok.ring_round(-1, n - lag)
        elif 12 + lag <= n < 24 + lag:
            cot.ring_round(-1, n - 12 - lag)
        if n == 0:
            lax.fori_loop(16, 24, turn_gu, 0)
        if n == 1:
            tok.second_near("b")
        if n == 2:
            tok.second_near("c")
            cot.send_first()
        if n == 3:
            tok.second_far("b")
            tok.second_far("c")
            pltpu.make_async_copy(down_hbm, flat, wsem.at[1]).wait()
        if n == 4:
            tok.wait_other_own()
            tok.multiply_own(w_gu, total)
        if 1 <= n <= 16:
            k = n - 1
            tok.wait_other(k, k - lag)
            tok.multiply_round(w_gu, total, k, k - lag)
        if 5 <= n < 9:
            lax.fori_loop(4 * n - 20, 4 * n - 16, turn_down, 0)
        if 9 <= n < 13:
            lax.fori_loop(6 * n - 54, 6 * n - 48, turn_back, 0)
        if n == 7:
            cot.wait_first_a()
            cot.send_second("a")
            cot.wait_first_bc()
            cot.send_second("b")
            cot.send_second("c")
        if n == 10:
            cot.send_own("b", (0,))
            cot.second_near("b")
            cot.send_own("c", (0,))
            cot.second_near("c")
            cot.send_own("a", (0,))
            cot.second_near("a")
        if n == 11:
            cot.second_far("a")
        if n == 12:
            cot.second_far("b")
            cot.second_far("c")
        if n == 16:
            before, copies.sent = copies.sent, []
            load_gate_up()
            for d in range(1, 8):
                copies.arrived(("meta", d), meta.at[(p.seg - d) % 8], far[7 - d])
            lax.fori_loop(0, 16, activate, 0)
        if n == 17:
            cot.wait_other_own()
            cot.multiply_own(w_down, hgrad)
        if 15 <= n <= 28:
            k = n - 1
            cot.wait_other(k - 14, k - 12 - lag)
            cot.multiply_round(w_down, hgrad, k - 14, k - 12 - lag)
        if n == 20:
            for copy in before:
                copy.wait_send()
            pl.semaphore_signal(
                free, inc=1, device_id=p.at(sibling=True), device_id_type=MESH
            )
        if n == 21:
            pl.semaphore_wait(free, 1)
        if n == 28:
            lax.fori_loop(0, 16, backward, 0)
        if 29 <= n < 37:
            lax.fori_loop(2 * n - 58, 2 * n - 56, weight_grad, 0)
        if n == 37:
            dgrad = pltpu.make_async_copy(flat, dgrad_hbm, osem)
            dgrad.start()
            wait_gate_up()
        turn("bc", n - first_bc)
        produce("bc", n - first_bc + 2)
        turn("a", n - first_a)
        produce("a", n - first_a + 2)
        for which, start in ((out, 0), (inp, 16)):
            k = n - first_bc - start
            if k == 17:
                which.sum_second("b")
            if k == 18:
                which.sum_second("c")
        if n == first_a + 18:
            out.sum_second("a")
        if n == first_a + 22:
            for part in PARTS:
                out.sum_third(part, out_ref)
    inp.sum_second("a")
    for part in PARTS:
        inp.sum_third(part, in_ref)
    for kind in ("a", "bc"):
        for group in sent[kind][32 - SLOTS :]:
            for copy in group:
                copy.wait_send()
    copies.drain()
    back.drain()
    dgrad.wait()


def per_device(
    tokens, router_logits, routes, loss_weights, cotangent, gate_weight, up_weight, down_weight
):
    share = jax.nn.sigmoid(router_logits[:, 0] - router_logits[:, 1])
    experts = jnp.arange(8, dtype=jnp.int32)[:, None]
    combine = jnp.where(routes[None, :, 0] == experts, share[None, :], 0.0) + jnp.where(
        routes[None, :, 1] == experts, 1.0 - share[None, :], 0.0
    )
    scale = combine * (loss_weights.astype(F32) / 4096.0)[None, :]
    row = jnp.arange(8)[None, :, None]
    meta = jnp.where(row == 0, combine[:, None, :], jnp.where(row == 1, scale[:, None, :], 0.0))

    gate5 = gate_weight.reshape(NZ, NX, 3, FEAT, 256)
    up5 = up_weight.reshape(NZ, NX, 3, FEAT, 256)
    down2 = down_weight.reshape(256, 6144)
    vmem = pl.BlockSpec(memory_space=pltpu.VMEM)
    hbm = pl.BlockSpec(memory_space=pl.ANY)
    n_gather, n_scatter = 288, 288

    output, input_grad, dgrad = pl.pallas_call(
        moe_kernel,
        name="moe",
        out_shape=(
            jax.ShapeDtypeStruct((192, TOK), BF),
            jax.ShapeDtypeStruct((192, TOK), BF),
            jax.ShapeDtypeStruct((256, 6144), BF),
        ),
        in_specs=[vmem, vmem, vmem, hbm, hbm, hbm],
        out_specs=(vmem, vmem, hbm),
        scratch_shapes=[
            pltpu.VMEM((2, 96, 256, TOK), BF),
            pltpu.VMEM((2, 96, 256, TOK), BF),
            pltpu.VMEM((24, 2, 4, 64, 256), BF),
            pltpu.VMEM((24, 4, 64, 256), BF),
            pltpu.VMEM((24, 256, 256), BF),
            pltpu.VMEM((256, 6144), BF),
            pltpu.VMEM((NY, 512, 256), F32),
            pltpu.VMEM((NY, 256, 256), F32),
            pltpu.VMEM((NY, 256, 256), BF),
            pltpu.VMEM((NY, 2, 256, TOK), BF),
            pltpu.VMEM((NY, 2, 512, TOK), BF),
            pltpu.VMEM((8, 8, TOK), F32),
            pltpu.VMEM((2, 2, 14, 256, TOK), BF),
            pltpu.VMEM((2, 2, 2, 12, 256, TOK), BF),
            pltpu.VMEM((SLOTS, 6, 256, TOK), BF),
            pltpu.VMEM((SLOTS, 6, 256, TOK), BF),
            pltpu.VMEM((2, 3, 5, 256, TOK), BF),
            pltpu.VMEM((2, 3, 64, TOK), BF),
            pltpu.VMEM((2, 2, 7, 64, TOK), BF),
            pltpu.VMEM((2, 5, 4, 64, TOK), BF),
            pltpu.SemaphoreType.DMA((2,)),
            pltpu.SemaphoreType.DMA,
            pltpu.SemaphoreType.REGULAR,
            pltpu.SemaphoreType.DMA((n_gather,)),
            pltpu.SemaphoreType.DMA((n_gather,)),
            pltpu.SemaphoreType.DMA((n_scatter,)),
            pltpu.SemaphoreType.DMA((n_scatter,)),
        ],
        compiler_params=pltpu.CompilerParams(
            collective_id=1, has_side_effects=True, vmem_limit_bytes=62 * 2**20
        ),
    )(meta, tokens.T, cotangent.T, gate5, up5, down2)
    return (output.T, input_grad.T, dgrad.reshape(1, 256, 6144))


def solution(mesh):
    in_specs = (
        P("segment", "fsdp"),
        P("segment", None),
        P("segment", None),
        P("segment"),
        P("segment", "fsdp"),
        P("segment", None, "fsdp"),
        P("segment", None, "fsdp"),
        P("segment", "fsdp", None),
    )
    out_specs = (P("segment", "fsdp"), P("segment", "fsdp"), P("segment", "fsdp", None))
    return jax.shard_map(
        per_device, mesh=mesh, in_specs=in_specs, out_specs=out_specs, check_vma=False
    )
```

```python
import functools

import jax
import jax.numpy as jnp
from jax import lax
from jax.experimental import pallas as pl
from jax.experimental.pallas import tpu as pltpu
from jax.sharding import PartitionSpec as P

MESH = pl.DeviceIdType.MESH
BF = jnp.bfloat16
F32 = jnp.float32
NX, NY, NZ = 4, 4, 8
SLOTS = 4
FEAT, TOK = 64, 128


def dot(a, b):
    return lax.dot_general(a, b, (((1,), (0,)), ((), ())), preferred_element_type=F32)


def dot_nt(a, b):
    return lax.dot_general(a, b, (((1,), (1,)), ((), ())), preferred_element_type=F32)


class Place:
    def __init__(self):
        seg, fsdp = lax.axis_index("segment"), lax.axis_index("fsdp")
        self.seg = seg
        self.y, self.c = seg // 2, seg % 2
        self.z, self.x = fsdp // NX, fsdp % NX
        self.other = 1 - self.c
        self.xs = [self.x] + [lax.rem(self.x + d, NX) for d in range(1, NX)]
        self.ys = [self.y] + [lax.rem(self.y + d, NY) for d in range(1, NY)]
        self.zs = [self.z] + [lax.rem(self.z + d, NZ) for d in range(1, NZ)]
        self.segs = [seg] + [lax.rem(seg + d, 8) for d in range(1, 8)]
        self.za = [z * 4 for z in self.zs]
        self.xb = [32 + x * 8 for x in self.xs]
        self.yc = [64 + y * 8 for y in self.ys]
        self.y2 = [y * 2 for y in self.ys]
        self.x2 = [x * 2 for x in self.xs]
        self.half = [z // 4 for z in self.zs]
        self.low = [mult(lax.rem(z, 4) * FEAT, FEAT) for z in self.zs]
        self.quarter = [lax.rem(z, 4) for z in self.zs]
        self.known = {}

    def at(self, dx=0, dy=0, dz=0, sibling=False):
        key = (dx % NX, dy % NY, dz % NZ, sibling)
        if key not in self.known:
            dx, dy, dz, _ = key
            c = self.other if sibling else self.c
            self.known[key] = (self.ys[dy] * 2 + c, self.zs[dz] * NX + self.xs[dx])
        return self.known[key]

    def brick(self, part, ahead, rel):
        if part == "a":
            return self.za[ahead % NZ] + self.ys[rel % NY]
        if part == "b":
            return self.xb[ahead % NX] + self.y2[rel % NY]
        return self.yc[ahead % NY] + self.x2[rel % NX]

    def weight(self, part, ahead, rel):
        if part == "a":
            return self.zs[ahead % NZ]
        if part == "b":
            return 8 + self.x2[ahead % NX]
        return 16 + self.x2[rel % NX]

    def row(self, part, ahead, rel):
        return self.ys[(ahead if part == "c" else rel) % NY]


def enter(devices):
    barrier = pltpu.get_barrier_semaphore()
    for device in devices:
        pl.semaphore_signal(barrier, inc=1, device_id=device, device_id_type=MESH)
    return lambda: pl.semaphore_wait(barrier, len(devices))


SIZE = {"a": 1, "b": 2, "c": 2}
PARTS = ("a", "b", "c")


def ring_to(p, part, sign):
    return {"a": p.at(dz=sign), "b": p.at(dx=sign), "c": p.at(dy=sign)}[part]


def gather_order(part, sign):
    hops = 3 if part == "a" else 1
    rows, last = ((0, 1, 3, 2), (0, 1)) if sign > 0 else ((0, 3, 2, 1), (3, 2))
    return [(h, r) for h in range(1, hops + 1) for r in rows] + [(hops + 1, r) for r in last]


def scatter_order(part, sign):
    if part == "a":
        rows, last = ((0, 1, 2, 3), (2, 3)) if sign > 0 else ((2, 3, 0, 1), (0, 1))
        return [(4, r) for r in last] + [(h, r) for h in (3, 2, 1) for r in rows]
    rows, last = ((1, 2, 3, 0), (2, 0)) if sign > 0 else ((2, 1, 3, 0), (1, 3))
    return [(2, r) for r in last] + [(1, r) for r in rows]


def mult(value, of):
    return pl.multiple_of(value, of)


class Copies:
    def __init__(self, send, recv):
        self.send, self.recv = send, recv
        self.index = {}
        self.sent = []

    def number(self, key):
        return self.index.setdefault(key, len(self.index))

    def make(self, key, src, dst, device):
        i = self.number(key)
        return pltpu.make_async_remote_copy(
            src_ref=src,
            dst_ref=dst,
            send_sem=self.send.at[i],
            recv_sem=self.recv.at[i],
            device_id=device,
            device_id_type=MESH,
        )

    def start(self, key, src, dst, device):
        copy = self.make(key, src, dst, device)
        copy.start()
        self.sent.append(copy)

    def arrived(self, key, ref, device):
        self.make(key, ref, ref, device).wait_recv()

    def drain(self):
        for copy in self.sent:
            copy.wait_send()
        self.sent.clear()

    def take(self, start):
        kept, self.sent = self.sent, []
        start()
        taken, self.sent = self.sent, kept
        return taken


class Gather:
    def __init__(self, name, place, copies, buf):
        self.name, self.at, self.copies, self.buf = name, place, copies, buf

    def key(self, *rest):
        return (self.name,) + rest

    def atoms(self, dx, dz):
        p = self.at
        own = mult(p.xs[dx % NX] * FEAT, FEAT)
        half, low = p.half[dz % NZ], p.low[dz % NZ]
        return (
            self.buf.at[p.c, p.za[dz % NZ] + p.y, pl.ds(own, FEAT)],
            self.buf.at[p.c, p.xb[dx % NX] + p.y2[0] + half, pl.ds(low, FEAT)],
            self.buf.at[p.c, p.yc[0] + p.x2[dx % NX] + half, pl.ds(low, FEAT)],
        )

    def put_own(self, block_t):
        for k, ref in enumerate(self.atoms(0, 0)):
            ref[...] = block_t[k * FEAT : (k + 1) * FEAT]

    def send_first(self):
        p = self.at
        a, b, c = self.atoms(0, 0)
        for d in range(1, NX):
            self.copies.start(self.key("a1", d), a, a, p.at(dx=d))
        for d in range(1, NZ):
            self.copies.start(self.key("b1", d), b, b, p.at(dz=d))
            self.copies.start(self.key("c1", d), c, c, p.at(dz=d))

    def wait_first_a(self):
        p = self.at
        for d in range(1, NX):
            a, _, _ = self.atoms(-d, 0)
            self.copies.arrived(self.key("a1", d), a, p.at(dx=-d))

    def wait_first_bc(self):
        p = self.at
        for d in range(1, NZ):
            _, b, c = self.atoms(0, -d)
            self.copies.arrived(self.key("b1", d), b, p.at(dz=-d))
            self.copies.arrived(self.key("c1", d), c, p.at(dz=-d))

    def second(self, part, rel):
        p = self.at
        base = p.brick(part, 0, rel)
        return self.buf.at[p.c, base] if part == "a" else self.buf.at[p.c, pl.ds(base, 2)]

    def half(self, part, rel, sign):
        block = self.second(part, rel)
        if part == "a":
            return block.at[pl.ds(0 if sign > 0 else 128, 128)]
        return block.at[pl.ds(0 if sign > 0 else 1, 1)]

    def second_to(self, part, sign):
        return self.at.at(dx=sign) if part == "c" else self.at.at(dy=sign)

    def send_second(self, part):
        block = self.second(part, 0)
        for sign in (1, -1):
            self.copies.start(self.key(part + "2", sign), block, block, self.second_to(part, sign))

    def second_near(self, part):
        for sign in (-1, 1):
            rel = -sign % 4
            self.copies.arrived(
                self.key(part + "2", sign), self.second(part, rel), self.second_to(part, -sign)
            )
            half = self.half(part, rel, sign)
            self.copies.start(self.key(part + "2far", sign), half, half, self.second_to(part, sign))
            self.send_own(part, (rel,))

    def second_far(self, part):
        for sign in (1, -1):
            half = self.half(part, 2, sign)
            self.copies.arrived(
                self.key(part + "2far", sign), half, self.second_to(part, -sign)
            )
        self.send_own(part, (2,))
        ref = self.span(part, self.at.c)
        self.copies.start(self.key("own", part), ref, ref, self.at.at(sibling=True))

    def chunk(self, part, base):
        return self.buf.at[self.at.c, pl.ds(base, SIZE[part])]

    def base(self, part, back, rel):
        return self.at.brick(part, -back, rel)

    def span(self, part, c):
        p = self.at
        first, count = {
            "a": (p.za[0], 4), "b": (p.xb[0], 8), "c": (p.yc[0], 8)
        }[part]
        return self.buf.at[c, pl.ds(first, count)]

    def send_own(self, part, rels):
        for rel in rels:
            ref = self.chunk(part, self.base(part, 0, rel))
            for sign in (1, -1):
                self.copies.start(self.key(part, sign, 1, rel), ref, ref, ring_to(self.at, part, sign))

    def messages(self, s, u):
        found = []
        if 0 <= s < 14:
            found += [("a", sign) + gather_order("a", sign)[s] for sign in (1, -1)]
        if 0 <= u < 12:
            part = ("b", "c")[u % 2]
            found += [(part, sign) + gather_order(part, sign)[u // 2] for sign in (1, -1)]
        return found

    def ring_round(self, s, u):
        for part, sign, hop, rel in self.messages(s, u):
            ref = self.chunk(part, self.base(part, sign * hop, rel))
            self.copies.arrived(self.key(part, sign, hop, rel), ref, ring_to(self.at, part, -sign))
            if (hop + 1, rel) in gather_order(part, sign):
                self.copies.start(
                    self.key(part, sign, hop + 1, rel), ref, ref, ring_to(self.at, part, sign)
                )
            self.copies.start(
                self.key("sib", part, sign, hop, rel), ref, ref, self.at.at(sibling=True)
            )

    def wait_other(self, s, u):
        p = self.at
        for part, sign, hop, rel in self.messages(s, u):
            ref = self.buf.at[p.other, pl.ds(self.base(part, sign * hop, rel), SIZE[part])]
            self.copies.arrived(self.key("sib", part, sign, hop, rel), ref, p.at(sibling=True))

    def wait_other_own(self):
        for part in ("a", "b", "c"):
            self.copies.arrived(
                self.key("own", part), self.span(part, self.at.other), self.at.at(sibling=True)
            )

    def both(self, b):
        return jnp.concatenate([self.buf[0, b], self.buf[1, b]], axis=1)

    def multiply_single(self, weights, total, b, w, row):
        total[row] += dot(weights(w), self.both(b))

    def multiply_chunk(self, weights, total, b, w, row):
        rhs = jnp.concatenate([self.both(b), self.both(b + 1)], axis=0)
        total[row] += dot(jnp.concatenate([weights(w), weights(w + 1)], axis=1), rhs)

    def multiply_own(self, weights, total):
        p = self.at

        def step(t, carry):
            self.multiply_single(weights, total, p.za[0] + t, p.z, t)
            self.multiply_chunk(weights, total, p.xb[0] + 2 * t, 8 + p.x2[0], t)
            self.multiply_chunk(weights, total, p.yc[0] + 2 * t, 16 + 2 * t, p.y)
            return carry

        lax.fori_loop(0, 4, step, 0)

    def multiply_round(self, weights, total, s, u):
        p = self.at
        messages = self.messages(s, u)
        if not messages:
            return
        facts = [
            [f(part, -sign * hop, rel) for f in (p.brick, p.weight, p.row)]
            for part, sign, hop, rel in messages
        ]

        def step(t, carry):
            def of(i):
                return [jnp.where(t == 0, u, v) for u, v in zip(facts[i], facts[i + 1])]

            if messages[0][0] == "a":
                self.multiply_single(weights, total, *of(0))
            if messages[-1][0] != "a":
                self.multiply_chunk(weights, total, *of(len(facts) - 2))
            return carry

        lax.fori_loop(0, 2, step, 0)


def load_blocks(hbm, part_ref, sem):
    for z in range(NZ):
        pltpu.make_async_copy(hbm.at[z, :, 0], part_ref(z), sem).start()
    for x in range(NX):
        for h in range(2):
            for part, first in ((1, 8), (2, 16)):
                pltpu.make_async_copy(
                    hbm.at[pl.ds(h * 4, 4), x, part], part_ref(first + x * 2 + h), sem
                ).start()


class Scatter:
    def __init__(
        self, name, first, place, copies, lhs, rhs, pairs, ring_a, ring_bc, mine, stage, bufs
    ):
        self.name, self.first, self.at, self.copies = name, first, place, copies
        self.lhs, self.rhs, self.pairs = lhs, rhs, pairs
        self.ring_a, self.ring_bc, self.mine, self.stage = ring_a, ring_bc, mine, stage
        self.two, self.three_a, self.three_bc, self.sums = bufs

    def key(self, *rest):
        return (self.name,) + rest

    def base(self, part, ahead, rel):
        return self.at.brick(part, ahead, rel)

    def chunks(self, kind, j):
        part, n = ("a", j) if kind == "a" else (("b", "c")[j % 2], j // 2)
        count = 14 if kind == "a" else 6
        if n < count:
            return [(part, sign) + scatter_order(part, sign)[n] for sign in (1, -1)]
        return [(part, 0, 0, rel) for rel in ((1, 2), (3, 0))[n - count]]

    def place_of(self, chunk):
        kind = "a" if chunk[0] == "a" else "bc"
        for j in range(16):
            chunks = self.chunks(kind, j)
            if chunk in chunks:
                k = chunks.index(chunk)
                return (self.first + j) % SLOTS, (k if kind == "a" else 2 + 2 * k)

    def produce(self, kind, j):
        p = self.at
        slot = (self.first + j) % SLOTS
        chunks = self.chunks(kind, j)
        bases = [self.base(part, sign * hop, rel) for part, sign, hop, rel in chunks]
        facts = [
            [f(part, sign * hop, rel) for f in (p.weight, p.row)]
            for part, sign, hop, rel in chunks
        ]

        def one(w, rhs, at):
            value = dot(self.lhs(w), rhs).astype(BF)
            self.mine[slot, at] = value[:, 0:TOK]
            self.stage[slot, at] = value[:, TOK:]

        def rhs_of(row):
            return jnp.concatenate([self.rhs(row, p.c), self.rhs(row, p.other)], axis=1)

        def step(t, carry):
            w, row = [jnp.where(t == 0, u, v) for u, v in zip(*facts)]
            rhs = rhs_of(row)
            if kind == "a":
                one(w, rhs, t)
            else:
                one(w, rhs, 2 + 2 * t)
                one(w + 1, rhs, 3 + 2 * t)
            return carry

        lax.fori_loop(0, 2, step, 0)
        for chunk, base in zip(chunks, bases):
            _, at = self.place_of(chunk)
            size = SIZE[chunk[0]]
            self.copies.start(
                self.key("sib") + chunk,
                self.stage.at[slot, pl.ds(at, size)],
                self.pairs.at[pl.ds(base, size)],
                p.at(sibling=True),
            )

    def landing(self, part, sign, i):
        side = 0 if sign > 0 else 1
        if part == "a":
            return self.ring_a.at[side, pl.ds(i, 1)]
        return self.ring_bc.at[("b", "c").index(part), side, pl.ds(2 * i, 2)]

    def came(self, part, sign, i):
        ref = self.landing(part, sign, i)
        self.copies.arrived(self.key(part, sign, i), ref, ring_to(self.at, part, -sign))
        return ref

    def gather_up(self, chunk, base, arrivals):
        part = chunk[0]
        size = SIZE[part]
        ref = self.pairs.at[pl.ds(base, size)]
        self.copies.arrived(self.key("sib") + chunk, ref, self.at.at(sibling=True))
        slot, at = self.place_of(chunk)
        refs = [self.came(part, sign, i) for sign, i in arrivals]
        for t in range(size):
            value = self.mine[slot, at + t].astype(F32) + self.pairs[base + t].astype(F32)
            for came in refs:
                value += came[t].astype(F32)
            self.pairs[base + t] = value.astype(BF)
        return ref

    def send_round(self, kind, j):
        for chunk in self.chunks(kind, j):
            part, sign, hop, rel = chunk
            if sign == 0:
                continue
            order = scatter_order(part, sign)
            arrivals = [(sign, order.index((hop + 1, rel)))] if (hop + 1, rel) in order else []
            i = order.index((hop, rel))
            ref = self.gather_up(chunk, self.base(part, sign * hop, rel), arrivals)
            self.copies.start(
                self.key(part, sign, i), ref, self.landing(part, sign, i), ring_to(self.at, part, sign)
            )

    def finish_ring(self, part, rels):
        for rel in rels:
            arrivals = [(sign, scatter_order(part, sign).index((1, rel))) for sign in (1, -1)]
            self.gather_up((part, 0, 0, rel), self.base(part, 0, rel), arrivals)
            if rel:
                bricks, slot, device = self.second(part, rel)
                self.copies.start(
                    self.key(part + "2", rel),
                    self.pairs.at[bricks],
                    self.two.at[rel - 1, slot],
                    device,
                )

    def second(self, part, d):
        p = self.at
        base = p.brick(part, 0, d)
        if part == "a":
            return pl.ds(base, 1), pl.ds(0, 1), p.at(dy=d)
        if part == "b":
            return pl.ds(base, 2), pl.ds(1, 2), p.at(dy=d)
        return pl.ds(base, 2), pl.ds(3, 2), p.at(dx=d)

    def sum_second(self, part):
        p = self.at
        slots = {"a": (0,), "b": (1, 2), "c": (3, 4)}[part]
        for d in range(1, 4):
            _, slot, _ = self.second(part, d)
            device = p.at(dx=-d) if part == "c" else p.at(dy=-d)
            self.copies.arrived(self.key(part + "2", d), self.two.at[d - 1, slot], device)
        for t, slot in enumerate(slots):
            mine = p.brick(part, 0, 0) + t
            value = self.pairs[mine].astype(F32)
            for d in range(3):
                value += self.two[d, slot].astype(F32)
            self.sums[slot] = value.astype(BF).reshape(4, 64, TOK)
        if part == "a":
            for d in range(1, NX):
                self.copies.start(
                    self.key("a3", d), self.sums.at[0, p.xs[d]], self.three_a.at[d - 1], p.at(dx=d)
                )
            return
        first, i = {"b": (1, 0), "c": (3, 1)}[part]
        for d in range(1, NZ):
            self.copies.start(
                self.key(part + "3", d),
                self.sums.at[first + p.half[d], p.quarter[d]],
                self.three_bc.at[i, d - 1],
                p.at(dz=d),
            )

    def sum_third(self, part, out_ref):
        p = self.at
        if part == "a":
            value = self.sums[0, p.x].astype(F32)
            for d in range(1, NX):
                self.copies.arrived(self.key("a3", d), self.three_a.at[d - 1], p.at(dx=-d))
                value += self.three_a[d - 1].astype(F32)
            out_ref[0:FEAT] = value.astype(BF)
            return
        first, i = {"b": (1, 0), "c": (3, 1)}[part]
        value = self.sums[first + p.half[0], p.quarter[0]].astype(F32)
        for d in range(1, NZ):
            self.copies.arrived(self.key(part + "3", d), self.three_bc.at[i, d - 1], p.at(dz=-d))
            value += self.three_bc[i, d - 1].astype(F32)
        out_ref[(i + 1) * FEAT : (i + 2) * FEAT] = value.astype(BF)


def moe_kernel(
    logits_ref,
    routes_ref,
    losses_ref,
    tok_ref,
    cot_ref,
    gate_hbm,
    up_hbm,
    down_hbm,
    out_ref,
    in_ref,
    dgrad_hbm,
    tok_buf,
    cot_buf,
    wgu,
    wd,
    wdt,
    flat,
    total,
    hgrad,
    scaled,
    hid,
    grads,
    weighing,
    meta,
    ring_a,
    ring_bc,
    mine,
    stage,
    two,
    three_a,
    three_bc,
    sums,
    wsem,
    osem,
    free,
    send,
    recv,
    send2,
    recv2,
):
    p = Place()
    copies = Copies(send, recv)
    back = Copies(send2, recv2)
    tok = Gather("tok", p, copies, tok_buf)
    cot = Gather("cot", p, copies, cot_buf)
    here = p.at()[1]
    far = [(p.segs[d], here) for d in range(1, 8)]
    line = [p.at(dx=d) for d in range(1, NX)] + [p.at(dz=d) for d in range(1, NZ)]
    entered = enter(line + far)

    def load_gate_up():
        load_blocks(gate_hbm, lambda w: wgu.at[w, 0], wsem.at[0])
        load_blocks(up_hbm, lambda w: wgu.at[w, 1], wsem.at[0])

    def wait_gate_up():
        pltpu.make_async_copy(wgu, wgu, wsem.at[0]).wait()

    load_gate_up()
    pltpu.make_async_copy(down_hbm, flat, wsem.at[1]).start()

    tok.put_own(tok_ref)
    cot.put_own(cot_ref)
    share = jax.nn.sigmoid(logits_ref[0:1] - logits_ref[1:2])
    scale = losses_ref[...].astype(F32) / 4096.0
    weighing[...] = jnp.zeros_like(weighing)
    for e in range(8):
        combine = jnp.where(routes_ref[0:1] == e, share, 0.0) + jnp.where(
            routes_ref[1:2] == e, 1.0 - share, 0.0
        )
        weighing[e, 0:1] = combine
        weighing[e, 1:2] = combine * scale
    meta[p.seg] = weighing[p.seg]
    total[...] = jnp.zeros_like(total)
    hgrad[...] = jnp.zeros_like(hgrad)
    entered()

    tok.send_first()
    for d in range(1, 8):
        copies.start(("meta", d), weighing.at[p.segs[d]], meta.at[p.seg], far[d - 1])

    def turn_gu(w, carry):
        for k in range(2):
            block = wgu[w, k].reshape(256, 256)
            wgu[w, k] = block.T.reshape(4, 64, 256)
        return carry

    def turn_down(i, carry):
        block = flat[:, pl.ds(mult(i * 384, 384), 384)].T
        z, x = i // 2, (i % 2) * 2
        for k in range(2):
            rows = block[k * 192 : (k + 1) * 192]
            wd[z, x + k] = rows[0:64]
            wd[8 + (x + k) * 2 + z // 4, z % 4] = rows[64:128]
            wd[16 + (x + k) * 2 + z // 4, z % 4] = rows[128:192]
        return carry

    def turn_back(w, carry):
        wdt[w] = wd[w].reshape(256, 256).T
        return carry

    def w_gu(w):
        return wgu[w].reshape(512, 256)

    def w_down(w):
        return wdt[w]

    def activate(i, carry):
        y, r = i // 4, i % 4
        low = mult(r * 64, 64)
        gate = total[y, pl.ds(low, 64)]
        upward = total[y, pl.ds(mult(256 + r * 64, 64), 64)]
        first, second = meta[2 * y], meta[2 * y + 1]
        share = jnp.concatenate([first[0:1], second[0:1]], axis=1)
        scale = jnp.concatenate([first[1:2], second[1:2]], axis=1)
        sigma = jax.nn.sigmoid(gate)
        active = gate * sigma
        hidden = active * upward
        weighted = (hidden * share).astype(BF)
        hid[y, 0, pl.ds(low, 64)] = weighted[:, 0:128]
        hid[y, 1, pl.ds(low, 64)] = weighted[:, 128:256]
        scaled[y, pl.ds(low, 64)] = (hidden * scale).astype(BF)
        total[y, pl.ds(low, 64)] = upward * (sigma * (1.0 + gate * (1.0 - sigma))) * scale
        total[y, pl.ds(mult(256 + r * 64, 64), 64)] = active * scale
        return carry

    def backward(i, carry):
        y, r = i // 4, i % 4
        low = mult(r * 64, 64)
        high = mult(256 + r * 64, 64)
        grad = hgrad[y, pl.ds(low, 64)]
        gate_grad = (grad * total[y, pl.ds(low, 64)]).astype(BF)
        up_grad = (grad * total[y, pl.ds(high, 64)]).astype(BF)
        for c in range(2):
            grads[y, c, pl.ds(low, 64)] = gate_grad[:, c * 128 : (c + 1) * 128]
            grads[y, c, pl.ds(high, 64)] = up_grad[:, c * 128 : (c + 1) * 128]
        return carry

    def weight_grad(i, carry):
        z, x = i // 2, (i % 2) * 2
        low = mult((z % 4) * FEAT, FEAT)
        acc = jnp.zeros((256, 384), F32)
        for y in range(NY):
            halves = []
            for c in range(2):
                rows = []
                for k in range(2):
                    xk = x + k
                    rows.append(cot_buf[c, z * 4 + y, pl.ds(mult(xk * FEAT, FEAT), FEAT), :])
                    rows.append(cot_buf[c, 32 + (xk * 4 + y) * 2 + z // 4, pl.ds(low, FEAT), :])
                    rows.append(cot_buf[c, 64 + (y * 4 + xk) * 2 + z // 4, pl.ds(low, FEAT), :])
                halves.append(jnp.concatenate(rows, axis=0))
            acc += dot_nt(scaled[y], jnp.concatenate(halves, axis=1))
        flat[:, pl.ds(mult(i * 384, 384), 384)] = acc.astype(BF)
        return carry

    pairs = tok_buf

    def lhs_in(w):
        return jnp.concatenate(
            [wgu[w, 0].reshape(256, 256), wgu[w, 1].reshape(256, 256)], axis=1
        )

    def bufs(i):
        return (two.at[i], three_a.at[i], three_bc.at[i], sums.at[i])

    out = Scatter(
        "out", 0, p, back, lambda w: wd[w].reshape(256, 256), lambda y, c: hid[y, c],
        pairs.at[0], ring_a.at[0], ring_bc.at[0], mine, stage, bufs(0),
    )
    inp = Scatter(
        "in", 16, p, back, lhs_in, lambda y, c: grads[y, c],
        pairs.at[1], ring_a.at[1], ring_bc.at[1], mine, stage, bufs(1),
    )
    sent = {"a": [], "bc": []}

    def step_of(n):
        return (out, n) if n < 16 else (inp, n - 16)

    def produce(kind, n):
        if not 0 <= n < 32:
            return
        which, j = step_of(n)
        if n >= SLOTS:
            for copy in sent[kind][n - SLOTS]:
                copy.wait_send()
        sent[kind].append(back.take(lambda: which.produce(kind, j)))

    def turn(kind, n):
        if not 0 <= n < 32:
            return
        which, j = step_of(n)
        if kind == "a":
            if j < 14:
                which.send_round("a", j)
            else:
                which.finish_ring("a", ((1, 2), (3, 0))[j - 14])
        elif j < 12:
            which.send_round("bc", j)
        else:
            which.finish_ring(("b", "c")[j % 2], ((1, 2), (3, 0))[(j - 12) // 2])

    tok.wait_first_a()
    tok.send_second("a")
    tok.send_own("a", (0,))
    wait_gate_up()
    lax.fori_loop(0, 8, turn_gu, 0)
    tok.second_near("a")
    tok.wait_first_bc()
    for part in ("b", "c"):
        tok.send_second(part)
        tok.send_own(part, (0,))
    tok.second_far("a")
    lax.fori_loop(8, 16, turn_gu, 0)

    lag, first_bc, first_a = 3, 23, 27
    for n in range(first_a + 32):
        if n < 14:
            tok.ring_round(n, -1)
        elif n < 28:
            cot.ring_round(n - 14, -1)
        if lag <= n < 12 + lag:
            tok.ring_round(-1, n - lag)
        elif 12 + lag <= n < 24 + lag:
            cot.ring_round(-1, n - 12 - lag)
        if n == 0:
            lax.fori_loop(16, 24, turn_gu, 0)
        if n == 1:
            tok.second_near("b")
        if n == 2:
            tok.second_near("c")
            cot.send_first()
        if n == 3:
            tok.second_far("b")
            tok.second_far("c")
            pltpu.make_async_copy(down_hbm, flat, wsem.at[1]).wait()
        if n == 4:
            tok.wait_other_own()
            tok.multiply_own(w_gu, total)
        if 2 <= n <= 17:
            k = n - 2
            tok.wait_other(k, k - lag)
            tok.multiply_round(w_gu, total, k, k - lag)
        if 5 <= n < 9:
            lax.fori_loop(4 * n - 20, 4 * n - 16, turn_down, 0)
        if 9 <= n < 13:
            lax.fori_loop(6 * n - 54, 6 * n - 48, turn_back, 0)
        if n == 7:
            cot.wait_first_a()
            cot.send_second("a")
            cot.wait_first_bc()
            cot.send_second("b")
            cot.send_second("c")
        if n == 10:
            cot.send_own("b", (0,))
            cot.second_near("b")
            cot.send_own("c", (0,))
            cot.second_near("c")
            cot.send_own("a", (0,))
            cot.second_near("a")
        if n == 11:
            cot.second_far("a")
        if n == 12:
            cot.second_far("b")
            cot.second_far("c")
        if n == 17:
            before, copies.sent = copies.sent, []
            load_gate_up()
            for d in range(1, 8):
                copies.arrived(("meta", d), meta.at[p.segs[8 - d]], far[7 - d])
            lax.fori_loop(0, 16, activate, 0)
        if n == 17:
            cot.wait_other_own()
            cot.multiply_own(w_down, hgrad)
        if 16 <= n <= 29:
            k = n - 2
            cot.wait_other(k - 14, k - 12 - lag)
            cot.multiply_round(w_down, hgrad, k - 14, k - 12 - lag)
        if n == 20:
            for copy in before:
                copy.wait_send()
            pl.semaphore_signal(
                free, inc=1, device_id=p.at(sibling=True), device_id_type=MESH
            )
        if n == 21:
            pl.semaphore_wait(free, 1)
        if n == 29:
            lax.fori_loop(0, 16, backward, 0)
        if 29 <= n < 37:
            lax.fori_loop(2 * n - 58, 2 * n - 56, weight_grad, 0)
        if n == 37:
            dgrad = pltpu.make_async_copy(flat, dgrad_hbm, osem)
            dgrad.start()
            wait_gate_up()
        turn("bc", n - first_bc)
        produce("bc", n - first_bc + 2)
        turn("a", n - first_a)
        produce("a", n - first_a + 2)
        for which, start in ((out, 0), (inp, 16)):
            k = n - first_bc - start
            if k == 17:
                which.sum_second("b")
            if k == 18:
                which.sum_second("c")
        if n == first_a + 18:
            out.sum_second("a")
        if n == first_a + 22:
            for part in PARTS:
                out.sum_third(part, out_ref)
    inp.sum_second("a")
    for part in PARTS:
        inp.sum_third(part, in_ref)
    for kind in ("a", "bc"):
        for group in sent[kind][32 - SLOTS :]:
            for copy in group:
                copy.wait_send()
    copies.drain()
    back.drain()
    dgrad.wait()


def per_device(
    tokens, router_logits, routes, loss_weights, cotangent, gate_weight, up_weight, down_weight
):
    gate5 = gate_weight.reshape(NZ, NX, 3, FEAT, 256)
    up5 = up_weight.reshape(NZ, NX, 3, FEAT, 256)
    down2 = down_weight.reshape(256, 6144)
    vmem = pl.BlockSpec(memory_space=pltpu.VMEM)
    hbm = pl.BlockSpec(memory_space=pl.ANY)
    n_gather, n_scatter = 288, 288

    output, input_grad, dgrad = pl.pallas_call(
        moe_kernel,
        name="moe",
        out_shape=(
            jax.ShapeDtypeStruct((192, TOK), BF),
            jax.ShapeDtypeStruct((192, TOK), BF),
            jax.ShapeDtypeStruct((256, 6144), BF),
        ),
        in_specs=[vmem] * 5 + [hbm] * 3,
        out_specs=(vmem, vmem, hbm),
        scratch_shapes=[
            pltpu.VMEM((2, 96, 256, TOK), BF),
            pltpu.VMEM((2, 96, 256, TOK), BF),
            pltpu.VMEM((24, 2, 4, 64, 256), BF),
            pltpu.VMEM((24, 4, 64, 256), BF),
            pltpu.VMEM((24, 256, 256), BF),
            pltpu.VMEM((256, 6144), BF),
            pltpu.VMEM((NY, 512, 256), F32),
            pltpu.VMEM((NY, 256, 256), F32),
            pltpu.VMEM((NY, 256, 256), BF),
            pltpu.VMEM((NY, 2, 256, TOK), BF),
            pltpu.VMEM((NY, 2, 512, TOK), BF),
            pltpu.VMEM((8, 8, TOK), F32),
            pltpu.VMEM((8, 8, TOK), F32),
            pltpu.VMEM((2, 2, 14, 256, TOK), BF),
            pltpu.VMEM((2, 2, 2, 12, 256, TOK), BF),
            pltpu.VMEM((SLOTS, 6, 256, TOK), BF),
            pltpu.VMEM((SLOTS, 6, 256, TOK), BF),
            pltpu.VMEM((2, 3, 5, 256, TOK), BF),
            pltpu.VMEM((2, 3, 64, TOK), BF),
            pltpu.VMEM((2, 2, 7, 64, TOK), BF),
            pltpu.VMEM((2, 5, 4, 64, TOK), BF),
            pltpu.SemaphoreType.DMA((2,)),
            pltpu.SemaphoreType.DMA,
            pltpu.SemaphoreType.REGULAR,
            pltpu.SemaphoreType.DMA((n_gather,)),
            pltpu.SemaphoreType.DMA((n_gather,)),
            pltpu.SemaphoreType.DMA((n_scatter,)),
            pltpu.SemaphoreType.DMA((n_scatter,)),
        ],
        compiler_params=pltpu.CompilerParams(
            collective_id=1, has_side_effects=True, vmem_limit_bytes=62 * 2**20
        ),
    )(
        router_logits.T,
        routes.T,
        loss_weights.reshape(1, TOK),
        tokens.T,
        cotangent.T,
        gate5,
        up5,
        down2,
    )
    return (output.T, input_grad.T, dgrad.reshape(1, 256, 6144))


def solution(mesh):
    in_specs = (
        P("segment", "fsdp"),
        P("segment", None),
        P("segment", None),
        P("segment"),
        P("segment", "fsdp"),
        P("segment", None, "fsdp"),
        P("segment", None, "fsdp"),
        P("segment", "fsdp", None),
    )
    out_specs = (P("segment", "fsdp"), P("segment", "fsdp"), P("segment", "fsdp", None))
    return jax.shard_map(
        per_device, mesh=mesh, in_specs=in_specs, out_specs=out_specs, check_vma=False
    )
```

```python
import functools

import jax
import jax.numpy as jnp
from jax import lax
from jax.experimental import pallas as pl
from jax.experimental.pallas import tpu as pltpu
from jax.sharding import PartitionSpec as P

MESH = pl.DeviceIdType.MESH
BF = jnp.bfloat16
F32 = jnp.float32
NX, NY, NZ = 4, 4, 8
SLOTS = 4
FEAT, TOK = 64, 128


def dot(a, b):
    return lax.dot_general(a, b, (((1,), (0,)), ((), ())), preferred_element_type=F32)


def dot_nt(a, b):
    return lax.dot_general(a, b, (((1,), (1,)), ((), ())), preferred_element_type=F32)


class Place:
    def __init__(self):
        seg, fsdp = lax.axis_index("segment"), lax.axis_index("fsdp")
        self.seg = seg
        self.y, self.c = seg // 2, seg % 2
        self.z, self.x = fsdp // NX, fsdp % NX
        self.other = 1 - self.c
        self.xs = [self.x] + [lax.rem(self.x + d, NX) for d in range(1, NX)]
        self.ys = [self.y] + [lax.rem(self.y + d, NY) for d in range(1, NY)]
        self.zs = [self.z] + [lax.rem(self.z + d, NZ) for d in range(1, NZ)]
        self.segs = [seg] + [lax.rem(seg + d, 8) for d in range(1, 8)]
        self.za = [z * 4 for z in self.zs]
        self.xb = [32 + x * 8 for x in self.xs]
        self.yc = [64 + y * 8 for y in self.ys]
        self.y2 = [y * 2 for y in self.ys]
        self.x2 = [x * 2 for x in self.xs]
        self.half = [z // 4 for z in self.zs]
        self.low = [mult(lax.rem(z, 4) * FEAT, FEAT) for z in self.zs]
        self.quarter = [lax.rem(z, 4) for z in self.zs]
        self.known = {}

    def at(self, dx=0, dy=0, dz=0, sibling=False):
        key = (dx % NX, dy % NY, dz % NZ, sibling)
        if key not in self.known:
            dx, dy, dz, _ = key
            c = self.other if sibling else self.c
            self.known[key] = (self.ys[dy] * 2 + c, self.zs[dz] * NX + self.xs[dx])
        return self.known[key]

    def brick(self, part, ahead, rel):
        if part == "a":
            return self.za[ahead % NZ] + self.ys[rel % NY]
        if part == "b":
            return self.xb[ahead % NX] + self.y2[rel % NY]
        return self.yc[ahead % NY] + self.x2[rel % NX]

    def weight(self, part, ahead, rel):
        if part == "a":
            return self.zs[ahead % NZ]
        if part == "b":
            return 8 + self.x2[ahead % NX]
        return 16 + self.x2[rel % NX]

    def row(self, part, ahead, rel):
        return self.ys[(ahead if part == "c" else rel) % NY]


def enter(devices):
    barrier = pltpu.get_barrier_semaphore()
    for device in devices:
        pl.semaphore_signal(barrier, inc=1, device_id=device, device_id_type=MESH)
    return lambda: pl.semaphore_wait(barrier, len(devices))


SIZE = {"a": 1, "b": 2, "c": 2}
PARTS = ("a", "b", "c")


def ring_to(p, part, sign):
    return {"a": p.at(dz=sign), "b": p.at(dx=sign), "c": p.at(dy=sign)}[part]


def gather_order(part, sign):
    hops = 3 if part == "a" else 1
    rows, last = ((0, 1, 3, 2), (0, 1)) if sign > 0 else ((0, 3, 2, 1), (3, 2))
    return [(h, r) for h in range(1, hops + 1) for r in rows] + [(hops + 1, r) for r in last]


def scatter_order(part, sign):
    if part == "a":
        rows, last = ((0, 1, 2, 3), (2, 3)) if sign > 0 else ((2, 3, 0, 1), (0, 1))
        return [(4, r) for r in last] + [(h, r) for h in (3, 2, 1) for r in rows]
    rows, last = ((1, 2, 3, 0), (2, 0)) if sign > 0 else ((2, 1, 3, 0), (1, 3))
    return [(2, r) for r in last] + [(1, r) for r in rows]


def mult(value, of):
    return pl.multiple_of(value, of)


class Copies:
    def __init__(self, send, recv):
        self.send, self.recv = send, recv
        self.index = {}
        self.sent = []

    def number(self, key):
        return self.index.setdefault(key, len(self.index))

    def make(self, key, src, dst, device):
        i = self.number(key)
        return pltpu.make_async_remote_copy(
            src_ref=src,
            dst_ref=dst,
            send_sem=self.send.at[i],
            recv_sem=self.recv.at[i],
            device_id=device,
            device_id_type=MESH,
        )

    def start(self, key, src, dst, device):
        copy = self.make(key, src, dst, device)
        copy.start()
        self.sent.append(copy)

    def arrived(self, key, ref, device):
        self.make(key, ref, ref, device).wait_recv()

    def drain(self):
        for copy in self.sent:
            copy.wait_send()
        self.sent.clear()

    def take(self, start):
        kept, self.sent = self.sent, []
        start()
        taken, self.sent = self.sent, kept
        return taken


class Gather:
    def __init__(self, name, place, copies, buf):
        self.name, self.at, self.copies, self.buf = name, place, copies, buf

    def key(self, *rest):
        return (self.name,) + rest

    def atoms(self, dx, dz):
        p = self.at
        own = mult(p.xs[dx % NX] * FEAT, FEAT)
        half, low = p.half[dz % NZ], p.low[dz % NZ]
        return (
            self.buf.at[p.c, p.za[dz % NZ] + p.y, pl.ds(own, FEAT)],
            self.buf.at[p.c, p.xb[dx % NX] + p.y2[0] + half, pl.ds(low, FEAT)],
            self.buf.at[p.c, p.yc[0] + p.x2[dx % NX] + half, pl.ds(low, FEAT)],
        )

    def put_own(self, block_t):
        for k, ref in enumerate(self.atoms(0, 0)):
            ref[...] = block_t[k * FEAT : (k + 1) * FEAT]

    def send_first(self):
        p = self.at
        a, b, c = self.atoms(0, 0)
        for d in range(1, NX):
            self.copies.start(self.key("a1", d), a, a, p.at(dx=d))
        for d in range(1, NZ):
            self.copies.start(self.key("b1", d), b, b, p.at(dz=d))
            self.copies.start(self.key("c1", d), c, c, p.at(dz=d))

    def wait_first_a(self):
        p = self.at
        for d in range(1, NX):
            a, _, _ = self.atoms(-d, 0)
            self.copies.arrived(self.key("a1", d), a, p.at(dx=-d))

    def wait_first_bc(self):
        p = self.at
        for d in range(1, NZ):
            _, b, c = self.atoms(0, -d)
            self.copies.arrived(self.key("b1", d), b, p.at(dz=-d))
            self.copies.arrived(self.key("c1", d), c, p.at(dz=-d))

    def second(self, part, rel):
        p = self.at
        base = p.brick(part, 0, rel)
        return self.buf.at[p.c, base] if part == "a" else self.buf.at[p.c, pl.ds(base, 2)]

    def half(self, part, rel, sign):
        block = self.second(part, rel)
        if part == "a":
            return block.at[pl.ds(0 if sign > 0 else 128, 128)]
        return block.at[pl.ds(0 if sign > 0 else 1, 1)]

    def second_to(self, part, sign):
        return self.at.at(dx=sign) if part == "c" else self.at.at(dy=sign)

    def send_second(self, part):
        block = self.second(part, 0)
        for sign in (1, -1):
            self.copies.start(self.key(part + "2", sign), block, block, self.second_to(part, sign))

    def second_near(self, part):
        for sign in (-1, 1):
            rel = -sign % 4
            self.copies.arrived(
                self.key(part + "2", sign), self.second(part, rel), self.second_to(part, -sign)
            )
            half = self.half(part, rel, sign)
            self.copies.start(self.key(part + "2far", sign), half, half, self.second_to(part, sign))
            self.send_own(part, (rel,))

    def second_far(self, part):
        for sign in (1, -1):
            half = self.half(part, 2, sign)
            self.copies.arrived(
                self.key(part + "2far", sign), half, self.second_to(part, -sign)
            )
        self.send_own(part, (2,))
        ref = self.span(part, self.at.c)
        self.copies.start(self.key("own", part), ref, ref, self.at.at(sibling=True))

    def chunk(self, part, base):
        return self.buf.at[self.at.c, pl.ds(base, SIZE[part])]

    def base(self, part, back, rel):
        return self.at.brick(part, -back, rel)

    def span(self, part, c):
        p = self.at
        first, count = {
            "a": (p.za[0], 4), "b": (p.xb[0], 8), "c": (p.yc[0], 8)
        }[part]
        return self.buf.at[c, pl.ds(first, count)]

    def send_own(self, part, rels):
        for rel in rels:
            ref = self.chunk(part, self.base(part, 0, rel))
            for sign in (1, -1):
                self.copies.start(self.key(part, sign, 1, rel), ref, ref, ring_to(self.at, part, sign))

    def messages(self, s, u):
        found = []
        if 0 <= s < 14:
            found += [("a", sign) + gather_order("a", sign)[s] for sign in (1, -1)]
        if 0 <= u < 12:
            part = ("b", "c")[u % 2]
            found += [(part, sign) + gather_order(part, sign)[u // 2] for sign in (1, -1)]
        return found

    def ring_round(self, s, u):
        for part, sign, hop, rel in self.messages(s, u):
            ref = self.chunk(part, self.base(part, sign * hop, rel))
            self.copies.arrived(self.key(part, sign, hop, rel), ref, ring_to(self.at, part, -sign))
            if (hop + 1, rel) in gather_order(part, sign):
                self.copies.start(
                    self.key(part, sign, hop + 1, rel), ref, ref, ring_to(self.at, part, sign)
                )
            self.copies.start(
                self.key("sib", part, sign, hop, rel), ref, ref, self.at.at(sibling=True)
            )

    def wait_other(self, s, u):
        p = self.at
        for part, sign, hop, rel in self.messages(s, u):
            ref = self.buf.at[p.other, pl.ds(self.base(part, sign * hop, rel), SIZE[part])]
            self.copies.arrived(self.key("sib", part, sign, hop, rel), ref, p.at(sibling=True))

    def wait_other_own(self):
        for part in ("a", "b", "c"):
            self.copies.arrived(
                self.key("own", part), self.span(part, self.at.other), self.at.at(sibling=True)
            )

    def both(self, b):
        return jnp.concatenate([self.buf[0, b], self.buf[1, b]], axis=1)

    def multiply_single(self, weights, total, b, w, row):
        total[row] += dot(weights(w), self.both(b))

    def multiply_chunk(self, weights, total, b, w, row):
        rhs = jnp.concatenate([self.both(b), self.both(b + 1)], axis=0)
        total[row] += dot(jnp.concatenate([weights(w), weights(w + 1)], axis=1), rhs)

    def multiply_own(self, weights, total):
        p = self.at

        def step(t, carry):
            self.multiply_single(weights, total, p.za[0] + t, p.z, t)
            self.multiply_chunk(weights, total, p.xb[0] + 2 * t, 8 + p.x2[0], t)
            self.multiply_chunk(weights, total, p.yc[0] + 2 * t, 16 + 2 * t, p.y)
            return carry

        lax.fori_loop(0, 4, step, 0)

    def multiply_round(self, weights, total, s, u):
        p = self.at
        messages = self.messages(s, u)
        if not messages:
            return
        facts = [
            [f(part, -sign * hop, rel) for f in (p.brick, p.weight, p.row)]
            for part, sign, hop, rel in messages
        ]

        def step(t, carry):
            def of(i):
                return [jnp.where(t == 0, u, v) for u, v in zip(facts[i], facts[i + 1])]

            if messages[0][0] == "a":
                self.multiply_single(weights, total, *of(0))
            if messages[-1][0] != "a":
                self.multiply_chunk(weights, total, *of(len(facts) - 2))
            return carry

        lax.fori_loop(0, 2, step, 0)


def load_blocks(hbm, part_ref, sem):
    for z in range(NZ):
        pltpu.make_async_copy(hbm.at[z, :, 0], part_ref(z), sem).start()
    for x in range(NX):
        for h in range(2):
            for part, first in ((1, 8), (2, 16)):
                pltpu.make_async_copy(
                    hbm.at[pl.ds(h * 4, 4), x, part], part_ref(first + x * 2 + h), sem
                ).start()


class Scatter:
    def __init__(
        self, name, first, place, copies, lhs, rhs, pairs, ring_a, ring_bc, mine, stage, bufs
    ):
        self.name, self.first, self.at, self.copies = name, first, place, copies
        self.lhs, self.rhs, self.pairs = lhs, rhs, pairs
        self.ring_a, self.ring_bc, self.mine, self.stage = ring_a, ring_bc, mine, stage
        self.two, self.three_a, self.three_bc, self.sums = bufs

    def key(self, *rest):
        return (self.name,) + rest

    def base(self, part, ahead, rel):
        return self.at.brick(part, ahead, rel)

    def chunks(self, kind, j):
        part, n = ("a", j) if kind == "a" else (("b", "c")[j % 2], j // 2)
        count = 14 if kind == "a" else 6
        if n < count:
            return [(part, sign) + scatter_order(part, sign)[n] for sign in (1, -1)]
        return [(part, 0, 0, rel) for rel in ((1, 2), (3, 0))[n - count]]

    def place_of(self, chunk):
        kind = "a" if chunk[0] == "a" else "bc"
        for j in range(16):
            chunks = self.chunks(kind, j)
            if chunk in chunks:
                k = chunks.index(chunk)
                return (self.first + j) % SLOTS, (k if kind == "a" else 2 + 2 * k)

    def produce(self, kind, j):
        p = self.at
        slot = (self.first + j) % SLOTS
        chunks = self.chunks(kind, j)
        bases = [self.base(part, sign * hop, rel) for part, sign, hop, rel in chunks]
        facts = [
            [f(part, sign * hop, rel) for f in (p.weight, p.row)]
            for part, sign, hop, rel in chunks
        ]

        def one(w, rhs, at):
            value = dot(self.lhs(w), rhs).astype(BF)
            self.mine[slot, at] = value[:, 0:TOK]
            self.stage[slot, at] = value[:, TOK:]

        def rhs_of(row):
            return jnp.concatenate([self.rhs(row, p.c), self.rhs(row, p.other)], axis=1)

        def step(t, carry):
            w, row = [jnp.where(t == 0, u, v) for u, v in zip(*facts)]
            rhs = rhs_of(row)
            if kind == "a":
                one(w, rhs, t)
            else:
                one(w, rhs, 2 + 2 * t)
                one(w + 1, rhs, 3 + 2 * t)
            return carry

        lax.fori_loop(0, 2, step, 0)
        for chunk, base in zip(chunks, bases):
            _, at = self.place_of(chunk)
            size = SIZE[chunk[0]]
            self.copies.start(
                self.key("sib") + chunk,
                self.stage.at[slot, pl.ds(at, size)],
                self.pairs.at[pl.ds(base, size)],
                p.at(sibling=True),
            )

    def landing(self, part, sign, i):
        side = 0 if sign > 0 else 1
        if part == "a":
            return self.ring_a.at[side, pl.ds(i, 1)]
        return self.ring_bc.at[("b", "c").index(part), side, pl.ds(2 * i, 2)]

    def came(self, part, sign, i):
        ref = self.landing(part, sign, i)
        self.copies.arrived(self.key(part, sign, i), ref, ring_to(self.at, part, -sign))
        return ref

    def gather_up(self, chunk, base, arrivals):
        part = chunk[0]
        size = SIZE[part]
        ref = self.pairs.at[pl.ds(base, size)]
        self.copies.arrived(self.key("sib") + chunk, ref, self.at.at(sibling=True))
        slot, at = self.place_of(chunk)
        refs = [self.came(part, sign, i) for sign, i in arrivals]
        for t in range(size):
            value = self.mine[slot, at + t].astype(F32) + self.pairs[base + t].astype(F32)
            for came in refs:
                value += came[t].astype(F32)
            self.pairs[base + t] = value.astype(BF)
        return ref

    def send_round(self, kind, j):
        for chunk in self.chunks(kind, j):
            part, sign, hop, rel = chunk
            if sign == 0:
                continue
            order = scatter_order(part, sign)
            arrivals = [(sign, order.index((hop + 1, rel)))] if (hop + 1, rel) in order else []
            i = order.index((hop, rel))
            ref = self.gather_up(chunk, self.base(part, sign * hop, rel), arrivals)
            self.copies.start(
                self.key(part, sign, i), ref, self.landing(part, sign, i), ring_to(self.at, part, sign)
            )

    def finish_ring(self, part, rels):
        for rel in rels:
            arrivals = [(sign, scatter_order(part, sign).index((1, rel))) for sign in (1, -1)]
            self.gather_up((part, 0, 0, rel), self.base(part, 0, rel), arrivals)
            if rel:
                bricks, slot, device = self.second(part, rel)
                self.copies.start(
                    self.key(part + "2", rel),
                    self.pairs.at[bricks],
                    self.two.at[rel - 1, slot],
                    device,
                )

    def second(self, part, d):
        p = self.at
        base = p.brick(part, 0, d)
        if part == "a":
            return pl.ds(base, 1), pl.ds(0, 1), p.at(dy=d)
        if part == "b":
            return pl.ds(base, 2), pl.ds(1, 2), p.at(dy=d)
        return pl.ds(base, 2), pl.ds(3, 2), p.at(dx=d)

    def sum_second(self, part):
        p = self.at
        slots = {"a": (0,), "b": (1, 2), "c": (3, 4)}[part]
        for d in range(1, 4):
            _, slot, _ = self.second(part, d)
            device = p.at(dx=-d) if part == "c" else p.at(dy=-d)
            self.copies.arrived(self.key(part + "2", d), self.two.at[d - 1, slot], device)
        for t, slot in enumerate(slots):
            mine = p.brick(part, 0, 0) + t
            value = self.pairs[mine].astype(F32)
            for d in range(3):
                value += self.two[d, slot].astype(F32)
            self.sums[slot] = value.astype(BF).reshape(4, 64, TOK)
        if part == "a":
            for d in range(1, NX):
                self.copies.start(
                    self.key("a3", d), self.sums.at[0, p.xs[d]], self.three_a.at[d - 1], p.at(dx=d)
                )
            return
        first, i = {"b": (1, 0), "c": (3, 1)}[part]
        for d in range(1, NZ):
            self.copies.start(
                self.key(part + "3", d),
                self.sums.at[first + p.half[d], p.quarter[d]],
                self.three_bc.at[i, d - 1],
                p.at(dz=d),
            )

    def sum_third(self, part, out_ref):
        p = self.at
        if part == "a":
            value = self.sums[0, p.x].astype(F32)
            for d in range(1, NX):
                self.copies.arrived(self.key("a3", d), self.three_a.at[d - 1], p.at(dx=-d))
                value += self.three_a[d - 1].astype(F32)
            out_ref[0:FEAT] = value.astype(BF)
            return
        first, i = {"b": (1, 0), "c": (3, 1)}[part]
        value = self.sums[first + p.half[0], p.quarter[0]].astype(F32)
        for d in range(1, NZ):
            self.copies.arrived(self.key(part + "3", d), self.three_bc.at[i, d - 1], p.at(dz=-d))
            value += self.three_bc[i, d - 1].astype(F32)
        out_ref[(i + 1) * FEAT : (i + 2) * FEAT] = value.astype(BF)


def moe_kernel(
    logits_ref,
    routes_ref,
    losses_ref,
    tok_ref,
    cot_ref,
    gate_hbm,
    up_hbm,
    down_hbm,
    out_ref,
    in_ref,
    dgrad_hbm,
    tok_buf,
    cot_buf,
    wgu,
    wd,
    wdt,
    flat,
    total,
    hgrad,
    scaled,
    hid,
    grads,
    weighing,
    meta,
    ring_a,
    ring_bc,
    mine,
    stage,
    two,
    three_a,
    three_bc,
    sums,
    wsem,
    osem,
    free,
    send,
    recv,
    send2,
    recv2,
):
    p = Place()
    copies = Copies(send, recv)
    back = Copies(send2, recv2)
    tok = Gather("tok", p, copies, tok_buf)
    cot = Gather("cot", p, copies, cot_buf)
    here = p.at()[1]
    far = [(p.segs[d], here) for d in range(1, 8)]
    line = [p.at(dx=d) for d in range(1, NX)] + [p.at(dz=d) for d in range(1, NZ)]
    entered = enter(line + far)

    def load_gate_up():
        load_blocks(gate_hbm, lambda w: wgu.at[w, 0], wsem.at[0])
        load_blocks(up_hbm, lambda w: wgu.at[w, 1], wsem.at[0])

    def wait_gate_up():
        pltpu.make_async_copy(wgu, wgu, wsem.at[0]).wait()

    load_gate_up()
    pltpu.make_async_copy(down_hbm, flat, wsem.at[1]).start()

    tok.put_own(tok_ref)
    cot.put_own(cot_ref)
    share = jax.nn.sigmoid(logits_ref[0:1] - logits_ref[1:2])
    scale = losses_ref[...].astype(F32) / 4096.0
    weighing[...] = jnp.zeros_like(weighing)
    for e in range(8):
        combine = jnp.where(routes_ref[0:1] == e, share, 0.0) + jnp.where(
            routes_ref[1:2] == e, 1.0 - share, 0.0
        )
        weighing[e, 0:1] = combine
        weighing[e, 1:2] = combine * scale
    meta[p.seg] = weighing[p.seg]
    total[...] = jnp.zeros_like(total)
    hgrad[...] = jnp.zeros_like(hgrad)
    entered()

    tok.send_first()
    for d in range(1, 8):
        copies.start(("meta", d), weighing.at[p.segs[d]], meta.at[p.seg], far[d - 1])

    def turn_gu(w, carry):
        for k in range(2):
            block = wgu[w, k].reshape(256, 256)
            wgu[w, k] = block.T.reshape(4, 64, 256)
        return carry

    def turn_down(i, carry):
        block = flat[:, pl.ds(mult(i * 384, 384), 384)].T
        z, x = i // 2, (i % 2) * 2
        for k in range(2):
            rows = block[k * 192 : (k + 1) * 192]
            wd[z, x + k] = rows[0:64]
            wd[8 + (x + k) * 2 + z // 4, z % 4] = rows[64:128]
            wd[16 + (x + k) * 2 + z // 4, z % 4] = rows[128:192]
        return carry

    def turn_back(w, carry):
        wdt[w] = wd[w].reshape(256, 256).T
        return carry

    def w_gu(w):
        return wgu[w].reshape(512, 256)

    def w_down(w):
        return wdt[w]

    def activate(i, carry):
        y, r = i // 4, i % 4
        low = mult(r * 64, 64)
        gate = total[y, pl.ds(low, 64)]
        upward = total[y, pl.ds(mult(256 + r * 64, 64), 64)]
        first, second = meta[2 * y], meta[2 * y + 1]
        share = jnp.concatenate([first[0:1], second[0:1]], axis=1)
        scale = jnp.concatenate([first[1:2], second[1:2]], axis=1)
        sigma = jax.nn.sigmoid(gate)
        active = gate * sigma
        hidden = active * upward
        weighted = (hidden * share).astype(BF)
        hid[y, 0, pl.ds(low, 64)] = weighted[:, 0:128]
        hid[y, 1, pl.ds(low, 64)] = weighted[:, 128:256]
        scaled[y, pl.ds(low, 64)] = (hidden * scale).astype(BF)
        total[y, pl.ds(low, 64)] = upward * (sigma * (1.0 + gate * (1.0 - sigma))) * scale
        total[y, pl.ds(mult(256 + r * 64, 64), 64)] = active * scale
        return carry

    def backward(i, carry):
        y, r = i // 4, i % 4
        low = mult(r * 64, 64)
        high = mult(256 + r * 64, 64)
        grad = hgrad[y, pl.ds(low, 64)]
        gate_grad = (grad * total[y, pl.ds(low, 64)]).astype(BF)
        up_grad = (grad * total[y, pl.ds(high, 64)]).astype(BF)
        for c in range(2):
            grads[y, c, pl.ds(low, 64)] = gate_grad[:, c * 128 : (c + 1) * 128]
            grads[y, c, pl.ds(high, 64)] = up_grad[:, c * 128 : (c + 1) * 128]
        return carry

    def weight_grad(i, carry):
        z, x = i // 2, (i % 2) * 2
        low = mult((z % 4) * FEAT, FEAT)
        acc = jnp.zeros((256, 384), F32)
        for y in range(NY):
            halves = []
            for c in range(2):
                rows = []
                for k in range(2):
                    xk = x + k
                    rows.append(cot_buf[c, z * 4 + y, pl.ds(mult(xk * FEAT, FEAT), FEAT), :])
                    rows.append(cot_buf[c, 32 + (xk * 4 + y) * 2 + z // 4, pl.ds(low, FEAT), :])
                    rows.append(cot_buf[c, 64 + (y * 4 + xk) * 2 + z // 4, pl.ds(low, FEAT), :])
                halves.append(jnp.concatenate(rows, axis=0))
            acc += dot_nt(scaled[y], jnp.concatenate(halves, axis=1))
        flat[:, pl.ds(mult(i * 384, 384), 384)] = acc.astype(BF)
        return carry

    pairs = tok_buf

    def lhs_in(w):
        return jnp.concatenate(
            [wgu[w, 0].reshape(256, 256), wgu[w, 1].reshape(256, 256)], axis=1
        )

    def bufs(i):
        return (two.at[i], three_a.at[i], three_bc.at[i], sums.at[i])

    out = Scatter(
        "out", 0, p, back, lambda w: wd[w].reshape(256, 256), lambda y, c: hid[y, c],
        pairs.at[0], ring_a.at[0], ring_bc.at[0], mine, stage, bufs(0),
    )
    inp = Scatter(
        "in", 16, p, back, lhs_in, lambda y, c: grads[y, c],
        pairs.at[1], ring_a.at[1], ring_bc.at[1], mine, stage, bufs(1),
    )
    sent = {"a": [], "bc": []}

    def step_of(n):
        return (out, n) if n < 16 else (inp, n - 16)

    def produce(kind, n):
        if not 0 <= n < 32:
            return
        which, j = step_of(n)
        if n >= SLOTS:
            for copy in sent[kind][n - SLOTS]:
                copy.wait_send()
        sent[kind].append(back.take(lambda: which.produce(kind, j)))

    def turn(kind, n):
        if not 0 <= n < 32:
            return
        which, j = step_of(n)
        if kind == "a":
            if j < 14:
                which.send_round("a", j)
            else:
                which.finish_ring("a", ((1, 2), (3, 0))[j - 14])
        elif j < 12:
            which.send_round("bc", j)
        else:
            which.finish_ring(("b", "c")[j % 2], ((1, 2), (3, 0))[(j - 12) // 2])

    tok.wait_first_a()
    tok.send_second("a")
    tok.send_own("a", (0,))
    wait_gate_up()
    lax.fori_loop(0, 8, turn_gu, 0)
    tok.second_near("a")
    tok.wait_first_bc()
    for part in ("b", "c"):
        tok.send_second(part)
        tok.send_own(part, (0,))
    tok.second_far("a")
    lax.fori_loop(8, 16, turn_gu, 0)

    lag, first_bc, first_a = 3, 23, 27
    for n in range(first_a + 32):
        if n < 14:
            tok.ring_round(n, -1)
        elif n < 28:
            cot.ring_round(n - 14, -1)
        if lag <= n < 12 + lag:
            tok.ring_round(-1, n - lag)
        elif 12 + lag <= n < 24 + lag:
            cot.ring_round(-1, n - 12 - lag)
        if n == 0:
            lax.fori_loop(16, 24, turn_gu, 0)
        if n == 1:
            tok.second_near("b")
        if n == 2:
            tok.second_near("c")
            cot.send_first()
        if n == 3:
            tok.second_far("b")
            tok.second_far("c")
            pltpu.make_async_copy(down_hbm, flat, wsem.at[1]).wait()
        if n == 4:
            tok.wait_other_own()
            tok.multiply_own(w_gu, total)
        if 2 <= n <= 17:
            k = n - 2
            tok.wait_other(k, k - lag)
            tok.multiply_round(w_gu, total, k, k - lag)
        if 5 <= n < 9:
            lax.fori_loop(4 * n - 20, 4 * n - 16, turn_down, 0)
        if 9 <= n < 13:
            lax.fori_loop(6 * n - 54, 6 * n - 48, turn_back, 0)
        if n == 7:
            cot.wait_first_a()
            cot.send_second("a")
            cot.wait_first_bc()
            cot.send_second("b")
            cot.send_second("c")
        if n == 10:
            cot.send_own("b", (0,))
            cot.second_near("b")
            cot.send_own("c", (0,))
            cot.second_near("c")
            cot.send_own("a", (0,))
            cot.second_near("a")
        if n == 11:
            cot.second_far("a")
        if n == 12:
            cot.second_far("b")
            cot.second_far("c")
        if n == 17:
            before, copies.sent = copies.sent, []
            load_gate_up()
            for d in range(1, 8):
                copies.arrived(("meta", d), meta.at[p.segs[8 - d]], far[7 - d])
            lax.fori_loop(0, 16, activate, 0)
        if n == 17:
            cot.wait_other_own()
            cot.multiply_own(w_down, hgrad)
        if 16 <= n <= 29:
            k = n - 2
            cot.wait_other(k - 14, k - 12 - lag)
            cot.multiply_round(w_down, hgrad, k - 14, k - 12 - lag)
        if n == 19:
            for copy in before:
                copy.wait_send()
            pl.semaphore_signal(
                free, inc=1, device_id=p.at(sibling=True), device_id_type=MESH
            )
        if n == 20:
            pl.semaphore_wait(free, 1)
        if n == 29:
            lax.fori_loop(0, 16, backward, 0)
        if 29 <= n < 37:
            lax.fori_loop(2 * n - 58, 2 * n - 56, weight_grad, 0)
        if n == 37:
            dgrad = pltpu.make_async_copy(flat, dgrad_hbm, osem)
            dgrad.start()
        if n == 36:
            wait_gate_up()
        turn("bc", n - first_bc)
        produce("bc", n - first_bc + 3)
        turn("a", n - first_a)
        produce("a", n - first_a + 3)
        for which, start in ((out, 0), (inp, 16)):
            k = n - first_bc - start
            if k == 17:
                which.sum_second("b")
            if k == 18:
                which.sum_second("c")
        if n == first_a + 18:
            out.sum_second("a")
        if n == first_a + 22:
            for part in PARTS:
                out.sum_third(part, out_ref)
    inp.sum_second("a")
    for part in PARTS:
        inp.sum_third(part, in_ref)
    for kind in ("a", "bc"):
        for group in sent[kind][32 - SLOTS :]:
            for copy in group:
                copy.wait_send()
    copies.drain()
    back.drain()
    dgrad.wait()


def hand_out_kernel(out_in, in_in, grad_in, out_ref, in_ref, grad_ref, sems):
    copies = [
        pltpu.make_async_copy(out_in, out_ref, sems.at[0]),
        pltpu.make_async_copy(in_in, in_ref, sems.at[1]),
    ]
    for k in range(8):
        rows = pl.ds(32 * k, 32)
        copies.append(
            pltpu.make_async_copy(grad_in.at[rows], grad_ref.at[rows], sems.at[2 + k])
        )
    for copy in copies:
        copy.start()
    for copy in copies:
        copy.wait()


def per_device(
    tokens, router_logits, routes, loss_weights, cotangent, gate_weight, up_weight, down_weight
):
    gate5 = gate_weight.reshape(NZ, NX, 3, FEAT, 256)
    up5 = up_weight.reshape(NZ, NX, 3, FEAT, 256)
    down2 = down_weight.reshape(256, 6144)
    vmem = pl.BlockSpec(memory_space=pltpu.VMEM)
    hbm = pl.BlockSpec(memory_space=pl.ANY)
    n_gather, n_scatter = 288, 288

    output, input_grad, dgrad = pl.pallas_call(
        moe_kernel,
        name="moe",
        out_shape=(
            jax.ShapeDtypeStruct((192, TOK), BF),
            jax.ShapeDtypeStruct((192, TOK), BF),
            jax.ShapeDtypeStruct((256, 6144), BF),
        ),
        in_specs=[vmem] * 5 + [hbm] * 3,
        out_specs=(vmem, vmem, hbm),
        scratch_shapes=[
            pltpu.VMEM((2, 96, 256, TOK), BF),
            pltpu.VMEM((2, 96, 256, TOK), BF),
            pltpu.VMEM((24, 2, 4, 64, 256), BF),
            pltpu.VMEM((24, 4, 64, 256), BF),
            pltpu.VMEM((24, 256, 256), BF),
            pltpu.VMEM((256, 6144), BF),
            pltpu.VMEM((NY, 512, 256), F32),
            pltpu.VMEM((NY, 256, 256), F32),
            pltpu.VMEM((NY, 256, 256), BF),
            pltpu.VMEM((NY, 2, 256, TOK), BF),
            pltpu.VMEM((NY, 2, 512, TOK), BF),
            pltpu.VMEM((8, 8, TOK), F32),
            pltpu.VMEM((8, 8, TOK), F32),
            pltpu.VMEM((2, 2, 14, 256, TOK), BF),
            pltpu.VMEM((2, 2, 2, 12, 256, TOK), BF),
            pltpu.VMEM((SLOTS, 6, 256, TOK), BF),
            pltpu.VMEM((SLOTS, 6, 256, TOK), BF),
            pltpu.VMEM((2, 3, 5, 256, TOK), BF),
            pltpu.VMEM((2, 3, 64, TOK), BF),
            pltpu.VMEM((2, 2, 7, 64, TOK), BF),
            pltpu.VMEM((2, 5, 4, 64, TOK), BF),
            pltpu.SemaphoreType.DMA((2,)),
            pltpu.SemaphoreType.DMA,
            pltpu.SemaphoreType.REGULAR,
            pltpu.SemaphoreType.DMA((n_gather,)),
            pltpu.SemaphoreType.DMA((n_gather,)),
            pltpu.SemaphoreType.DMA((n_scatter,)),
            pltpu.SemaphoreType.DMA((n_scatter,)),
        ],
        compiler_params=pltpu.CompilerParams(
            collective_id=1, has_side_effects=True, vmem_limit_bytes=62 * 2**20
        ),
    )(
        router_logits.T,
        routes.T,
        loss_weights.reshape(1, TOK),
        tokens.T,
        cotangent.T,
        gate5,
        up5,
        down2,
    )
    output, input_grad, dgrad = pl.pallas_call(
        hand_out_kernel,
        name="hand_out",
        out_shape=(
            jax.ShapeDtypeStruct((192, TOK), BF),
            jax.ShapeDtypeStruct((192, TOK), BF),
            jax.ShapeDtypeStruct((256, 6144), BF),
        ),
        in_specs=[hbm] * 3,
        out_specs=(hbm,) * 3,
        scratch_shapes=[pltpu.SemaphoreType.DMA((10,))],
    )(output, input_grad, dgrad)
    return (output.T, input_grad.T, dgrad.reshape(1, 256, 6144))


def solution(mesh):
    in_specs = (
        P("segment", "fsdp"),
        P("segment", None),
        P("segment", None),
        P("segment"),
        P("segment", "fsdp"),
        P("segment", None, "fsdp"),
        P("segment", None, "fsdp"),
        P("segment", "fsdp", None),
    )
    out_specs = (P("segment", "fsdp"), P("segment", "fsdp"), P("segment", "fsdp", None))
    return jax.shard_map(
        per_device, mesh=mesh, in_specs=in_specs, out_specs=out_specs, check_vma=False
    )
```
